32 devices in a mesh: wide: 16 (over z, y, x), narrow: 2 (over core).
Axes of the slice: x: 2, y: 2, z: 4, core: 2. Of those that a mesh axis runs over, the one named last changes fastest.
Arguments:
- kernel: float32 [2048, 64, 128], P(('wide', 'narrow')), may hold values from 0 to 0.015625
- volume: float32 [2048, 64], P(('wide', 'narrow')), may hold values from 0.5 to 4
- velocity: float32 [2048, 3, 64], P(('wide', 'narrow')), may hold values from -6 to 6
- block_brick: int32 [2048, 1], P(('wide', 'narrow')), may hold values from 0 to 15; in each aligned block of 64 rows (0 to 63, 64 to 127, ...) at most 8 rows name the same one
- block_tile: int32 [2048], P(('wide', 'narrow')), may hold values from 0 to 127
- fluid_velocity: float32 [3, 64, 16, 512], P(None, 'wide', 'narrow'), may hold values from -6 to 6
Outputs:
- particle_drag: float32 [2048, 3, 64], P(('wide', 'narrow'))
- pressure: float32 [64, 16, 512], P('wide', 'narrow')
- fluid_next: float32 [3, 64, 16, 512], P(None, 'wide', 'narrow')
The draws below stay inside these ranges and needn't reach their ends.
Inputs may be any that keep to these rules, and one draw needn't show every extreme that they name: `block_brick`: among the 64 blocks of one device, at most 8 name the same brick, a bound that some block reaches.
All inputs are finite; a program needn't handle non-finite values.
Results may differ from the reference program's by a relative error of at most 0.00007.
Values sent between devices are 32-bit elements; how exact they have to be, the bound alone decides.
A program may use at most 64 MiB of HBM per device.

```python
import math
import jax
import jax.numpy as jnp
import numpy as np
from jax import lax

PART_BLK = 64
TILE_CELLS = 128
CX = 4
CZ = 8
NY = 512
BLK_DEV = 64
SWEEPS = 6
TILES_DEV = 128
CAP = 8
BLOCKS = 2048
NX = 64
NZ = 16
N_WIDE = 16
N_NARROW = 2


def touch_ends(array, rng, smallest, high):
    longest = array.shape.index(max(array.shape))
    spots = []
    for shift in (0, 1):
        where = [jax.random.randint(jax.random.fold_in(rng, axis), (), 0, length) for axis, length in enumerate(array.shape)]
        where[longest] = (where[longest] + shift) % array.shape[longest]
        spots.append(tuple(where))
    return array.at[spots[0]].set(smallest).at[spots[1]].set(high)


def shard_levels(rng, dims, pieces, least, high):
    factor_of = 1.0
    for axis_at, shards_of in pieces:
        heights = jax.random.uniform(jax.random.fold_in(jax.random.fold_in(rng, 6), axis_at), (shards_of,), jnp.float32, least / len(pieces), high / len(pieces))
        factor_of = factor_of * jnp.repeat(jnp.exp(heights), dims[axis_at] // shards_of).reshape((-1,) + (1,) * (len(dims) - 1 - axis_at))
    return factor_of


def routed_block(key, own, number, rows, number_of, top, bound, slope):
    ranking = jax.random.permutation(key, number_of)
    heavy_load, usual = portions_of(number_of, rows * top, bound, slope, True), portions_of(number_of, rows * top, bound, slope, False)
    places = jnp.arange(number_of)

    def named(lengths, rotation):
        used = int((lengths > 0).sum())
        fixed = max(1, used // 4)
        passed = fixed + (places - fixed + rotation * (used - fixed)) % max(1, number_of - fixed)
        return jnp.zeros((number_of,), jnp.int32).at[ranking[jnp.where(places < fixed, places, passed)]].set(jnp.asarray(lengths, jnp.int32))

    lengths = jnp.where(number % 4 == 0, named(heavy_load, number // 4), named(usual, number - number // 4 - 1))
    mixed = jax.random.permutation(jax.random.fold_in(own, 3), number_of)
    giver, sink = mixed[0:number_of // 2 * 2:2], mixed[1:number_of // 2 * 2:2]
    slack = jnp.minimum(lengths[giver] - 1, bound - lengths[sink]) // 2
    slack = jnp.where((giver == ranking[0]) | (sink == ranking[0]) | (lengths[sink] == 0), 0, jnp.maximum(slack, 0))
    passed = jax.random.randint(jax.random.fold_in(own, 4), (number_of // 2,), 0, 1 << 20) % (slack + 1)
    lengths = lengths.at[giver].add(-passed).at[sink].add(passed)
    items = jnp.searchsorted(jnp.cumsum(lengths), jnp.arange(rows * top), side="right").astype(jnp.int32)
    listing = items.reshape(top, rows).T
    listing = listing[jax.random.permutation(jax.random.fold_in(own, 1), rows)]
    rotation = jax.random.randint(jax.random.fold_in(own, 2), (rows, 1), 0, top)
    return jnp.take_along_axis(listing, (jnp.arange(top)[None, :] + rotation) % top, axis=1)


def portions_of(number_of, total, reach, skew, full):
    weights = [(1 << 20) // math.isqrt(standing ** skew) + 1 for standing in range(1, number_of + 1)]
    largest = reach if full else min(reach, max(-(-total // number_of), total * weights[0] // sum(weights)))
    least = 1 if total - largest >= number_of - 1 else 0
    counts, surplus = [largest] + [least] * (number_of - 1), total - largest - least * (number_of - 1)
    while surplus > 0:
        free = [i for i in range(1, number_of) if counts[i] < largest] or [i for i in range(1, number_of) if counts[i] < reach]
        whole, left = sum([weights[i] for i in free]), surplus
        for i in free:
            addition = min(reach - counts[i], max(1, left * weights[i] // whole), surplus)
            counts[i] = counts[i] + addition
            surplus = surplus - addition
    return np.array(counts)


def gaussian(own_key, dims, deviation, bound, shards=(), held_as=jnp.bfloat16):
    array = jax.random.normal(own_key, dims, jnp.float32) * deviation
    if len(shards) > 0:
        array = shard_levels(own_key, dims, shards, -0.22, 0.18) * array
    return jnp.clip(array, min=-bound, max=bound).astype(held_as)


def setup_inputs(seed: int = 0) -> dict:
    arg_keys = jax.random.split(jax.random.key(seed), 7)
    kernel = jnp.clip(0.015625 * jax.random.uniform(arg_keys[0], (BLOCKS, PART_BLK, TILE_CELLS), jnp.float32) ** shard_levels(arg_keys[0], (BLOCKS, PART_BLK, TILE_CELLS), ((0, 32),), -0.2, 0.2), 0.0, 0.015625)
    volume = jnp.clip(jnp.exp(math.log(4.0) - 2.0794415 * jax.random.uniform(arg_keys[1], (BLOCKS, PART_BLK), jnp.float32) ** shard_levels(arg_keys[1], (BLOCKS, PART_BLK), ((0, 32),), -0.2, 0.2)), 0.5, 4.0)
    velocity = gaussian(arg_keys[2], (BLOCKS, 3, PART_BLK), 1.0, 6.0, ((0, 32),), jnp.float32)
    block_brick_keys = jax.random.split(jax.random.fold_in(arg_keys[3], 1), BLOCKS // BLK_DEV)
    block_brick_turns = jax.random.permutation(jax.random.fold_in(arg_keys[3], 3), BLOCKS // BLK_DEV)
    block_brick = jax.vmap(lambda own, number: routed_block(jax.random.fold_in(arg_keys[3], 2), own, number, BLK_DEV, N_WIDE, 1, CAP, 2))(block_brick_keys, block_brick_turns).reshape((BLOCKS, 1))
    block_tile = touch_ends(jax.random.randint(arg_keys[4], (BLOCKS,), 0, TILES_DEV), jax.random.fold_in(arg_keys[4], 1), 0, TILES_DEV - 1).astype(jnp.int32)
    fluid_velocity = gaussian(arg_keys[5], (3, NX, NZ, NY), 1.0, 6.0, ((1, 16), (2, 2)), jnp.float32)
    return {"kernel": kernel, "volume": volume, "velocity": velocity, "block_brick": block_brick, "block_tile": block_tile, "fluid_velocity": fluid_velocity}


highest = lax.Precision.HIGHEST


def neighbours(padded):
    return [padded[..., 2:, 1:-1, 1:-1], padded[..., :-2, 1:-1, 1:-1],
            padded[..., 1:-1, 2:, 1:-1], padded[..., 1:-1, :-2, 1:-1],
            padded[..., 1:-1, 1:-1, 2:], padded[..., 1:-1, 1:-1, :-2]]


def to_grid(tiled):
    count = tiled.shape[0]
    shaped = tiled.reshape(count, N_WIDE, N_NARROW, CX, CZ, NY)
    return shaped.transpose(0, 1, 3, 2, 4, 5).reshape(count, NX, NZ, NY)


def from_grid(field):
    count = field.shape[0]
    shaped = field.reshape(count, N_WIDE, CX, N_NARROW, CZ, NY)
    return shaped.transpose(0, 1, 3, 2, 4, 5).reshape(count, N_WIDE * N_NARROW * TILES_DEV, TILE_CELLS)


def pressure_sides(pressure):
    padded = jnp.pad(pressure, 1)
    return neighbours(padded)


def reference(kernel, volume, velocity, block_brick, block_tile, fluid_velocity):
    blocks = kernel.shape[0]
    device = jnp.arange(blocks, dtype=jnp.int32) // BLK_DEV
    slab = device % N_NARROW
    target = (block_brick[:, 0] * N_NARROW + slab) * TILES_DEV + block_tile
    carried = jnp.concatenate([volume[:, None, :], volume[:, None, :] * velocity], axis=1)
    partial_value = jnp.einsum("bkp,bpc->bkc", carried, kernel, precision=highest)
    tile_total = N_WIDE * N_NARROW * TILES_DEV
    summed = jax.ops.segment_sum(partial_value, target, num_segments=tile_total)
    spread = to_grid(summed.transpose(1, 0, 2))
    solid_share = spread[0]
    momentum = spread[1:]
    growth = (1.0 + solid_share) ** 2
    provisional = (fluid_velocity + growth * momentum) / (1.0 + growth * solid_share)
    void_share = 1.0 / (1.0 + solid_share)
    stacked = jnp.concatenate([void_share * provisional, void_share[None]], axis=0)
    sides = neighbours(jnp.pad(stacked, ((0, 0), (1, 1), (1, 1), (1, 1))))
    source = -0.5 * (sides[0][0] - sides[1][0] + sides[2][1] - sides[3][1] + sides[4][2] - sides[5][2])
    weights = [0.5 * (void_share + side[3]) for side in sides]
    diagonal = weights[0] + weights[1] + weights[2] + weights[3] + weights[4] + weights[5]
    pressure = source / diagonal
    for sweep_index in range(SWEEPS - 1):
        beside_all = pressure_sides(pressure)
        total = source
        for which in range(6):
            total = total + weights[which] * beside_all[which]
        pressure = total / diagonal
    beside_all = pressure_sides(pressure)
    fluid_next = provisional - 0.5 * jnp.stack([beside_all[0] - beside_all[1], beside_all[2] - beside_all[3], beside_all[4] - beside_all[5]])
    returned = jnp.concatenate([growth * fluid_next, growth[None]], axis=0)
    picked = from_grid(returned)[:, target]
    sampled = jnp.einsum("kbc,bpc->bkp", picked, kernel, precision=highest)
    particle_drag = volume[:, None, :] * sampled[:, :3] - carried[:, 1:] * sampled[:, 3:4]
    return particle_drag, pressure, fluid_next
```

```python
import functools

import jax
import jax.numpy as jnp
from jax import lax
from jax.experimental import pallas as pl
from jax.experimental.pallas import tpu as pltpu
from jax.sharding import PartitionSpec as P

SWEEPS = 6
MESH = pl.DeviceIdType.MESH
f32 = jnp.float32
bf16 = jnp.bfloat16


def split(value):
    high = value.astype(bf16)
    return high, (value - high.astype(f32)).astype(bf16)


def dot(a, b):
    return jnp.dot(a, b, preferred_element_type=f32)


def body(
    n_wide, n_narrow, cap,
    kernel_hbm, volume_ref, velocity_ref, brick_ref, tile_ref, fluid_ref,
    drag_ref, pressure_ref, next_ref,
    kernel_buf, pieces, rows, sent_tiles, got_tiles, sent, got,
    sent_growth, got_growth, sent_next, got_next,
    first, first_z, first_gx, first_gz, press, press_z, press_gx, press_gz,
    load_sem, send_sem, recv_sem, side_send, side_recv,
):
    wide, narrow = lax.axis_index("wide"), lax.axis_index("narrow")
    blocks, particles, lanes = kernel_buf.shape
    _, cx, cz, ny = fluid_ref.shape
    nq = ny // lanes
    plane = nq * cz
    tiles = cx * plane
    slots = n_wide * cap

    load = pltpu.make_async_copy(kernel_hbm, kernel_buf, load_sem)
    load.start()

    barrier = pltpu.get_barrier_semaphore()

    def greet(step, carry):
        pl.semaphore_signal(
            barrier, inc=1, device_id=(lax.rem(wide + step, n_wide), narrow), device_id_type=MESH
        )
        return carry

    lax.fori_loop(1, n_wide, greet, 0)
    for shift in (-1, 1):
        here = (narrow > 0) if shift < 0 else (narrow < n_narrow - 1)

        @pl.when(here)
        def _():
            pl.semaphore_signal(
                barrier, inc=1, device_id=(wide, narrow + shift), device_id_type=MESH
            )

    for at_edge, index, ghosts in (
        (wide == 0, 0, (first_gx, press_gx)),
        (wide == n_wide - 1, 1, (first_gx, press_gx)),
        (narrow == 0, 0, (first_gz, press_gz)),
        (narrow == n_narrow - 1, 1, (first_gz, press_gz)),
    ):

        @pl.when(at_edge)
        def _():
            ghosts[0][index] = jnp.zeros(ghosts[0].shape[1:], f32)
            for e in range(SWEEPS):
                ghosts[1][e, index] = jnp.zeros(ghosts[1].shape[2:], f32)

    rows_b = lax.broadcasted_iota(jnp.int32, (blocks, blocks), 0)
    cols_b = lax.broadcasted_iota(jnp.int32, (blocks, blocks), 1)
    target_row = jnp.broadcast_to(brick_ref[...].astype(f32), (blocks, blocks))
    target_col = jnp.sum(jnp.where(rows_b == cols_b, target_row, 0.0), axis=1, keepdims=True)
    same = jnp.where(target_col == target_row, 1.0, 0.0)
    position_row = jnp.sum(jnp.where(rows_b < cols_b, same, 0.0), axis=0, keepdims=True)
    position_col = jnp.sum(jnp.where(cols_b < rows_b, same, 0.0), axis=1, keepdims=True)
    placed_row = target_row[:1] * cap + position_row
    placed_col = target_col * cap + position_col
    slot_col = lax.broadcasted_iota(jnp.int32, (slots, blocks), 0).astype(f32)
    place = jnp.where(slot_col == placed_row, 1.0, 0.0)
    tile_col = jnp.sum(place * tile_ref[...].astype(f32), axis=1, keepdims=True)
    sent_tiles[...] = jnp.broadcast_to(tile_col, (slots, lanes)).reshape(n_wide, cap, lanes)

    beside_z = jnp.where(narrow > 0, 1, 0) + jnp.where(narrow < n_narrow - 1, 1, 0)
    pl.semaphore_wait(barrier, n_wide - 1 + beside_z)

    def passing(phase, source, target, step):
        partner = lax.rem(wide + step, n_wide)
        return pltpu.make_async_remote_copy(
            src_ref=source.at[partner],
            dst_ref=target.at[wide],
            send_sem=send_sem.at[phase, step],
            recv_sem=recv_sem.at[phase, step],
            device_id=(partner, narrow),
            device_id_type=MESH,
        )

    def start_all(phase, source, target):
        def go(step, carry):
            passing(phase, source, target, step).start()
            return carry

        lax.fori_loop(1, n_wide, go, 0)
        target[wide] = source[wide]

    def wait_all(phase, source, target):
        def go(step, carry):
            passing(phase, source, target, step).wait_recv()
            return carry

        lax.fori_loop(1, n_wide, go, 0)

    def end_all(phase, source, target):
        def go(step, carry):
            passing(phase, source, target, step).wait_send()
            return carry

        lax.fori_loop(1, n_wide, go, 0)

    start_all(0, sent_tiles, got_tiles)

    volume = volume_ref[...]
    carried = [volume] + [volume * velocity_ref[a] for a in range(3)]
    for k in range(4):
        high = carried[k].astype(bf16).astype(f32)
        low = carried[k] - high
        rows[pl.ds(k, blocks, stride=8), :] = jnp.concatenate([high, high], axis=1)
        rows[pl.ds(4 + k, blocks, stride=8), :] = jnp.concatenate(
            [low, jnp.zeros_like(low)], axis=1
        )
    load.wait()
    group = 8

    def contract(step, carry):
        base = pl.multiple_of(step * group, group)
        weights = kernel_buf[pl.ds(base, group)]
        high, low = split(weights)
        both = jnp.concatenate([high, low], axis=1)
        pieces[pl.ds(base, group)] = both
        at = pl.ds(pl.multiple_of(base * 8, 8), group * 8)
        left = rows[at, :].reshape(group, 8, lanes).astype(bf16)
        out = lax.dot_general(
            left, both, (((2,), (1,)), ((0,), (0,))), preferred_element_type=f32
        )
        rows[at, :] = out.reshape(group * 8, lanes)
        return carry

    lax.fori_loop(0, blocks // group, contract, 0)
    own = [
        split(rows[pl.ds(k, blocks, stride=8), :] + rows[pl.ds(4 + k, blocks, stride=8), :])
        for k in range(4)
    ]
    right = jnp.concatenate(
        [jnp.concatenate([o[0] for o in own], axis=1), jnp.concatenate([o[1] for o in own], axis=1)],
        axis=0,
    )
    place = jnp.concatenate([place, place], axis=1).astype(bf16)
    in_slots = dot(place, right)
    for k in range(4):
        sent[:, k] = in_slots[:, k * lanes : (k + 1) * lanes].reshape(n_wide, cap, lanes)
    start_all(1, sent, got)

    wait_all(0, sent_tiles, got_tiles)
    order = lax.broadcasted_iota(jnp.int32, (slots, tiles), 1)
    x_of, q_of, z_of = order // plane, (order // cz) % nq, order % cz
    tile_of = ((x_of * cz + z_of) * nq + q_of).astype(f32)
    tile_slots = got_tiles[...].reshape(slots, lanes)
    selector = jnp.where(tile_slots == tile_of, 1.0, 0.0)
    turned = jnp.transpose(selector).astype(bf16)
    selector = selector.astype(bf16)
    turned = jnp.concatenate([turned, turned], axis=1)
    selector = jnp.concatenate([selector, selector], axis=1)

    fluid = [
        jnp.concatenate(
            [
                fluid_ref[a, x, :, q * lanes : (q + 1) * lanes]
                for x in range(cx)
                for q in range(nq)
            ],
            axis=0,
        )
        for a in range(3)
    ]

    wait_all(1, sent, got)
    arrived = [split(got[:, k].reshape(slots, lanes)) for k in range(4)]
    right = jnp.concatenate(
        [jnp.concatenate([o[i] for o in arrived], axis=1) for i in range(2)], axis=0
    )
    spread = dot(turned, right)
    solid = spread[:, :lanes]
    growth = (1.0 + solid) * (1.0 + solid)
    scale = 1.0 / (1.0 + growth * solid)
    provisional = [
        (fluid[a] + growth * spread[:, (a + 1) * lanes : (a + 2) * lanes]) * scale
        for a in range(3)
    ]
    void = 1.0 / (1.0 + solid)
    shape = (cx, nq, cz, lanes)
    stacked = [(void * provisional[a]).reshape(shape) for a in range(3)] + [void.reshape(shape)]

    def sides_of(e, source, source_z, ghost_x, ghost_z, fields):
        count = len(fields)
        high_rows = count * plane
        for x in range(cx):
            for i in range(count):
                source[x, i * plane : (i + 1) * plane, :] = fields[i][x].reshape(plane, lanes)
        for i in range(count):
            for side, z in ((0, 0), (1, cz - 1)):
                for x in range(cx):
                    source_z[side, (x * count + i) * nq : (x * count + i + 1) * nq, :] = fields[i][
                        x, :, z, :
                    ]

        def copies(along, side):
            if along == 0:
                src = source.at[0 if side == 0 else cx - 1]
                dst, to = ghost_x.at[1 - side], (wide + (1 if side else -1), narrow)
            else:
                src, dst = source_z.at[side], ghost_z.at[1 - side]
                to = (wide, narrow + (1 if side else -1))
            return pltpu.make_async_remote_copy(
                src_ref=src,
                dst_ref=dst,
                send_sem=side_send.at[e, along * 2 + side],
                recv_sem=side_recv.at[e, along * 2 + side],
                device_id=to,
                device_id_type=MESH,
            )

        has = (
            (wide > 0, wide < n_wide - 1),
            (narrow > 0, narrow < n_narrow - 1),
        )
        for along in range(2):
            for side in range(2):

                @pl.when(has[along][side])
                def _():
                    copies(along, side).start()

        lane = lax.broadcasted_iota(jnp.int32, shape, 3)
        row = lax.broadcasted_iota(jnp.int32, shape, 2)
        zero = jnp.zeros((cx, 1, cz, lanes), f32)
        in_y = []
        for p in fields:
            up = pltpu.roll(p, lanes - 1, 3)
            down = pltpu.roll(p, 1, 3)
            up = jnp.where(lane == lanes - 1, jnp.concatenate([up[:, 1:], zero], axis=1), up)
            down = jnp.where(lane == 0, jnp.concatenate([zero, down[:, :-1]], axis=1), down)
            in_y.append((up, down))
        for along in range(2):
            for side in range(2):

                @pl.when(has[along][1 - side])
                def _():
                    copies(along, side).wait_recv()

        result = []
        for i, p in enumerate(fields):
            low = ghost_x[0, i * plane : (i + 1) * plane, :].reshape((1,) + shape[1:])
            high = ghost_x[1, i * plane : (i + 1) * plane, :].reshape((1,) + shape[1:])

            def row_ghost(side):
                return jnp.concatenate(
                    [
                        jnp.broadcast_to(
                            ghost_z[side, (x * count + i) * nq + q : (x * count + i) * nq + q + 1, :],
                            (cz, lanes),
                        )
                        for x in range(cx)
                        for q in range(nq)
                    ],
                    axis=0,
                ).reshape(shape)

            z_up = jnp.where(row == cz - 1, row_ghost(1), pltpu.roll(p, cz - 1, 2))
            z_down = jnp.where(row == 0, row_ghost(0), pltpu.roll(p, 1, 2))
            result.append(
                (
                    jnp.concatenate([p[1:], high], axis=0),
                    jnp.concatenate([low, p[:-1]], axis=0),
                    z_up,
                    z_down,
                    in_y[i][0],
                    in_y[i][1],
                )
            )
        for along in range(2):
            for side in range(2):

                @pl.when(has[along][side])
                def _():
                    copies(along, side).wait_send()

        return result

    beside = sides_of(0, first, first_z, first_gx, first_gz, stacked)

    def give_back(values, target, start):
        wide_values = [split(v) for v in values]
        right = jnp.concatenate(
            [jnp.concatenate([o[i] for o in wide_values], axis=1) for i in range(2)], axis=0
        )
        picked = dot(selector, right)
        for k in range(len(values)):
            target[:, start + k] = picked[:, k * lanes : (k + 1) * lanes].reshape(
                n_wide, cap, lanes
            )

    give_back([growth], sent_growth, 0)
    start_all(2, sent_growth, got_growth)

    source = -0.5 * (
        beside[0][0] - beside[0][1] + beside[1][2] - beside[1][3] + beside[2][4] - beside[2][5]
    )
    here_void = stacked[3]
    weights = [0.5 * (here_void + beside[3][i]) for i in range(6)]
    diagonal = weights[0] + weights[1] + weights[2] + weights[3] + weights[4] + weights[5]
    inverse = 1.0 / diagonal
    weights = [w * inverse for w in weights]
    source = source * inverse
    pressure = source
    for sweep in range(SWEEPS):
        around = sides_of(
            1 + sweep,
            press.at[sweep],
            press_z.at[sweep],
            press_gx.at[sweep],
            press_gz.at[sweep],
            [pressure],
        )[0]
        if sweep < SWEEPS - 1:
            total = source
            for i in range(6):
                total = total + weights[i] * around[i]
            pressure = total
    steps = [around[0] - around[1], around[2] - around[3], around[4] - around[5]]
    following = [provisional[a] - 0.5 * steps[a].reshape(tiles, lanes) for a in range(3)]
    give_back([growth * v for v in following], sent_next, 0)
    start_all(3, sent_next, got_next)

    for x in range(cx):
        for q in range(nq):
            cut = slice(q * lanes, (q + 1) * lanes)
            at = (x * nq + q) * cz
            pressure_ref[x, :, cut] = pressure[x, q]
            for a in range(3):
                next_ref[a, x, :, cut] = following[a][at : at + cz]

    slot_row = lax.broadcasted_iota(jnp.int32, (blocks, slots), 1).astype(f32)
    back = jnp.where(slot_row == placed_col, 1.0, 0.0).astype(bf16)

    def place_back(target, k, row):
        high, low = split(target[:, k].reshape(slots, lanes))
        out = dot(back, jnp.concatenate([high, low], axis=1))
        rows[pl.ds(row, blocks, stride=8), :] = out[:, :lanes]
        rows[pl.ds(4 + row, blocks, stride=8), :] = out[:, lanes:]

    wait_all(2, sent_growth, got_growth)
    place_back(got_growth, 0, 3)
    wait_all(3, sent_next, got_next)
    for k in range(3):
        place_back(got_next, k, k)

    def sample(step, carry):
        base = pl.multiple_of(step * group, group)
        at = pl.ds(pl.multiple_of(base * 8, 8), group * 8)
        left = rows[at, :].reshape(group, 8, lanes).astype(bf16)
        out = lax.dot_general(
            left,
            pieces[pl.ds(base, group)],
            (((2,), (2,)), ((0,), (0,))),
            preferred_element_type=f32,
        )
        rows[at, :] = out.reshape(group * 8, lanes)
        return carry

    lax.fori_loop(0, blocks // group, sample, 0)

    def sampled(k):
        top = rows[pl.ds(k, blocks, stride=8), :]
        low = rows[pl.ds(4 + k, blocks, stride=8), :]
        return (top + low)[:, :particles] + pltpu.roll(top, particles, 1)[:, :particles]

    fourth = sampled(3)
    for k in range(3):
        drag_ref[k] = volume * sampled(k) - carried[1 + k] * fourth

    for phase, source, target in (
        (0, sent_tiles, got_tiles),
        (1, sent, got),
        (2, sent_growth, got_growth),
        (3, sent_next, got_next),
    ):
        end_all(phase, source, target)


def solution(mesh):
    n_wide, n_narrow = mesh.shape["wide"], mesh.shape["narrow"]

    def local(kernel, volume, velocity, block_brick, block_tile, fluid_velocity):
        blocks, particles, lanes = kernel.shape
        _, cx, cz, ny = fluid_velocity.shape
        cap = max(2, (2 * blocks + n_wide - 1) // n_wide)
        cap = (cap + 7) // 8 * 8
        nq = ny // lanes
        plane = nq * cz
        vmem = pltpu.VMEM
        any_spec = pl.BlockSpec(memory_space=pl.ANY)
        vmem_spec = pl.BlockSpec(memory_space=pltpu.VMEM)
        flux = [
            vmem((n_wide, cap, lanes), f32),
            vmem((n_wide, cap, lanes), f32),
            vmem((n_wide, 4, cap, lanes), f32),
            vmem((n_wide, 4, cap, lanes), f32),
            vmem((n_wide, 1, cap, lanes), f32),
            vmem((n_wide, 1, cap, lanes), f32),
            vmem((n_wide, 3, cap, lanes), f32),
            vmem((n_wide, 3, cap, lanes), f32),
        ]
        halo = [
            vmem((cx, 4 * plane, lanes), f32),
            vmem((2, 4 * cx * nq, lanes), f32),
            vmem((2, 4 * plane, lanes), f32),
            vmem((2, 4 * cx * nq, lanes), f32),
            vmem((SWEEPS, cx, plane, lanes), f32),
            vmem((SWEEPS, 2, cx * nq, lanes), f32),
            vmem((SWEEPS, 2, plane, lanes), f32),
            vmem((SWEEPS, 2, cx * nq, lanes), f32),
        ]
        drag, pressure, following = pl.pallas_call(
            functools.partial(body, n_wide, n_narrow, cap),
            out_shape=(
                jax.ShapeDtypeStruct((3, blocks, particles), f32),
                jax.ShapeDtypeStruct((cx, cz, ny), f32),
                jax.ShapeDtypeStruct((3, cx, cz, ny), f32),
            ),
            in_specs=[any_spec] + [vmem_spec] * 5,
            out_specs=(vmem_spec,) * 3,
            scratch_shapes=[
                vmem((blocks, particles, lanes), f32),
                vmem((blocks, 2 * particles, lanes), bf16),
                vmem((blocks * 8, lanes), f32),
            ]
            + flux
            + halo
            + [
                pltpu.SemaphoreType.DMA,
                pltpu.SemaphoreType.DMA((4, n_wide)),
                pltpu.SemaphoreType.DMA((4, n_wide)),
                pltpu.SemaphoreType.DMA((SWEEPS + 1, 4)),
                pltpu.SemaphoreType.DMA((SWEEPS + 1, 4)),
            ],
            compiler_params=pltpu.CompilerParams(
                collective_id=0, has_side_effects=True, vmem_limit_bytes=40 * 1024 * 1024
            ),
        )(
            kernel,
            volume,
            jnp.transpose(velocity, (1, 0, 2)),
            block_brick.reshape(1, blocks),
            block_tile.reshape(1, blocks),
            fluid_velocity,
        )
        return jnp.transpose(drag, (1, 0, 2)), pressure, following

    return jax.shard_map(
        local,
        mesh=mesh,
        in_specs=(
            P(("wide", "narrow"), None, None),
            P(("wide", "narrow"), None),
            P(("wide", "narrow"), None, None),
            P(("wide", "narrow"), None),
            P(("wide", "narrow")),
            P(None, "wide", "narrow", None),
        ),
        out_specs=(
            P(("wide", "narrow"), None, None),
            P("wide", "narrow", None),
            P(None, "wide", "narrow", None),
        ),
        check_vma=False,
    )
```

```python
import functools

import jax
import jax.numpy as jnp
from jax import lax
from jax.experimental import pallas as pl
from jax.experimental.pallas import tpu as pltpu
from jax.sharding import PartitionSpec as P

SWEEPS = 6
MESH = pl.DeviceIdType.MESH
f32 = jnp.float32
bf16 = jnp.bfloat16


def split(value):
    high = value.astype(bf16)
    return high, (value - high.astype(f32)).astype(bf16)


def dot(a, b):
    return jnp.dot(a, b, preferred_element_type=f32)


def body(
    n_wide, n_narrow, cap,
    kernel_hbm, volume_hbm, velocity_hbm, brick_hbm, tile_hbm, fluid_hbm,
    drag_ref, pressure_ref, next_ref,
    kernel_buf, volume_ref, velocity_ref, brick_ref, tile_ref, fluid_ref, pieces, rows, sent_tiles, got_tiles, sent, got,
    sent_growth, got_growth, sent_next, got_next,
    first, first_z, first_gx, first_gz, press, press_z, press_gx, press_gz,
    load_sem, send_sem, recv_sem, side_send, side_recv,
):
    wide, narrow = lax.axis_index("wide"), lax.axis_index("narrow")
    blocks, particles, lanes = kernel_buf.shape
    _, cx, cz, ny = fluid_ref.shape
    nq = ny // lanes
    plane = nq * cz
    tiles = cx * plane
    slots = n_wide * cap

    loads = [
        pltpu.make_async_copy(here, there, load_sem.at[i])
        for i, (here, there) in enumerate(
            (
                (brick_hbm, brick_ref),
                (tile_hbm, tile_ref),
                (volume_hbm, volume_ref),
                (velocity_hbm, velocity_ref),
                (kernel_hbm, kernel_buf),
                (fluid_hbm, fluid_ref),
            )
        )
    ]
    for load in loads:
        load.start()

    barrier = pltpu.get_barrier_semaphore()

    def greet(step, carry):
        pl.semaphore_signal(
            barrier, inc=1, device_id=(lax.rem(wide + step, n_wide), narrow), device_id_type=MESH
        )
        return carry

    lax.fori_loop(1, n_wide, greet, 0)
    for shift in (-1, 1):
        here = (narrow > 0) if shift < 0 else (narrow < n_narrow - 1)

        @pl.when(here)
        def _():
            pl.semaphore_signal(
                barrier, inc=1, device_id=(wide, narrow + shift), device_id_type=MESH
            )

    for at_edge, index, ghosts in (
        (wide == 0, 0, (first_gx, press_gx)),
        (wide == n_wide - 1, 1, (first_gx, press_gx)),
        (narrow == 0, 0, (first_gz, press_gz)),
        (narrow == n_narrow - 1, 1, (first_gz, press_gz)),
    ):

        @pl.when(at_edge)
        def _():
            ghosts[0][index] = jnp.zeros(ghosts[0].shape[1:], f32)
            for e in range(SWEEPS):
                ghosts[1][e, index] = jnp.zeros(ghosts[1].shape[2:], f32)

    loads[0].wait()
    loads[1].wait()
    rows_b = lax.broadcasted_iota(jnp.int32, (blocks, blocks), 0)
    cols_b = lax.broadcasted_iota(jnp.int32, (blocks, blocks), 1)
    target_row = jnp.broadcast_to(brick_ref[...].astype(f32), (blocks, blocks))
    target_col = jnp.sum(jnp.where(rows_b == cols_b, target_row, 0.0), axis=1, keepdims=True)
    same = jnp.where(target_col == target_row, 1.0, 0.0)
    position_row = jnp.sum(jnp.where(rows_b < cols_b, same, 0.0), axis=0, keepdims=True)
    position_col = jnp.sum(jnp.where(cols_b < rows_b, same, 0.0), axis=1, keepdims=True)
    placed_row = target_row[:1] * cap + position_row
    placed_col = target_col * cap + position_col
    slot_col = lax.broadcasted_iota(jnp.int32, (slots, blocks), 0).astype(f32)
    place = jnp.where(slot_col == placed_row, 1.0, 0.0)
    tile_col = jnp.sum(place * tile_ref[...].astype(f32), axis=1, keepdims=True)
    sent_tiles[...] = jnp.broadcast_to(tile_col, (slots, lanes)).reshape(n_wide, cap, lanes)

    beside_z = jnp.where(narrow > 0, 1, 0) + jnp.where(narrow < n_narrow - 1, 1, 0)
    pl.semaphore_wait(barrier, n_wide - 1 + beside_z)

    def passing(phase, source, target, step):
        partner = lax.rem(wide + step, n_wide)
        return pltpu.make_async_remote_copy(
            src_ref=source.at[partner],
            dst_ref=target.at[wide],
            send_sem=send_sem.at[phase, step],
            recv_sem=recv_sem.at[phase, step],
            device_id=(partner, narrow),
            device_id_type=MESH,
        )

    def start_all(phase, source, target):
        def go(step, carry):
            passing(phase, source, target, step).start()
            return carry

        lax.fori_loop(1, n_wide, go, 0)
        target[wide] = source[wide]

    def wait_all(phase, source, target):
        def go(step, carry):
            passing(phase, source, target, step).wait_recv()
            return carry

        lax.fori_loop(1, n_wide, go, 0)

    def end_all(phase, source, target):
        def go(step, carry):
            passing(phase, source, target, step).wait_send()
            return carry

        lax.fori_loop(1, n_wide, go, 0)

    start_all(0, sent_tiles, got_tiles)

    loads[2].wait()
    loads[3].wait()
    volume = volume_ref[...]
    carried = [volume] + [volume * velocity_ref[a] for a in range(3)]
    for k in range(4):
        high = carried[k].astype(bf16).astype(f32)
        low = carried[k] - high
        rows[pl.ds(k, blocks, stride=8), :] = jnp.concatenate([high, high], axis=1)
        rows[pl.ds(4 + k, blocks, stride=8), :] = jnp.concatenate(
            [low, jnp.zeros_like(low)], axis=1
        )
    loads[4].wait()
    group = 8

    def contract(step, carry):
        base = pl.multiple_of(step * group, group)
        weights = kernel_buf[pl.ds(base, group)]
        high, low = split(weights)
        both = jnp.concatenate([high, low], axis=1)
        pieces[pl.ds(base, group)] = both
        at = pl.ds(pl.multiple_of(base * 8, 8), group * 8)
        left = rows[at, :].reshape(group, 8, lanes).astype(bf16)
        out = lax.dot_general(
            left, both, (((2,), (1,)), ((0,), (0,))), preferred_element_type=f32
        )
        rows[at, :] = out.reshape(group * 8, lanes)
        return carry

    lax.fori_loop(0, blocks // group, contract, 0)
    own = [
        split(rows[pl.ds(k, blocks, stride=8), :] + rows[pl.ds(4 + k, blocks, stride=8), :])
        for k in range(4)
    ]
    right = jnp.concatenate(
        [jnp.concatenate([o[0] for o in own], axis=1), jnp.concatenate([o[1] for o in own], axis=1)],
        axis=0,
    )
    place = jnp.concatenate([place, place], axis=1).astype(bf16)
    in_slots = dot(place, right)
    for k in range(4):
        sent[:, k] = in_slots[:, k * lanes : (k + 1) * lanes].reshape(n_wide, cap, lanes)
    start_all(1, sent, got)

    wait_all(0, sent_tiles, got_tiles)
    order = lax.broadcasted_iota(jnp.int32, (slots, tiles), 1)
    x_of, q_of, z_of = order // plane, (order // cz) % nq, order % cz
    tile_of = ((x_of * cz + z_of) * nq + q_of).astype(f32)
    tile_slots = got_tiles[...].reshape(slots, lanes)
    selector = jnp.where(tile_slots == tile_of, 1.0, 0.0)
    turned = jnp.transpose(selector).astype(bf16)
    selector = selector.astype(bf16)
    turned = jnp.concatenate([turned, turned], axis=1)
    selector = jnp.concatenate([selector, selector], axis=1)

    loads[5].wait()
    fluid = [
        jnp.concatenate(
            [
                fluid_ref[a, x, :, q * lanes : (q + 1) * lanes]
                for x in range(cx)
                for q in range(nq)
            ],
            axis=0,
        )
        for a in range(3)
    ]

    wait_all(1, sent, got)
    arrived = [split(got[:, k].reshape(slots, lanes)) for k in range(4)]
    right = jnp.concatenate(
        [jnp.concatenate([o[i] for o in arrived], axis=1) for i in range(2)], axis=0
    )
    spread = dot(turned, right)
    solid = spread[:, :lanes]
    growth = (1.0 + solid) * (1.0 + solid)
    scale = 1.0 / (1.0 + growth * solid)
    provisional = [
        (fluid[a] + growth * spread[:, (a + 1) * lanes : (a + 2) * lanes]) * scale
        for a in range(3)
    ]
    void = 1.0 / (1.0 + solid)
    shape = (cx, nq, cz, lanes)
    stacked = [(void * provisional[a]).reshape(shape) for a in range(3)] + [void.reshape(shape)]

    def sides_of(e, source, source_z, ghost_x, ghost_z, fields):
        count = len(fields)
        high_rows = count * plane
        for x in range(cx):
            for i in range(count):
                source[x, i * plane : (i + 1) * plane, :] = fields[i][x].reshape(plane, lanes)
        for i in range(count):
            for side, z in ((0, 0), (1, cz - 1)):
                for x in range(cx):
                    source_z[side, (x * count + i) * nq : (x * count + i + 1) * nq, :] = fields[i][
                        x, :, z, :
                    ]

        def copies(along, side):
            if along == 0:
                src = source.at[0 if side == 0 else cx - 1]
                dst, to = ghost_x.at[1 - side], (wide + (1 if side else -1), narrow)
            else:
                src, dst = source_z.at[side], ghost_z.at[1 - side]
                to = (wide, narrow + (1 if side else -1))
            return pltpu.make_async_remote_copy(
                src_ref=src,
                dst_ref=dst,
                send_sem=side_send.at[e, along * 2 + side],
                recv_sem=side_recv.at[e, along * 2 + side],
                device_id=to,
                device_id_type=MESH,
            )

        has = (
            (wide > 0, wide < n_wide - 1),
            (narrow > 0, narrow < n_narrow - 1),
        )
        for along in range(2):
            for side in range(2):

                @pl.when(has[along][side])
                def _():
                    copies(along, side).start()

        lane = lax.broadcasted_iota(jnp.int32, shape, 3)
        row = lax.broadcasted_iota(jnp.int32, shape, 2)
        zero = jnp.zeros((cx, 1, cz, lanes), f32)
        in_y = []
        for p in fields:
            up = pltpu.roll(p, lanes - 1, 3)
            down = pltpu.roll(p, 1, 3)
            up = jnp.where(lane == lanes - 1, jnp.concatenate([up[:, 1:], zero], axis=1), up)
            down = jnp.where(lane == 0, jnp.concatenate([zero, down[:, :-1]], axis=1), down)
            in_y.append((up, down))
        for along in range(2):
            for side in range(2):

                @pl.when(has[along][1 - side])
                def _():
                    copies(along, side).wait_recv()

        result = []
        for i, p in enumerate(fields):
            low = ghost_x[0, i * plane : (i + 1) * plane, :].reshape((1,) + shape[1:])
            high = ghost_x[1, i * plane : (i + 1) * plane, :].reshape((1,) + shape[1:])

            def row_ghost(side):
                return jnp.concatenate(
                    [
                        jnp.broadcast_to(
                            ghost_z[side, (x * count + i) * nq + q : (x * count + i) * nq + q + 1, :],
                            (cz, lanes),
                        )
                        for x in range(cx)
                        for q in range(nq)
                    ],
                    axis=0,
                ).reshape(shape)

            z_up = jnp.where(row == cz - 1, row_ghost(1), pltpu.roll(p, cz - 1, 2))
            z_down = jnp.where(row == 0, row_ghost(0), pltpu.roll(p, 1, 2))
            result.append(
                (
                    jnp.concatenate([p[1:], high], axis=0),
                    jnp.concatenate([low, p[:-1]], axis=0),
                    z_up,
                    z_down,
                    in_y[i][0],
                    in_y[i][1],
                )
            )
        for along in range(2):
            for side in range(2):

                @pl.when(has[along][side])
                def _():
                    copies(along, side).wait_send()

        return result

    beside = sides_of(0, first, first_z, first_gx, first_gz, stacked)

    def give_back(values, target, start):
        wide_values = [split(v) for v in values]
        right = jnp.concatenate(
            [jnp.concatenate([o[i] for o in wide_values], axis=1) for i in range(2)], axis=0
        )
        picked = dot(selector, right)
        for k in range(len(values)):
            target[:, start + k] = picked[:, k * lanes : (k + 1) * lanes].reshape(
                n_wide, cap, lanes
            )

    give_back([growth], sent_growth, 0)
    start_all(2, sent_growth, got_growth)

    source = -0.5 * (
        beside[0][0] - beside[0][1] + beside[1][2] - beside[1][3] + beside[2][4] - beside[2][5]
    )
    here_void = stacked[3]
    weights = [0.5 * (here_void + beside[3][i]) for i in range(6)]
    diagonal = weights[0] + weights[1] + weights[2] + weights[3] + weights[4] + weights[5]
    inverse = 1.0 / diagonal
    weights = [w * inverse for w in weights]
    source = source * inverse
    pressure = source
    for sweep in range(SWEEPS):
        around = sides_of(
            1 + sweep,
            press.at[sweep],
            press_z.at[sweep],
            press_gx.at[sweep],
            press_gz.at[sweep],
            [pressure],
        )[0]
        if sweep < SWEEPS - 1:
            total = source
            for i in range(6):
                total = total + weights[i] * around[i]
            pressure = total
    steps = [around[0] - around[1], around[2] - around[3], around[4] - around[5]]
    following = [provisional[a] - 0.5 * steps[a].reshape(tiles, lanes) for a in range(3)]
    give_back([growth * v for v in following], sent_next, 0)
    start_all(3, sent_next, got_next)

    for x in range(cx):
        for q in range(nq):
            cut = slice(q * lanes, (q + 1) * lanes)
            at = (x * nq + q) * cz
            pressure_ref[x, :, cut] = pressure[x, q]
            for a in range(3):
                next_ref[a, x, :, cut] = following[a][at : at + cz]

    slot_row = lax.broadcasted_iota(jnp.int32, (blocks, slots), 1).astype(f32)
    back = jnp.where(slot_row == placed_col, 1.0, 0.0).astype(bf16)

    def place_back(target, k, row):
        high, low = split(target[:, k].reshape(slots, lanes))
        out = dot(back, jnp.concatenate([high, low], axis=1))
        rows[pl.ds(row, blocks, stride=8), :] = out[:, :lanes]
        rows[pl.ds(4 + row, blocks, stride=8), :] = out[:, lanes:]

    wait_all(2, sent_growth, got_growth)
    place_back(got_growth, 0, 3)
    wait_all(3, sent_next, got_next)
    for k in range(3):
        place_back(got_next, k, k)

    def sample(step, carry):
        base = pl.multiple_of(step * group, group)
        at = pl.ds(pl.multiple_of(base * 8, 8), group * 8)
        left = rows[at, :].reshape(group, 8, lanes).astype(bf16)
        out = lax.dot_general(
            left,
            pieces[pl.ds(base, group)],
            (((2,), (2,)), ((0,), (0,))),
            preferred_element_type=f32,
        )
        rows[at, :] = out.reshape(group * 8, lanes)
        return carry

    lax.fori_loop(0, blocks // group, sample, 0)

    def sampled(k):
        top = rows[pl.ds(k, blocks, stride=8), :]
        low = rows[pl.ds(4 + k, blocks, stride=8), :]
        return (top + low)[:, :particles] + pltpu.roll(top, particles, 1)[:, :particles]

    fourth = sampled(3)
    for k in range(3):
        drag_ref[k] = volume * sampled(k) - carried[1 + k] * fourth

    for phase, source, target in (
        (0, sent_tiles, got_tiles),
        (1, sent, got),
        (2, sent_growth, got_growth),
        (3, sent_next, got_next),
    ):
        end_all(phase, source, target)


def hand_over(*refs):
    sources, targets, sems = refs[:3], refs[3:6], refs[6]
    copies = [pltpu.make_async_copy(sources[i], targets[i], sems.at[i]) for i in range(3)]
    for copy in copies:
        copy.start()
    for copy in copies:
        copy.wait()


def solution(mesh):
    n_wide, n_narrow = mesh.shape["wide"], mesh.shape["narrow"]

    def local(kernel, volume, velocity, block_brick, block_tile, fluid_velocity):
        blocks, particles, lanes = kernel.shape
        _, cx, cz, ny = fluid_velocity.shape
        cap = max(2, (2 * blocks + n_wide - 1) // n_wide)
        cap = (cap + 7) // 8 * 8
        nq = ny // lanes
        plane = nq * cz
        vmem = pltpu.VMEM
        any_spec = pl.BlockSpec(memory_space=pl.ANY)
        vmem_spec = pl.BlockSpec(memory_space=pltpu.VMEM)
        flux = [
            vmem((n_wide, cap, lanes), f32),
            vmem((n_wide, cap, lanes), f32),
            vmem((n_wide, 4, cap, lanes), f32),
            vmem((n_wide, 4, cap, lanes), f32),
            vmem((n_wide, 1, cap, lanes), f32),
            vmem((n_wide, 1, cap, lanes), f32),
            vmem((n_wide, 3, cap, lanes), f32),
            vmem((n_wide, 3, cap, lanes), f32),
        ]
        halo = [
            vmem((cx, 4 * plane, lanes), f32),
            vmem((2, 4 * cx * nq, lanes), f32),
            vmem((2, 4 * plane, lanes), f32),
            vmem((2, 4 * cx * nq, lanes), f32),
            vmem((SWEEPS, cx, plane, lanes), f32),
            vmem((SWEEPS, 2, cx * nq, lanes), f32),
            vmem((SWEEPS, 2, plane, lanes), f32),
            vmem((SWEEPS, 2, cx * nq, lanes), f32),
        ]
        drag, pressure, following = pl.pallas_call(
            functools.partial(body, n_wide, n_narrow, cap),
            out_shape=(
                jax.ShapeDtypeStruct((3, blocks, particles), f32),
                jax.ShapeDtypeStruct((cx, cz, ny), f32),
                jax.ShapeDtypeStruct((3, cx, cz, ny), f32),
            ),
            in_specs=[any_spec] * 6,
            out_specs=(vmem_spec,) * 3,
            scratch_shapes=[
                vmem((blocks, particles, lanes), f32),
                vmem((blocks, particles), f32),
                vmem((3, blocks, particles), f32),
                vmem((1, blocks), jnp.int32),
                vmem((1, blocks), jnp.int32),
                vmem((3, cx, cz, ny), f32),
                vmem((blocks, 2 * particles, lanes), bf16),
                vmem((blocks * 8, lanes), f32),
            ]
            + flux
            + halo
            + [
                pltpu.SemaphoreType.DMA((6,)),
                pltpu.SemaphoreType.DMA((4, n_wide)),
                pltpu.SemaphoreType.DMA((4, n_wide)),
                pltpu.SemaphoreType.DMA((SWEEPS + 1, 4)),
                pltpu.SemaphoreType.DMA((SWEEPS + 1, 4)),
            ],
            compiler_params=pltpu.CompilerParams(
                collective_id=0, has_side_effects=True, vmem_limit_bytes=60 * 1024 * 1024
            ),
        )(
            kernel,
            volume,
            jnp.transpose(velocity, (1, 0, 2)),
            block_brick.reshape(1, blocks),
            block_tile.reshape(1, blocks),
            fluid_velocity,
        )
        results = (drag, pressure, following)
        drag, pressure, following = pl.pallas_call(
            hand_over,
            out_shape=tuple(jax.ShapeDtypeStruct(r.shape, r.dtype) for r in results),
            in_specs=[any_spec] * 3,
            out_specs=(any_spec,) * 3,
            scratch_shapes=[pltpu.SemaphoreType.DMA((3,))],
        )(*results)
        return jnp.transpose(drag, (1, 0, 2)), pressure, following

    return jax.shard_map(
        local,
        mesh=mesh,
        in_specs=(
            P(("wide", "narrow"), None, None),
            P(("wide", "narrow"), None),
            P(("wide", "narrow"), None, None),
            P(("wide", "narrow"), None),
            P(("wide", "narrow")),
            P(None, "wide", "narrow", None),
        ),
        out_specs=(
            P(("wide", "narrow"), None, None),
            P("wide", "narrow", None),
            P(None, "wide", "narrow", None),
        ),
        check_vma=False,
    )
```

```python
import functools

import jax
import jax.numpy as jnp
from jax import lax
from jax.experimental import pallas as pl
from jax.experimental.pallas import tpu as pltpu
from jax.sharding import PartitionSpec as P

SWEEPS = 6
DEPTH = 3
DIRECTIONS = ((-1, 0), (1, 0), (0, -1), (0, 1), (-1, -1), (-1, 1), (1, -1), (1, 1))
MESH = pl.DeviceIdType.MESH
f32 = jnp.float32
bf16 = jnp.bfloat16


def split(value):
    high = value.astype(bf16)
    return high, (value - high.astype(f32)).astype(bf16)


def dot(a, b):
    return jnp.dot(a, b, preferred_element_type=f32)


def body(
    n_wide, n_narrow, cap,
    kernel_hbm, volume_hbm, velocity_hbm, brick_hbm, tile_hbm, fluid_hbm,
    drag_ref, pressure_ref, next_ref,
    kernel_buf, volume_ref, velocity_ref, brick_ref, tile_ref, fluid_ref, pieces, rows, sent_tiles, got_tiles, sent, got,
    sent_growth, got_growth, sent_next, got_next,
    near_x, near_gx, near_z, near_gz, deep, deep_gx, deep_gz, corner, corner_g,
    load_sem, send_sem, recv_sem, side_send, side_recv,
):
    wide, narrow = lax.axis_index("wide"), lax.axis_index("narrow")
    blocks, particles, lanes = kernel_buf.shape
    _, cx, cz, ny = fluid_ref.shape
    nq = ny // lanes
    plane = nq * cz
    tiles = cx * plane
    slots = n_wide * cap

    loads = [
        pltpu.make_async_copy(here, there, load_sem.at[i])
        for i, (here, there) in enumerate(
            (
                (brick_hbm, brick_ref),
                (tile_hbm, tile_ref),
                (volume_hbm, volume_ref),
                (velocity_hbm, velocity_ref),
                (kernel_hbm, kernel_buf),
                (fluid_hbm, fluid_ref),
            )
        )
    ]
    for load in loads:
        load.start()

    barrier = pltpu.get_barrier_semaphore()

    def greet(step, carry):
        pl.semaphore_signal(
            barrier, inc=1, device_id=(lax.rem(wide + step, n_wide), narrow), device_id_type=MESH
        )
        return carry

    lax.fori_loop(1, n_wide, greet, 0)
    z_tiles = near_gz.shape[0] + 1

    def exists(dx, dz):
        inside = (wide + dx >= 0) & (wide + dx < n_wide)
        return inside & (narrow + dz >= 0) & (narrow + dz < n_narrow)

    for dx, dz in DIRECTIONS:
        if dz:

            @pl.when(exists(dx, dz))
            def _():
                pl.semaphore_signal(
                    barrier, inc=1, device_id=(wide + dx, narrow + dz), device_id_type=MESH
                )

    def lands_x(dx):
        return 0 if dx > 0 else 1

    def lands_z(dz):
        return 0 if dz > 0 or z_tiles == 2 else 1

    for dx, dz in DIRECTIONS:
        if dz and z_tiles == 2:
            absent = jnp.logical_not(exists(-dx, 0)) if dx else None
            if dx and dz < 0:
                continue
        else:
            absent = jnp.logical_not(exists(-dx, -dz))
        if absent is None:
            continue

        @pl.when(absent)
        def _():
            events = deep.shape[0]
            if dz == 0:
                near_gx[lands_x(dx)] = jnp.zeros(near_gx.shape[1:], f32)
                for e in range(events):
                    deep_gx[e, lands_x(dx)] = jnp.zeros(deep_gx.shape[2:], f32)
            elif dx == 0:
                near_gz[lands_z(dz)] = jnp.zeros(near_gz.shape[1:], f32)
                for e in range(events):
                    deep_gz[e, lands_z(dz)] = jnp.zeros(deep_gz.shape[2:], f32)
            else:
                for e in range(events):
                    corner_g[e, lands_x(dx), lands_z(dz)] = jnp.zeros(corner_g.shape[3:], f32)

    loads[0].wait()
    loads[1].wait()
    rows_b = lax.broadcasted_iota(jnp.int32, (blocks, blocks), 0)
    cols_b = lax.broadcasted_iota(jnp.int32, (blocks, blocks), 1)
    target_row = jnp.broadcast_to(brick_ref[...].astype(f32), (blocks, blocks))
    target_col = jnp.sum(jnp.where(rows_b == cols_b, target_row, 0.0), axis=1, keepdims=True)
    same = jnp.where(target_col == target_row, 1.0, 0.0)
    position_row = jnp.sum(jnp.where(rows_b < cols_b, same, 0.0), axis=0, keepdims=True)
    position_col = jnp.sum(jnp.where(cols_b < rows_b, same, 0.0), axis=1, keepdims=True)
    placed_row = target_row[:1] * cap + position_row
    placed_col = target_col * cap + position_col
    slot_col = lax.broadcasted_iota(jnp.int32, (slots, blocks), 0).astype(f32)
    place = jnp.where(slot_col == placed_row, 1.0, 0.0)
    tile_col = jnp.sum(place * tile_ref[...].astype(f32), axis=1, keepdims=True)
    sent_tiles[...] = jnp.broadcast_to(tile_col, (slots, lanes)).reshape(n_wide, cap, lanes)

    beside_x = jnp.where(wide > 0, 1, 0) + jnp.where(wide < n_wide - 1, 1, 0)
    beside_z = jnp.where(narrow > 0, 1, 0) + jnp.where(narrow < n_narrow - 1, 1, 0)
    pl.semaphore_wait(barrier, n_wide - 1 + beside_z * (1 + beside_x))

    def passing(phase, source, target, step):
        partner = lax.rem(wide + step, n_wide)
        return pltpu.make_async_remote_copy(
            src_ref=source.at[partner],
            dst_ref=target.at[wide],
            send_sem=send_sem.at[phase, step],
            recv_sem=recv_sem.at[phase, step],
            device_id=(partner, narrow),
            device_id_type=MESH,
        )

    def start_all(phase, source, target):
        def go(step, carry):
            passing(phase, source, target, step).start()
            return carry

        lax.fori_loop(1, n_wide, go, 0)
        target[wide] = source[wide]

    def wait_all(phase, source, target):
        def go(step, carry):
            passing(phase, source, target, step).wait_recv()
            return carry

        lax.fori_loop(1, n_wide, go, 0)

    def end_all(phase, source, target):
        def go(step, carry):
            passing(phase, source, target, step).wait_send()
            return carry

        lax.fori_loop(1, n_wide, go, 0)

    start_all(0, sent_tiles, got_tiles)

    loads[2].wait()
    loads[3].wait()
    volume = volume_ref[...]
    carried = [volume] + [volume * velocity_ref[a] for a in range(3)]
    for k in range(4):
        high = carried[k].astype(bf16).astype(f32)
        low = carried[k] - high
        rows[pl.ds(k, blocks, stride=8), :] = jnp.concatenate([high, high], axis=1)
        rows[pl.ds(4 + k, blocks, stride=8), :] = jnp.concatenate(
            [low, jnp.zeros_like(low)], axis=1
        )
    loads[4].wait()
    group = 8

    def contract(step, carry):
        base = pl.multiple_of(step * group, group)
        weights = kernel_buf[pl.ds(base, group)]
        high, low = split(weights)
        both = jnp.concatenate([high, low], axis=1)
        pieces[pl.ds(base, group)] = both
        at = pl.ds(pl.multiple_of(base * 8, 8), group * 8)
        left = rows[at, :].reshape(group, 8, lanes).astype(bf16)
        out = lax.dot_general(
            left, both, (((2,), (1,)), ((0,), (0,))), preferred_element_type=f32
        )
        rows[at, :] = out.reshape(group * 8, lanes)
        return carry

    lax.fori_loop(0, blocks // group, contract, 0)
    own = [
        split(rows[pl.ds(k, blocks, stride=8), :] + rows[pl.ds(4 + k, blocks, stride=8), :])
        for k in range(4)
    ]
    right = jnp.concatenate(
        [jnp.concatenate([o[0] for o in own], axis=1), jnp.concatenate([o[1] for o in own], axis=1)],
        axis=0,
    )
    place = jnp.concatenate([place, place], axis=1).astype(bf16)
    in_slots = dot(place, right)
    for k in range(4):
        sent[:, k] = in_slots[:, k * lanes : (k + 1) * lanes].reshape(n_wide, cap, lanes)
    start_all(1, sent, got)

    wait_all(0, sent_tiles, got_tiles)
    order = lax.broadcasted_iota(jnp.int32, (slots, tiles), 1)
    x_of, q_of, z_of = order // plane, (order // cz) % nq, order % cz
    tile_of = ((x_of * cz + z_of) * nq + q_of).astype(f32)
    tile_slots = got_tiles[...].reshape(slots, lanes)
    selector = jnp.where(tile_slots == tile_of, 1.0, 0.0)
    turned = jnp.transpose(selector).astype(bf16)
    selector = selector.astype(bf16)
    turned = jnp.concatenate([turned, turned], axis=1)
    selector = jnp.concatenate([selector, selector], axis=1)

    loads[5].wait()
    fluid = [
        jnp.concatenate(
            [
                fluid_ref[a, x, :, q * lanes : (q + 1) * lanes]
                for x in range(cx)
                for q in range(nq)
            ],
            axis=0,
        )
        for a in range(3)
    ]

    wait_all(1, sent, got)
    arrived = [split(got[:, k].reshape(slots, lanes)) for k in range(4)]
    right = jnp.concatenate(
        [jnp.concatenate([o[i] for o in arrived], axis=1) for i in range(2)], axis=0
    )
    spread = dot(turned, right)
    solid = spread[:, :lanes]
    growth = (1.0 + solid) * (1.0 + solid)
    scale = 1.0 / (1.0 + growth * solid)
    provisional = [
        (fluid[a] + growth * spread[:, (a + 1) * lanes : (a + 2) * lanes]) * scale
        for a in range(3)
    ]
    void = 1.0 / (1.0 + solid)
    shape = (nq, cz, lanes)

    def planes_of(value):
        return [value[x * plane : (x + 1) * plane].reshape(shape) for x in range(cx)]

    own_flux = [planes_of(void * provisional[a]) for a in range(3)]
    own_void = planes_of(void)

    def give_back(values, target, start):
        wide_values = [split(v) for v in values]
        right = jnp.concatenate(
            [jnp.concatenate([o[i] for o in wide_values], axis=1) for i in range(2)], axis=0
        )
        picked = dot(selector, right)
        for k in range(len(values)):
            target[:, start + k] = picked[:, k * lanes : (k + 1) * lanes].reshape(
                n_wide, cap, lanes
            )


    def ship(e, i, src, dst):
        dx, dz = DIRECTIONS[i]
        return pltpu.make_async_remote_copy(
            src_ref=src,
            dst_ref=dst,
            send_sem=side_send.at[e, i],
            recv_sem=side_recv.at[e, i],
            device_id=(wide + dx, narrow + dz),
            device_id_type=MESH,
        )

    def near_copy(i):
        dx, dz = DIRECTIONS[i]
        if dz == 0:
            return ship(0, i, near_x.at[0 if dx < 0 else 1], near_gx.at[lands_x(dx)])
        return ship(0, i, near_z, near_gz.at[lands_z(dz)])

    def deep_copy(e, i):
        dx, dz = DIRECTIONS[i]
        if dz == 0:
            start = 0 if dx < 0 else cx - DEPTH
            return ship(
                e + 1, i, deep.at[e, pl.ds(start, DEPTH)], deep_gx.at[e, lands_x(dx)]
            )
        if dx == 0:
            return ship(e + 1, i, deep.at[e], deep_gz.at[e, lands_z(dz)])
        return ship(
            e + 1,
            i,
            corner.at[e, 0 if dx < 0 else 1, 0 if dz < 0 else 1],
            corner_g.at[e, lands_x(dx), lands_z(dz)],
        )

    def each(directions, make, act, receiving=False):
        for i in directions:
            dx, dz = DIRECTIONS[i]

            @pl.when(exists(-dx, -dz) if receiving else exists(dx, dz))
            def _():
                getattr(make(i), act)()

    corner_spots = [(d, r) for d in range(1, DEPTH) for r in range(1, DEPTH + 1 - d)]

    def store_deep(e, planes):
        for x in range(cx):
            deep[e, x] = planes[x].reshape(plane, lanes)
        for sx in range(2):
            for sz in range(2):
                for n, (d, r) in enumerate(corner_spots):
                    x = d - 1 if sx == 0 else cx - d
                    z = r - 1 if sz == 0 else cz - r
                    corner[e, sx, sz, n * nq : (n + 1) * nq, :] = planes[x][:, z, :]

    row = lax.broadcasted_iota(jnp.int32, shape, 1)

    def tiles_from(own, others):
        if z_tiles == 2:
            first = narrow == 0
            return jnp.stack([jnp.where(first, own, others[0]), jnp.where(first, others[0], own)])
        return jnp.stack([others[0], own, others[1]])

    def own_of(value):
        if z_tiles == 2:
            return jnp.where(narrow == 0, value[0], value[1])
        return value[1]

    def corner_tile(e, side, which, d):
        tile = jnp.zeros(shape, f32)
        for n, (far, r) in enumerate(corner_spots):
            if far != d:
                continue
            spread_rows = jnp.stack(
                [
                    jnp.broadcast_to(
                        corner_g[e, side, which, n * nq + q : n * nq + q + 1, :], (cz, lanes)
                    )
                    for q in range(nq)
                ]
            )
            if z_tiles == 2:
                at = jnp.where(narrow == 0, r - 1, cz - r)
            else:
                at = cz - r if which == 0 else r - 1
            tile = jnp.where(row == at, spread_rows, tile)
        return tile

    def extended(e, planes):
        result = {}
        for x in range(cx):
            others = [deep_gz[e, t, x].reshape(shape) for t in range(z_tiles - 1)]
            result[x] = tiles_from(planes[x], others)
        for side in range(2):
            for d in range(1, DEPTH + 1):
                own = deep_gx[e, side, DEPTH - d if side == 0 else d - 1].reshape(shape)
                others = [corner_tile(e, side, t, d) for t in range(z_tiles - 1)]
                result[-d if side == 0 else cx - 1 + d] = tiles_from(own, others)
        return result

    def along_y(p):
        last = p.ndim - 1
        lane = lax.broadcasted_iota(jnp.int32, p.shape, last)
        up, down = pltpu.roll(p, lanes - 1, last), pltpu.roll(p, 1, last)
        if p.ndim == 4:
            zero = jnp.zeros_like(p[:, :1])
            next_up = jnp.concatenate([up[:, 1:], zero], axis=1)
            next_down = jnp.concatenate([zero, down[:, :-1]], axis=1)
        else:
            zero = jnp.zeros_like(p[:1])
            next_up = jnp.concatenate([up[1:], zero], axis=0)
            next_down = jnp.concatenate([zero, down[:-1]], axis=0)
        return jnp.where(lane == lanes - 1, next_up, up), jnp.where(lane == 0, next_down, down)

    def along_z(p):
        at = lax.broadcasted_iota(jnp.int32, p.shape, 2)
        up, down = pltpu.roll(p, cz - 1, 2), pltpu.roll(p, 1, 2)
        zero = jnp.zeros_like(p[:1])
        next_up = jnp.concatenate([up[1:], zero], axis=0)
        next_down = jnp.concatenate([zero, down[:-1]], axis=0)
        return jnp.where(at == cz - 1, next_up, up), jnp.where(at == 0, next_down, down)

    for side, x in ((0, 0), (1, cx - 1)):
        near_x[side, 0] = own_flux[0][x].reshape(plane, lanes)
        near_x[side, 1] = own_void[x].reshape(plane, lanes)
    for x in range(cx):
        near_z[0, x] = own_flux[1][x].reshape(plane, lanes)
        near_z[1, x] = own_void[x].reshape(plane, lanes)
    each((0, 1, 2, 3), near_copy, "start")
    store_deep(0, own_void)
    each((0, 1, 4, 5, 6, 7), lambda i: deep_copy(0, i), "start")

    void_y = [along_y(v) for v in own_void]
    flux_y = [along_y(v) for v in own_flux[2]]
    each((0, 1, 2, 3), near_copy, "wait_recv", True)

    def with_ghosts(planes, field):
        low = near_gx[0, field].reshape(shape)
        high = near_gx[1, field].reshape(shape)
        return [low] + planes + [high]

    flux_x, void_x = with_ghosts(own_flux[0], 0), with_ghosts(own_void, 1)
    void_inner, pressure = [], []
    for x in range(cx):
        flux_z, void_z = [
            tiles_from(own[x], [near_gz[t, field, x].reshape(shape) for t in range(z_tiles - 1)])
            for field, own in ((0, own_flux[1]), (1, own_void))
        ]
        void_inner.append(void_z)
        flux_up, flux_down = [own_of(v) for v in along_z(flux_z)]
        void_up, void_down = [own_of(v) for v in along_z(void_z)]
        source = -0.5 * (
            flux_x[x + 2] - flux_x[x] + flux_up - flux_down + flux_y[x][0] - flux_y[x][1]
        )
        around = void_x[x + 2] + void_x[x] + void_up + void_down + void_y[x][0] + void_y[x][1]
        pressure.append(source / (0.5 * (6.0 * own_void[x] + around)))

    def start_pressure(e, planes):
        store_deep(e, planes)
        each(range(8), lambda i: deep_copy(e, i), "start")

    def wait_pressure(e, planes):
        each(range(8), lambda i: deep_copy(e, i), "wait_recv", True)
        return extended(e, planes)

    start_pressure(1, pressure)
    give_back([growth], sent_growth, 0)
    start_all(2, sent_growth, got_growth)

    each((0, 1, 4, 5, 6, 7), lambda i: deep_copy(0, i), "wait_recv", True)
    shares = {x: void_inner[x] for x in range(cx)}
    for side in range(2):
        for d in range(1, DEPTH + 1):
            own = deep_gx[0, side, DEPTH - d if side == 0 else d - 1].reshape(shape)
            others = [corner_tile(0, side, t, d) for t in range(z_tiles - 1)]
            shares[-d if side == 0 else cx - 1 + d] = tiles_from(own, others)
    weights = {}
    for x in range(1 - DEPTH, cx + DEPTH - 1):
        here = shares[x]
        nearby = (shares[x + 1], shares[x - 1]) + along_z(here) + along_y(here)
        sums = [here + v for v in nearby]
        total = sums[0] + sums[1] + sums[2] + sums[3] + sums[4] + sums[5]
        factor = jnp.where(here > 0.0, 1.0 / total, 0.0)
        weights[x] = [v * factor for v in sums]

    event = 1
    current = wait_pressure(event, pressure)
    begun = current
    radius = DEPTH
    for sweep in range(SWEEPS - 1):
        if radius == 0:
            event += 1
            pressure = [own_of(current[x]) for x in range(cx)]
            start_pressure(event, pressure)
            current = wait_pressure(event, pressure)
            radius = DEPTH
        radius -= 1
        later = {}
        for x in range(-radius, cx + radius):
            p, w = current[x], weights[x]
            z_up, z_down = along_z(p)
            y_up, y_down = along_y(p)
            later[x] = (
                begun[x]
                + (w[0] * current[x + 1] + w[1] * current[x - 1])
                + (w[2] * z_up + w[3] * z_down)
                + (w[4] * y_up + w[5] * y_down)
            )
        current = later
    pressure = [own_of(current[x]) for x in range(cx)]
    steps = [[], [], []]
    for x in range(cx):
        z_up, z_down = along_z(current[x])
        y_up, y_down = along_y(pressure[x])
        steps[0].append(own_of(current[x + 1]) - own_of(current[x - 1]))
        steps[1].append(own_of(z_up) - own_of(z_down))
        steps[2].append(y_up - y_down)
    following = [
        provisional[a] - 0.5 * jnp.concatenate(steps[a], axis=0).reshape(tiles, lanes)
        for a in range(3)
    ]
    give_back([growth * v for v in following], sent_next, 0)
    start_all(3, sent_next, got_next)

    for x in range(cx):
        for q in range(nq):
            cut = slice(q * lanes, (q + 1) * lanes)
            at = (x * nq + q) * cz
            pressure_ref[x, :, cut] = pressure[x][q]
            for a in range(3):
                next_ref[a, x, :, cut] = following[a][at : at + cz]

    slot_row = lax.broadcasted_iota(jnp.int32, (blocks, slots), 1).astype(f32)
    back = jnp.where(slot_row == placed_col, 1.0, 0.0).astype(bf16)

    def place_back(target, k, row):
        high, low = split(target[:, k].reshape(slots, lanes))
        out = dot(back, jnp.concatenate([high, low], axis=1))
        rows[pl.ds(row, blocks, stride=8), :] = out[:, :lanes]
        rows[pl.ds(4 + row, blocks, stride=8), :] = out[:, lanes:]

    wait_all(2, sent_growth, got_growth)
    place_back(got_growth, 0, 3)
    wait_all(3, sent_next, got_next)
    for k in range(3):
        place_back(got_next, k, k)

    def sample(step, carry):
        base = pl.multiple_of(step * group, group)
        at = pl.ds(pl.multiple_of(base * 8, 8), group * 8)
        left = rows[at, :].reshape(group, 8, lanes).astype(bf16)
        out = lax.dot_general(
            left,
            pieces[pl.ds(base, group)],
            (((2,), (2,)), ((0,), (0,))),
            preferred_element_type=f32,
        )
        rows[at, :] = out.reshape(group * 8, lanes)
        return carry

    lax.fori_loop(0, blocks // group, sample, 0)

    def sampled(k):
        top = rows[pl.ds(k, blocks, stride=8), :]
        low = rows[pl.ds(4 + k, blocks, stride=8), :]
        return (top + low)[:, :particles] + pltpu.roll(top, particles, 1)[:, :particles]

    fourth = sampled(3)
    for k in range(3):
        drag_ref[k] = volume * sampled(k) - carried[1 + k] * fourth

    for phase, source, target in (
        (0, sent_tiles, got_tiles),
        (1, sent, got),
        (2, sent_growth, got_growth),
        (3, sent_next, got_next),
    ):
        end_all(phase, source, target)
    each((0, 1, 2, 3), near_copy, "wait_send")
    each((0, 1, 4, 5, 6, 7), lambda i: deep_copy(0, i), "wait_send")
    for e in range(1, event + 1):
        each(range(8), lambda i: deep_copy(e, i), "wait_send")


def solution(mesh):
    n_wide, n_narrow = mesh.shape["wide"], mesh.shape["narrow"]

    def local(kernel, volume, velocity, block_brick, block_tile, fluid_velocity):
        blocks, particles, lanes = kernel.shape
        _, cx, cz, ny = fluid_velocity.shape
        cap = max(2, (2 * blocks + n_wide - 1) // n_wide)
        cap = (cap + 7) // 8 * 8
        nq = ny // lanes
        plane = nq * cz
        vmem = pltpu.VMEM
        hbm_spec = pl.BlockSpec(memory_space=pl.ANY)
        vmem_spec = pl.BlockSpec(memory_space=pltpu.VMEM)
        flux = [
            vmem((n_wide, cap, lanes), f32),
            vmem((n_wide, cap, lanes), f32),
            vmem((n_wide, 4, cap, lanes), f32),
            vmem((n_wide, 4, cap, lanes), f32),
            vmem((n_wide, 1, cap, lanes), f32),
            vmem((n_wide, 1, cap, lanes), f32),
            vmem((n_wide, 3, cap, lanes), f32),
            vmem((n_wide, 3, cap, lanes), f32),
        ]
        events = 2 + (SWEEPS - 1) // DEPTH
        others = 1 if n_narrow == 2 else 2
        corner_rows = (DEPTH * (DEPTH - 1) // 2 * nq + 7) // 8 * 8
        halo = [
            vmem((2, 2, plane, lanes), f32),
            vmem((2, 2, plane, lanes), f32),
            vmem((2, cx, plane, lanes), f32),
            vmem((others, 2, cx, plane, lanes), f32),
            vmem((events, cx, plane, lanes), f32),
            vmem((events, 2, DEPTH, plane, lanes), f32),
            vmem((events, others, cx, plane, lanes), f32),
            vmem((events, 2, 2, corner_rows, lanes), f32),
            vmem((events, 2, others, corner_rows, lanes), f32),
        ]
        drag, pressure, following = pl.pallas_call(
            functools.partial(body, n_wide, n_narrow, cap),
            out_shape=(
                jax.ShapeDtypeStruct((3, blocks, particles), f32),
                jax.ShapeDtypeStruct((cx, cz, ny), f32),
                jax.ShapeDtypeStruct((3, cx, cz, ny), f32),
            ),
            in_specs=[hbm_spec] * 6,
            out_specs=(vmem_spec,) * 3,
            scratch_shapes=[
                vmem((blocks, particles, lanes), f32),
                vmem((blocks, particles), f32),
                vmem((3, blocks, particles), f32),
                vmem((1, blocks), jnp.int32),
                vmem((1, blocks), jnp.int32),
                vmem((3, cx, cz, ny), f32),
                vmem((blocks, 2 * particles, lanes), bf16),
                vmem((blocks * 8, lanes), f32),
            ]
            + flux
            + halo
            + [
                pltpu.SemaphoreType.DMA((6,)),
                pltpu.SemaphoreType.DMA((4, n_wide)),
                pltpu.SemaphoreType.DMA((4, n_wide)),
                pltpu.SemaphoreType.DMA((events + 1, 8)),
                pltpu.SemaphoreType.DMA((events + 1, 8)),
            ],
            compiler_params=pltpu.CompilerParams(
                collective_id=0, has_side_effects=True, vmem_limit_bytes=60 * 1024 * 1024
            ),
        )(
            kernel,
            volume,
            jnp.transpose(velocity, (1, 0, 2)),
            block_brick.reshape(1, blocks),
            block_tile.reshape(1, blocks),
            fluid_velocity,
        )
        return jnp.transpose(drag, (1, 0, 2)), pressure, following

    return jax.shard_map(
        local,
        mesh=mesh,
        in_specs=(
            P(("wide", "narrow"), None, None),
            P(("wide", "narrow"), None),
            P(("wide", "narrow"), None, None),
            P(("wide", "narrow"), None),
            P(("wide", "narrow")),
            P(None, "wide", "narrow", None),
        ),
        out_specs=(
            P(("wide", "narrow"), None, None),
            P("wide", "narrow", None),
            P(None, "wide", "narrow", None),
        ),
        check_vma=False,
    )
```

```python
import functools

import jax
import jax.numpy as jnp
from jax import lax
from jax.experimental import pallas as pl
from jax.experimental.pallas import tpu as pltpu
from jax.sharding import PartitionSpec as P

SWEEPS = 6
DEPTH = 3
DIRECTIONS = ((-1, 0), (1, 0), (0, -1), (0, 1), (-1, -1), (-1, 1), (1, -1), (1, 1))
MESH = pl.DeviceIdType.MESH
f32 = jnp.float32
bf16 = jnp.bfloat16


def split(value):
    high = value.astype(bf16)
    return high, (value - high.astype(f32)).astype(bf16)


def dot(a, b):
    return jnp.dot(a, b, preferred_element_type=f32)


def body(
    n_wide, n_narrow, cap,
    kernel_hbm, volume_hbm, velocity_hbm, brick_hbm, tile_hbm, fluid_hbm,
    drag_ref, pressure_ref, next_ref,
    kernel_buf, volume_ref, velocity_ref, brick_ref, tile_ref, fluid_ref, pieces, rows, sent_tiles, got_tiles, sent, got,
    sent_growth, got_growth, sent_next, got_next,
    near_x, near_gx, near_z, near_gz, deep, deep_gx, deep_gz, corner, corner_g,
    load_sem, send_sem, recv_sem, side_send, side_recv,
):
    wide, narrow = lax.axis_index("wide"), lax.axis_index("narrow")
    blocks, particles, lanes = kernel_buf.shape
    _, cx, cz, ny = fluid_ref.shape
    nq = ny // lanes
    plane = nq * cz
    tiles = cx * plane
    slots = n_wide * cap

    loads = [
        pltpu.make_async_copy(here, there, load_sem.at[i])
        for i, (here, there) in enumerate(
            (
                (brick_hbm, brick_ref),
                (tile_hbm, tile_ref),
                (volume_hbm, volume_ref),
                (velocity_hbm, velocity_ref),
                (kernel_hbm, kernel_buf),
                (fluid_hbm, fluid_ref),
            )
        )
    ]
    for load in loads:
        load.start()

    barrier = pltpu.get_barrier_semaphore()

    def greet(step, carry):
        pl.semaphore_signal(
            barrier, inc=1, device_id=(lax.rem(wide + step, n_wide), narrow), device_id_type=MESH
        )
        return carry

    lax.fori_loop(1, n_wide, greet, 0)
    z_tiles = near_gz.shape[0] + 1

    def exists(dx, dz):
        inside = (wide + dx >= 0) & (wide + dx < n_wide)
        return inside & (narrow + dz >= 0) & (narrow + dz < n_narrow)

    for dx, dz in DIRECTIONS:
        if dz:

            @pl.when(exists(dx, dz))
            def _():
                pl.semaphore_signal(
                    barrier, inc=1, device_id=(wide + dx, narrow + dz), device_id_type=MESH
                )

    def lands_x(dx):
        return 0 if dx > 0 else 1

    def lands_z(dz):
        return 0 if dz > 0 or z_tiles == 2 else 1

    for dx, dz in DIRECTIONS:
        if dz and z_tiles == 2:
            absent = jnp.logical_not(exists(-dx, 0)) if dx else None
            if dx and dz < 0:
                continue
        else:
            absent = jnp.logical_not(exists(-dx, -dz))
        if absent is None:
            continue

        @pl.when(absent)
        def _():
            events = deep.shape[0]
            if dz == 0:
                near_gx[lands_x(dx)] = jnp.zeros(near_gx.shape[1:], f32)
                for e in range(events):
                    deep_gx[e, lands_x(dx)] = jnp.zeros(deep_gx.shape[2:], f32)
            elif dx == 0:
                near_gz[lands_z(dz)] = jnp.zeros(near_gz.shape[1:], f32)
                for e in range(events):
                    deep_gz[e, lands_z(dz)] = jnp.zeros(deep_gz.shape[2:], f32)
            else:
                for e in range(events):
                    corner_g[e, lands_x(dx), lands_z(dz)] = jnp.zeros(corner_g.shape[3:], f32)

    loads[0].wait()
    loads[1].wait()
    rows_b = lax.broadcasted_iota(jnp.int32, (blocks, blocks), 0)
    cols_b = lax.broadcasted_iota(jnp.int32, (blocks, blocks), 1)
    target_row = jnp.broadcast_to(brick_ref[...].astype(f32), (blocks, blocks))
    target_col = jnp.sum(jnp.where(rows_b == cols_b, target_row, 0.0), axis=1, keepdims=True)
    same = jnp.where(target_col == target_row, 1.0, 0.0)
    position_row = jnp.sum(jnp.where(rows_b < cols_b, same, 0.0), axis=0, keepdims=True)
    position_col = jnp.sum(jnp.where(cols_b < rows_b, same, 0.0), axis=1, keepdims=True)
    placed_row = target_row[:1] * cap + position_row
    placed_col = target_col * cap + position_col
    slot_col = lax.broadcasted_iota(jnp.int32, (slots, blocks), 0).astype(f32)
    place = jnp.where(slot_col == placed_row, 1.0, 0.0)
    named = lax.broadcasted_iota(jnp.int32, (n_wide, blocks), 0).astype(f32) == target_row[:1]
    named = jnp.where(named, tile_ref[...].astype(f32), 0.0)
    at_lane = lax.broadcasted_iota(jnp.int32, (blocks, lanes), 1).astype(f32) == position_col
    at_lane = jnp.where(at_lane, 1.0, 0.0).astype(bf16)
    high, low = split(named)
    sent_tiles[...] = (dot(high, at_lane) + dot(low, at_lane)).reshape(n_wide, 1, lanes)

    def passing(phase, source, target, step):
        partner = lax.rem(wide + step, n_wide)
        return pltpu.make_async_remote_copy(
            src_ref=source.at[partner],
            dst_ref=target.at[wide],
            send_sem=send_sem.at[phase, step],
            recv_sem=recv_sem.at[phase, step],
            device_id=(partner, narrow),
            device_id_type=MESH,
        )

    def start_all(phase, source, target):
        def go(turn, carry):
            far = (turn + 1) // 2
            step = n_wide // 2 + far * (2 * (turn % 2) - 1)
            passing(phase, source, target, step).start()
            return carry

        lax.fori_loop(0, n_wide - 1, go, 0)
        target[wide] = source[wide]

    def wait_all(phase, source, target):
        def go(step, carry):
            passing(phase, source, target, step).wait_recv()
            return carry

        lax.fori_loop(1, n_wide, go, 0)

    def end_all(phase, source, target):
        def go(step, carry):
            passing(phase, source, target, step).wait_send()
            return carry

        lax.fori_loop(1, n_wide, go, 0)

    loads[2].wait()
    loads[3].wait()
    volume = volume_ref[...]
    carried = [volume] + [volume * velocity_ref[a] for a in range(3)]
    for k in range(4):
        high = carried[k].astype(bf16).astype(f32)
        low = carried[k] - high
        rows[pl.ds(k, blocks, stride=8), :] = jnp.concatenate([high, high], axis=1)
        rows[pl.ds(4 + k, blocks, stride=8), :] = jnp.concatenate(
            [low, jnp.zeros_like(low)], axis=1
        )
    loads[4].wait()
    group = 8

    def contract(step, carry):
        base = pl.multiple_of(step * group, group)
        weights = kernel_buf[pl.ds(base, group)]
        high, low = split(weights)
        both = jnp.concatenate([high, low], axis=1)
        pieces[pl.ds(base, group)] = both
        at = pl.ds(pl.multiple_of(base * 8, 8), group * 8)
        left = rows[at, :].reshape(group, 8, lanes).astype(bf16)
        out = lax.dot_general(
            left, both, (((2,), (1,)), ((0,), (0,))), preferred_element_type=f32
        )
        rows[at, :] = out.reshape(group * 8, lanes)
        return carry

    lax.fori_loop(0, blocks // group, contract, 0)
    own = [
        split(rows[pl.ds(k, blocks, stride=8), :] + rows[pl.ds(4 + k, blocks, stride=8), :])
        for k in range(4)
    ]
    beside_x = jnp.where(wide > 0, 1, 0) + jnp.where(wide < n_wide - 1, 1, 0)
    beside_z = jnp.where(narrow > 0, 1, 0) + jnp.where(narrow < n_narrow - 1, 1, 0)
    pl.semaphore_wait(barrier, n_wide - 1 + beside_z * (1 + beside_x))

    start_all(0, sent_tiles, got_tiles)
    right = jnp.concatenate(
        [jnp.concatenate([o[0] for o in own], axis=1), jnp.concatenate([o[1] for o in own], axis=1)],
        axis=0,
    )
    place = jnp.concatenate([place, place], axis=1).astype(bf16)
    in_slots = dot(place, right)
    for k in range(4):
        sent[:, k] = in_slots[:, k * lanes : (k + 1) * lanes].reshape(n_wide, cap, lanes)
    start_all(1, sent, got)

    wait_all(0, sent_tiles, got_tiles)
    order = lax.broadcasted_iota(jnp.int32, (slots, tiles), 1)
    x_of, q_of, z_of = order // plane, (order // cz) % nq, order % cz
    tile_of = ((x_of * cz + z_of) * nq + q_of).astype(f32)
    tile_rows = jnp.broadcast_to(got_tiles[...], (n_wide, cap, lanes)).reshape(slots, lanes)
    slot_at = lax.broadcasted_iota(jnp.int32, (slots, lanes), 0) % cap
    lane_at = lax.broadcasted_iota(jnp.int32, (slots, lanes), 1)
    tile_slots = jnp.sum(jnp.where(slot_at == lane_at, tile_rows, 0.0), axis=1, keepdims=True)
    selector = jnp.where(tile_slots == tile_of, 1.0, 0.0)
    turned = jnp.transpose(selector).astype(bf16)
    selector = selector.astype(bf16)
    turned = jnp.concatenate([turned, turned], axis=1)
    selector = jnp.concatenate([selector, selector], axis=1)

    loads[5].wait()
    fluid = [
        jnp.concatenate(
            [
                fluid_ref[a, x, :, q * lanes : (q + 1) * lanes]
                for x in range(cx)
                for q in range(nq)
            ],
            axis=0,
        )
        for a in range(3)
    ]

    wait_all(1, sent, got)
    arrived = [split(got[:, k].reshape(slots, lanes)) for k in range(4)]
    right = jnp.concatenate(
        [jnp.concatenate([o[i] for o in arrived], axis=1) for i in range(2)], axis=0
    )
    spread = dot(turned, right)
    solid = spread[:, :lanes]
    growth = (1.0 + solid) * (1.0 + solid)
    scale = 1.0 / (1.0 + growth * solid)
    provisional = [
        (fluid[a] + growth * spread[:, (a + 1) * lanes : (a + 2) * lanes]) * scale
        for a in range(3)
    ]
    void = 1.0 / (1.0 + solid)
    shape = (nq, cz, lanes)

    def planes_of(value):
        return [value[x * plane : (x + 1) * plane].reshape(shape) for x in range(cx)]

    own_flux = [planes_of(void * provisional[a]) for a in range(3)]
    own_void = planes_of(void)

    def give_back(values, target, start):
        wide_values = [split(v) for v in values]
        right = jnp.concatenate(
            [jnp.concatenate([o[i] for o in wide_values], axis=1) for i in range(2)], axis=0
        )
        picked = dot(selector, right)
        for k in range(len(values)):
            target[:, start + k] = picked[:, k * lanes : (k + 1) * lanes].reshape(
                n_wide, cap, lanes
            )


    def ship(e, i, src, dst):
        dx, dz = DIRECTIONS[i]
        return pltpu.make_async_remote_copy(
            src_ref=src,
            dst_ref=dst,
            send_sem=side_send.at[e, i],
            recv_sem=side_recv.at[e, i],
            device_id=(wide + dx, narrow + dz),
            device_id_type=MESH,
        )

    def near_copy(i):
        dx, dz = DIRECTIONS[i]
        if dz == 0:
            return ship(0, i, near_x.at[0 if dx < 0 else 1], near_gx.at[lands_x(dx)])
        return ship(0, i, near_z, near_gz.at[lands_z(dz)])

    def deep_copy(e, i):
        dx, dz = DIRECTIONS[i]
        if dz == 0:
            start = 0 if dx < 0 else cx - DEPTH
            return ship(
                e + 1, i, deep.at[e, pl.ds(start, DEPTH)], deep_gx.at[e, lands_x(dx)]
            )
        if dx == 0:
            return ship(e + 1, i, deep.at[e], deep_gz.at[e, lands_z(dz)])
        return ship(
            e + 1,
            i,
            corner.at[e, 0 if dx < 0 else 1, 0 if dz < 0 else 1],
            corner_g.at[e, lands_x(dx), lands_z(dz)],
        )

    def each(directions, make, act, receiving=False):
        for i in directions:
            dx, dz = DIRECTIONS[i]

            @pl.when(exists(-dx, -dz) if receiving else exists(dx, dz))
            def _():
                getattr(make(i), act)()

    corner_spots = [(d, r) for d in range(1, DEPTH) for r in range(1, DEPTH + 1 - d)]

    def store_deep(e, planes):
        for x in range(cx):
            deep[e, x] = planes[x].reshape(plane, lanes)
        for sx in range(2):
            for sz in range(2):
                for n, (d, r) in enumerate(corner_spots):
                    x = d - 1 if sx == 0 else cx - d
                    z = r - 1 if sz == 0 else cz - r
                    corner[e, sx, sz, n * nq : (n + 1) * nq, :] = planes[x][:, z, :]

    row = lax.broadcasted_iota(jnp.int32, shape, 1)

    def tiles_from(own, others):
        if z_tiles == 2:
            first = narrow == 0
            return jnp.stack([jnp.where(first, own, others[0]), jnp.where(first, others[0], own)])
        return jnp.stack([others[0], own, others[1]])

    def own_of(value):
        if z_tiles == 2:
            return jnp.where(narrow == 0, value[0], value[1])
        return value[1]

    def corner_tile(e, side, which, d):
        tile = jnp.zeros(shape, f32)
        for n, (far, r) in enumerate(corner_spots):
            if far != d:
                continue
            spread_rows = jnp.stack(
                [
                    jnp.broadcast_to(
                        corner_g[e, side, which, n * nq + q : n * nq + q + 1, :], (cz, lanes)
                    )
                    for q in range(nq)
                ]
            )
            if z_tiles == 2:
                at = jnp.where(narrow == 0, r - 1, cz - r)
            else:
                at = cz - r if which == 0 else r - 1
            tile = jnp.where(row == at, spread_rows, tile)
        return tile

    def extended(e, planes):
        result = {}
        for x in range(cx):
            others = [deep_gz[e, t, x].reshape(shape) for t in range(z_tiles - 1)]
            result[x] = tiles_from(planes[x], others)
        for side in range(2):
            for d in range(1, DEPTH + 1):
                own = deep_gx[e, side, DEPTH - d if side == 0 else d - 1].reshape(shape)
                others = [corner_tile(e, side, t, d) for t in range(z_tiles - 1)]
                result[-d if side == 0 else cx - 1 + d] = tiles_from(own, others)
        return result

    def along_y(p):
        last = p.ndim - 1
        lane = lax.broadcasted_iota(jnp.int32, p.shape, last)
        up, down = pltpu.roll(p, lanes - 1, last), pltpu.roll(p, 1, last)
        if p.ndim == 4:
            zero = jnp.zeros_like(p[:, :1])
            next_up = jnp.concatenate([up[:, 1:], zero], axis=1)
            next_down = jnp.concatenate([zero, down[:, :-1]], axis=1)
        else:
            zero = jnp.zeros_like(p[:1])
            next_up = jnp.concatenate([up[1:], zero], axis=0)
            next_down = jnp.concatenate([zero, down[:-1]], axis=0)
        return jnp.where(lane == lanes - 1, next_up, up), jnp.where(lane == 0, next_down, down)

    def along_z(p):
        at = lax.broadcasted_iota(jnp.int32, p.shape, 2)
        up, down = pltpu.roll(p, cz - 1, 2), pltpu.roll(p, 1, 2)
        zero = jnp.zeros_like(p[:1])
        next_up = jnp.concatenate([up[1:], zero], axis=0)
        next_down = jnp.concatenate([zero, down[:-1]], axis=0)
        return jnp.where(at == cz - 1, next_up, up), jnp.where(at == 0, next_down, down)

    for side, x in ((0, 0), (1, cx - 1)):
        near_x[side, 0] = own_flux[0][x].reshape(plane, lanes)
        near_x[side, 1] = own_void[x].reshape(plane, lanes)
    for x in range(cx):
        near_z[0, x] = own_flux[1][x].reshape(plane, lanes)
        near_z[1, x] = own_void[x].reshape(plane, lanes)
    each((0, 1, 2, 3), near_copy, "start")
    store_deep(0, own_void)
    each((0, 1, 4, 5, 6, 7), lambda i: deep_copy(0, i), "start")

    void_y = [along_y(v) for v in own_void]
    flux_y = [along_y(v) for v in own_flux[2]]
    each((0, 1, 2, 3), near_copy, "wait_recv", True)

    def with_ghosts(planes, field):
        low = near_gx[0, field].reshape(shape)
        high = near_gx[1, field].reshape(shape)
        return [low] + planes + [high]

    flux_x, void_x = with_ghosts(own_flux[0], 0), with_ghosts(own_void, 1)
    void_inner, pressure = [], []
    for x in range(cx):
        flux_z, void_z = [
            tiles_from(own[x], [near_gz[t, field, x].reshape(shape) for t in range(z_tiles - 1)])
            for field, own in ((0, own_flux[1]), (1, own_void))
        ]
        void_inner.append(void_z)
        flux_up, flux_down = [own_of(v) for v in along_z(flux_z)]
        void_up, void_down = [own_of(v) for v in along_z(void_z)]
        source = -0.5 * (
            flux_x[x + 2] - flux_x[x] + flux_up - flux_down + flux_y[x][0] - flux_y[x][1]
        )
        around = void_x[x + 2] + void_x[x] + void_up + void_down + void_y[x][0] + void_y[x][1]
        pressure.append(source / (0.5 * (6.0 * own_void[x] + around)))

    def start_pressure(e, planes):
        store_deep(e, planes)
        each(range(8), lambda i: deep_copy(e, i), "start")

    def wait_pressure(e, planes):
        each(range(8), lambda i: deep_copy(e, i), "wait_recv", True)
        return extended(e, planes)

    start_pressure(1, pressure)
    give_back([growth], sent_growth, 0)

    each((0, 1, 4, 5, 6, 7), lambda i: deep_copy(0, i), "wait_recv", True)
    shares = {x: void_inner[x] for x in range(cx)}
    for side in range(2):
        for d in range(1, DEPTH + 1):
            own = deep_gx[0, side, DEPTH - d if side == 0 else d - 1].reshape(shape)
            others = [corner_tile(0, side, t, d) for t in range(z_tiles - 1)]
            shares[-d if side == 0 else cx - 1 + d] = tiles_from(own, others)
    weights = {}
    for x in range(1 - DEPTH, cx + DEPTH - 1):
        here = shares[x]
        nearby = (shares[x + 1], shares[x - 1]) + along_z(here) + along_y(here)
        sums = [here + v for v in nearby]
        total = sums[0] + sums[1] + sums[2] + sums[3] + sums[4] + sums[5]
        factor = jnp.where(here > 0.0, 1.0 / total, 0.0)
        weights[x] = [v * factor for v in sums]

    event = 1
    current = wait_pressure(event, pressure)
    start_all(2, sent_growth, got_growth)
    begun = current
    radius = DEPTH
    for sweep in range(SWEEPS - 1):
        if radius == 0:
            event += 1
            pressure = [own_of(current[x]) for x in range(cx)]
            start_pressure(event, pressure)
            current = wait_pressure(event, pressure)
            radius = DEPTH
        radius -= 1
        later = {}
        for x in range(-radius, cx + radius):
            p, w = current[x], weights[x]
            z_up, z_down = along_z(p)
            y_up, y_down = along_y(p)
            later[x] = (
                begun[x]
                + (w[0] * current[x + 1] + w[1] * current[x - 1])
                + (w[2] * z_up + w[3] * z_down)
                + (w[4] * y_up + w[5] * y_down)
            )
        current = later
    pressure = [own_of(current[x]) for x in range(cx)]
    steps = [[], [], []]
    for x in range(cx):
        z_up, z_down = along_z(current[x])
        y_up, y_down = along_y(pressure[x])
        steps[0].append(own_of(current[x + 1]) - own_of(current[x - 1]))
        steps[1].append(own_of(z_up) - own_of(z_down))
        steps[2].append(y_up - y_down)
    following = [
        provisional[a] - 0.5 * jnp.concatenate(steps[a], axis=0).reshape(tiles, lanes)
        for a in range(3)
    ]
    give_back([growth * v for v in following], sent_next, 0)
    start_all(3, sent_next, got_next)

    for x in range(cx):
        for q in range(nq):
            cut = slice(q * lanes, (q + 1) * lanes)
            at = (x * nq + q) * cz
            pressure_ref[x, :, cut] = pressure[x][q]
            for a in range(3):
                next_ref[a, x, :, cut] = following[a][at : at + cz]

    slot_row = lax.broadcasted_iota(jnp.int32, (blocks, slots), 1).astype(f32)
    back = jnp.where(slot_row == placed_col, 1.0, 0.0).astype(bf16)

    def place_back(target, k, row):
        high, low = split(target[:, k].reshape(slots, lanes))
        out = dot(back, jnp.concatenate([high, low], axis=1))
        rows[pl.ds(row, blocks, stride=8), :] = out[:, :lanes]
        rows[pl.ds(4 + row, blocks, stride=8), :] = out[:, lanes:]

    wait_all(2, sent_growth, got_growth)
    place_back(got_growth, 0, 3)
    wait_all(3, sent_next, got_next)
    for k in range(3):
        place_back(got_next, k, k)

    def sample(step, carry):
        base = pl.multiple_of(step * group, group)
        at = pl.ds(pl.multiple_of(base * 8, 8), group * 8)
        left = rows[at, :].reshape(group, 8, lanes).astype(bf16)
        out = lax.dot_general(
            left,
            pieces[pl.ds(base, group)],
            (((2,), (2,)), ((0,), (0,))),
            preferred_element_type=f32,
        )
        rows[at, :] = out.reshape(group * 8, lanes)
        return carry

    lax.fori_loop(0, blocks // group, sample, 0)

    def sampled(k):
        top = rows[pl.ds(k, blocks, stride=8), :]
        low = rows[pl.ds(4 + k, blocks, stride=8), :]
        return (top + low)[:, :particles] + pltpu.roll(top, particles, 1)[:, :particles]

    fourth = sampled(3)
    for k in range(3):
        drag_ref[k] = volume * sampled(k) - carried[1 + k] * fourth

    for phase, source, target in (
        (0, sent_tiles, got_tiles),
        (1, sent, got),
        (2, sent_growth, got_growth),
        (3, sent_next, got_next),
    ):
        end_all(phase, source, target)
    each((0, 1, 2, 3), near_copy, "wait_send")
    each((0, 1, 4, 5, 6, 7), lambda i: deep_copy(0, i), "wait_send")
    for e in range(1, event + 1):
        each(range(8), lambda i: deep_copy(e, i), "wait_send")


def solution(mesh):
    n_wide, n_narrow = mesh.shape["wide"], mesh.shape["narrow"]

    def local(kernel, volume, velocity, block_brick, block_tile, fluid_velocity):
        blocks, particles, lanes = kernel.shape
        _, cx, cz, ny = fluid_velocity.shape
        cap = max(2, (2 * blocks + n_wide - 1) // n_wide)
        cap = (cap + 7) // 8 * 8
        nq = ny // lanes
        plane = nq * cz
        vmem = pltpu.VMEM
        hbm_spec = pl.BlockSpec(memory_space=pltpu.HBM)
        vmem_spec = pl.BlockSpec(memory_space=pltpu.VMEM)
        flux = [
            vmem((n_wide, 1, lanes), f32),
            vmem((n_wide, 1, lanes), f32),
            vmem((n_wide, 4, cap, lanes), f32),
            vmem((n_wide, 4, cap, lanes), f32),
            vmem((n_wide, 1, cap, lanes), f32),
            vmem((n_wide, 1, cap, lanes), f32),
            vmem((n_wide, 3, cap, lanes), f32),
            vmem((n_wide, 3, cap, lanes), f32),
        ]
        events = 2 + (SWEEPS - 1) // DEPTH
        others = 1 if n_narrow == 2 else 2
        corner_rows = (DEPTH * (DEPTH - 1) // 2 * nq + 7) // 8 * 8
        halo = [
            vmem((2, 2, plane, lanes), f32),
            vmem((2, 2, plane, lanes), f32),
            vmem((2, cx, plane, lanes), f32),
            vmem((others, 2, cx, plane, lanes), f32),
            vmem((events, cx, plane, lanes), f32),
            vmem((events, 2, DEPTH, plane, lanes), f32),
            vmem((events, others, cx, plane, lanes), f32),
            vmem((events, 2, 2, corner_rows, lanes), f32),
            vmem((events, 2, others, corner_rows, lanes), f32),
        ]
        drag, pressure, following = pl.pallas_call(
            functools.partial(body, n_wide, n_narrow, cap),
            out_shape=(
                jax.ShapeDtypeStruct((3, blocks, particles), f32),
                jax.ShapeDtypeStruct((cx, cz, ny), f32),
                jax.ShapeDtypeStruct((3, cx, cz, ny), f32),
            ),
            in_specs=[hbm_spec] * 6,
            out_specs=(vmem_spec,) * 3,
            scratch_shapes=[
                vmem((blocks, particles, lanes), f32),
                vmem((blocks, particles), f32),
                vmem((3, blocks, particles), f32),
                vmem((1, blocks), jnp.int32),
                vmem((1, blocks), jnp.int32),
                vmem((3, cx, cz, ny), f32),
                vmem((blocks, 2 * particles, lanes), bf16),
                vmem((blocks * 8, lanes), f32),
            ]
            + flux
            + halo
            + [
                pltpu.SemaphoreType.DMA((6,)),
                pltpu.SemaphoreType.DMA((4, n_wide)),
                pltpu.SemaphoreType.DMA((4, n_wide)),
                pltpu.SemaphoreType.DMA((events + 1, 8)),
                pltpu.SemaphoreType.DMA((events + 1, 8)),
            ],
            compiler_params=pltpu.CompilerParams(
                collective_id=0, has_side_effects=True, vmem_limit_bytes=40 * 1024 * 1024
            ),
        )(
            *[
                pltpu.with_memory_space_constraint(operand, pltpu.HBM)
                for operand in (
                    kernel,
                    volume,
                    jnp.transpose(velocity, (1, 0, 2)),
                    block_brick.reshape(1, blocks),
                    block_tile.reshape(1, blocks),
                    fluid_velocity,
                )
            ]
        )
        return jnp.transpose(drag, (1, 0, 2)), pressure, following

    return jax.shard_map(
        local,
        mesh=mesh,
        in_specs=(
            P(("wide", "narrow"), None, None),
            P(("wide", "narrow"), None),
            P(("wide", "narrow"), None, None),
            P(("wide", "narrow"), None),
            P(("wide", "narrow")),
            P(None, "wide", "narrow", None),
        ),
        out_specs=(
            P(("wide", "narrow"), None, None),
            P("wide", "narrow", None),
            P(None, "wide", "narrow", None),
        ),
        check_vma=False,
    )
```

```python
import functools

import jax
import jax.numpy as jnp
from jax import lax
from jax.experimental import pallas as pl
from jax.experimental.pallas import tpu as pltpu
from jax.sharding import PartitionSpec as P

SWEEPS = 6
DEPTH = 3
DIRECTIONS = ((-1, 0), (1, 0), (0, -1), (0, 1), (-1, -1), (-1, 1), (1, -1), (1, 1))
MESH = pl.DeviceIdType.MESH
f32 = jnp.float32
bf16 = jnp.bfloat16


def split(value):
    high = value.astype(bf16)
    return high, (value - high.astype(f32)).astype(bf16)


def dot(a, b):
    return jnp.dot(a, b, preferred_element_type=f32)


def body(
    n_wide, n_narrow, cap,
    kernel_hbm, volume_hbm, velocity_hbm, brick_hbm, tile_hbm, fluid_hbm,
    drag_ref, pressure_ref, next_ref,
    kernel_buf, volume_ref, velocity_ref, brick_ref, tile_ref, fluid_ref, pieces, turned_pieces, rows, products, sent_tiles, got_tiles, sent, got,
    sent_growth, got_growth, sent_next, got_next,
    near_x, near_gx, near_z, near_gz, deep, deep_gx, deep_gz, corner, corner_g,
    load_sem, send_sem, recv_sem, side_send, side_recv,
):
    wide, narrow = lax.axis_index("wide"), lax.axis_index("narrow")
    blocks, particles, lanes = kernel_buf.shape
    _, cx, cz, ny = fluid_ref.shape
    nq = ny // lanes
    plane = nq * cz
    tiles = cx * plane
    slots = n_wide * cap

    loads = [
        pltpu.make_async_copy(here, there, load_sem.at[i])
        for i, (here, there) in enumerate(
            (
                (brick_hbm, brick_ref),
                (tile_hbm, tile_ref),
                (volume_hbm, volume_ref),
                (velocity_hbm, velocity_ref),
                (kernel_hbm, kernel_buf),
                (fluid_hbm, fluid_ref),
            )
        )
    ]
    for load in loads:
        load.start()

    barrier = pltpu.get_barrier_semaphore()

    def greet(step, carry):
        pl.semaphore_signal(
            barrier, inc=1, device_id=(lax.rem(wide + step, n_wide), narrow), device_id_type=MESH
        )
        return carry

    lax.fori_loop(1, n_wide, greet, 0)
    z_tiles = near_gz.shape[0] + 1

    def exists(dx, dz):
        inside = (wide + dx >= 0) & (wide + dx < n_wide)
        return inside & (narrow + dz >= 0) & (narrow + dz < n_narrow)

    for dx, dz in DIRECTIONS:
        if dz:

            @pl.when(exists(dx, dz))
            def _():
                pl.semaphore_signal(
                    barrier, inc=1, device_id=(wide + dx, narrow + dz), device_id_type=MESH
                )

    def lands_x(dx):
        return 0 if dx > 0 else 1

    def lands_z(dz):
        return 0 if dz > 0 or z_tiles == 2 else 1

    for dx, dz in DIRECTIONS:
        if dz and z_tiles == 2:
            absent = jnp.logical_not(exists(-dx, 0)) if dx else None
            if dx and dz < 0:
                continue
        else:
            absent = jnp.logical_not(exists(-dx, -dz))
        if absent is None:
            continue

        @pl.when(absent)
        def _():
            events = deep.shape[0]
            if dz == 0:
                near_gx[lands_x(dx)] = jnp.zeros(near_gx.shape[1:], f32)
                for e in range(events):
                    deep_gx[e, lands_x(dx)] = jnp.zeros(deep_gx.shape[2:], f32)
            elif dx == 0:
                near_gz[lands_z(dz)] = jnp.zeros(near_gz.shape[1:], f32)
                for e in range(events):
                    deep_gz[e, lands_z(dz)] = jnp.zeros(deep_gz.shape[2:], f32)
            else:
                for e in range(events):
                    corner_g[e, lands_x(dx), lands_z(dz)] = jnp.zeros(corner_g.shape[3:], f32)

    loads[0].wait()
    loads[1].wait()
    rows_b = lax.broadcasted_iota(jnp.int32, (blocks, blocks), 0)
    cols_b = lax.broadcasted_iota(jnp.int32, (blocks, blocks), 1)
    target_row = jnp.broadcast_to(brick_ref[...].astype(f32), (blocks, blocks))
    target_col = jnp.sum(jnp.where(rows_b == cols_b, target_row, 0.0), axis=1, keepdims=True)
    same = jnp.where(target_col == target_row, 1.0, 0.0)
    position_row = jnp.sum(jnp.where(rows_b < cols_b, same, 0.0), axis=0, keepdims=True)
    position_col = jnp.sum(jnp.where(cols_b < rows_b, same, 0.0), axis=1, keepdims=True)
    placed_row = target_row[:1] * cap + position_row
    placed_col = target_col * cap + position_col
    slot_col = lax.broadcasted_iota(jnp.int32, (slots, blocks), 0).astype(f32)
    place = jnp.where(slot_col == placed_row, 1.0, 0.0)
    named = lax.broadcasted_iota(jnp.int32, (n_wide, blocks), 0).astype(f32) == target_row[:1]
    named = jnp.where(named, tile_ref[...].astype(f32), 0.0)
    at_lane = lax.broadcasted_iota(jnp.int32, (blocks, lanes), 1).astype(f32) == position_col
    at_lane = jnp.where(at_lane, 1.0, 0.0).astype(bf16)
    high, low = split(named)
    sent_tiles[...] = (dot(high, at_lane) + dot(low, at_lane)).reshape(n_wide, 1, lanes)

    def passing(phase, source, target, step):
        partner = lax.rem(wide + step, n_wide)
        return pltpu.make_async_remote_copy(
            src_ref=source.at[partner],
            dst_ref=target.at[wide],
            send_sem=send_sem.at[phase, step],
            recv_sem=recv_sem.at[phase, step],
            device_id=(partner, narrow),
            device_id_type=MESH,
        )

    def start_all(phase, source, target):
        def go(turn, carry):
            far = (turn + 1) // 2
            step = n_wide // 2 + far * (2 * (turn % 2) - 1)
            passing(phase, source, target, step).start()
            return carry

        lax.fori_loop(0, n_wide - 1, go, 0)
        target[wide] = source[wide]

    def wait_all(phase, source, target):
        def go(step, carry):
            passing(phase, source, target, step).wait_recv()
            return carry

        lax.fori_loop(1, n_wide, go, 0)

    def end_all(phase, source, target):
        def go(step, carry):
            passing(phase, source, target, step).wait_send()
            return carry

        lax.fori_loop(1, n_wide, go, 0)

    loads[2].wait()
    loads[3].wait()
    volume = volume_ref[...]
    carried = [volume] + [volume * velocity_ref[a] for a in range(3)]
    for k in range(4):
        high = carried[k].astype(bf16).astype(f32)
        low = carried[k] - high
        rows[pl.ds(k, blocks, stride=8), :] = jnp.concatenate([high, high], axis=1)
        rows[pl.ds(4 + k, blocks, stride=8), :] = jnp.concatenate(
            [low, jnp.zeros_like(low)], axis=1
        )
    loads[4].wait()
    for b in range(blocks):
        both = jnp.concatenate(split(kernel_buf[b]), axis=0)
        pieces[b] = both
        at = slice(b * 8, b * 8 + 8)
        products[at, :] = dot(rows[at, :].astype(bf16), both)
    own = [
        split(
            products[pl.ds(k, blocks, stride=8), :] + products[pl.ds(4 + k, blocks, stride=8), :]
        )
        for k in range(4)
    ]
    beside_x = jnp.where(wide > 0, 1, 0) + jnp.where(wide < n_wide - 1, 1, 0)
    beside_z = jnp.where(narrow > 0, 1, 0) + jnp.where(narrow < n_narrow - 1, 1, 0)
    pl.semaphore_wait(barrier, n_wide - 1 + beside_z * (1 + beside_x))

    start_all(0, sent_tiles, got_tiles)
    right = jnp.concatenate(
        [jnp.concatenate([o[0] for o in own], axis=1), jnp.concatenate([o[1] for o in own], axis=1)],
        axis=0,
    )
    place = jnp.concatenate([place, place], axis=1).astype(bf16)
    in_slots = dot(place, right)
    for k in range(4):
        sent[:, k] = in_slots[:, k * lanes : (k + 1) * lanes].reshape(n_wide, cap, lanes)
    start_all(1, sent, got)

    group = 8

    def turn(step, carry):
        for b in range(group):
            turned_pieces[step * group + b] = jnp.transpose(pieces[step * group + b])
        return carry

    lax.fori_loop(0, blocks // group, turn, 0)

    wait_all(0, sent_tiles, got_tiles)
    order = lax.broadcasted_iota(jnp.int32, (slots, tiles), 1)
    x_of, q_of, z_of = order // plane, (order // cz) % nq, order % cz
    tile_of = ((x_of * cz + z_of) * nq + q_of).astype(f32)
    tile_rows = jnp.broadcast_to(got_tiles[...], (n_wide, cap, lanes)).reshape(slots, lanes)
    slot_at = lax.broadcasted_iota(jnp.int32, (slots, lanes), 0) % cap
    lane_at = lax.broadcasted_iota(jnp.int32, (slots, lanes), 1)
    tile_slots = jnp.sum(jnp.where(slot_at == lane_at, tile_rows, 0.0), axis=1, keepdims=True)
    selector = jnp.where(tile_slots == tile_of, 1.0, 0.0)
    turned = jnp.transpose(selector).astype(bf16)
    selector = selector.astype(bf16)
    turned = jnp.concatenate([turned, turned], axis=1)
    selector = jnp.concatenate([selector, selector], axis=1)

    loads[5].wait()
    fluid = [
        jnp.concatenate(
            [
                fluid_ref[a, x, :, q * lanes : (q + 1) * lanes]
                for x in range(cx)
                for q in range(nq)
            ],
            axis=0,
        )
        for a in range(3)
    ]

    wait_all(1, sent, got)
    arrived = [split(got[:, k].reshape(slots, lanes)) for k in range(4)]
    right = jnp.concatenate(
        [jnp.concatenate([o[i] for o in arrived], axis=1) for i in range(2)], axis=0
    )
    spread = dot(turned, right)
    solid = spread[:, :lanes]
    growth = (1.0 + solid) * (1.0 + solid)
    scale = 1.0 / (1.0 + growth * solid)
    provisional = [
        (fluid[a] + growth * spread[:, (a + 1) * lanes : (a + 2) * lanes]) * scale
        for a in range(3)
    ]
    void = 1.0 / (1.0 + solid)
    shape = (nq, cz, lanes)

    def planes_of(value):
        return [value[x * plane : (x + 1) * plane].reshape(shape) for x in range(cx)]

    own_flux = [planes_of(void * provisional[a]) for a in range(3)]
    own_void = planes_of(void)

    def give_back(values, target, start):
        wide_values = [split(v) for v in values]
        right = jnp.concatenate(
            [jnp.concatenate([o[i] for o in wide_values], axis=1) for i in range(2)], axis=0
        )
        picked = dot(selector, right)
        for k in range(len(values)):
            target[:, start + k] = picked[:, k * lanes : (k + 1) * lanes].reshape(
                n_wide, cap, lanes
            )


    def ship(e, i, src, dst):
        dx, dz = DIRECTIONS[i]
        return pltpu.make_async_remote_copy(
            src_ref=src,
            dst_ref=dst,
            send_sem=side_send.at[e, i],
            recv_sem=side_recv.at[e, i],
            device_id=(wide + dx, narrow + dz),
            device_id_type=MESH,
        )

    def near_copy(i):
        dx, dz = DIRECTIONS[i]
        if dz == 0:
            return ship(0, i, near_x.at[0 if dx < 0 else 1], near_gx.at[lands_x(dx)])
        return ship(0, i, near_z, near_gz.at[lands_z(dz)])

    def deep_copy(e, i):
        dx, dz = DIRECTIONS[i]
        if dz == 0:
            start = 0 if dx < 0 else cx - DEPTH
            return ship(
                e + 1, i, deep.at[e, pl.ds(start, DEPTH)], deep_gx.at[e, lands_x(dx)]
            )
        if dx == 0:
            return ship(e + 1, i, deep.at[e], deep_gz.at[e, lands_z(dz)])
        return ship(
            e + 1,
            i,
            corner.at[e, 0 if dx < 0 else 1, 0 if dz < 0 else 1],
            corner_g.at[e, lands_x(dx), lands_z(dz)],
        )

    def each(directions, make, act, receiving=False):
        for i in directions:
            dx, dz = DIRECTIONS[i]

            @pl.when(exists(-dx, -dz) if receiving else exists(dx, dz))
            def _():
                getattr(make(i), act)()

    corner_spots = [(d, r) for d in range(1, DEPTH) for r in range(1, DEPTH + 1 - d)]

    def store_deep(e, planes):
        for x in range(cx):
            deep[e, x] = planes[x].reshape(plane, lanes)
        for sx in range(2):
            for sz in range(2):
                for n, (d, r) in enumerate(corner_spots):
                    x = d - 1 if sx == 0 else cx - d
                    z = r - 1 if sz == 0 else cz - r
                    corner[e, sx, sz, n * nq : (n + 1) * nq, :] = planes[x][:, z, :]

    row = lax.broadcasted_iota(jnp.int32, shape, 1)

    def tiles_from(own, others):
        if z_tiles == 2:
            first = narrow == 0
            return jnp.stack([jnp.where(first, own, others[0]), jnp.where(first, others[0], own)])
        return jnp.stack([others[0], own, others[1]])

    def own_of(value):
        if z_tiles == 2:
            return jnp.where(narrow == 0, value[0], value[1])
        return value[1]

    def corner_tile(e, side, which, d):
        tile = jnp.zeros(shape, f32)
        for n, (far, r) in enumerate(corner_spots):
            if far != d:
                continue
            spread_rows = jnp.stack(
                [
                    jnp.broadcast_to(
                        corner_g[e, side, which, n * nq + q : n * nq + q + 1, :], (cz, lanes)
                    )
                    for q in range(nq)
                ]
            )
            if z_tiles == 2:
                at = jnp.where(narrow == 0, r - 1, cz - r)
            else:
                at = cz - r if which == 0 else r - 1
            tile = jnp.where(row == at, spread_rows, tile)
        return tile

    def extended(e, planes):
        result = {}
        for x in range(cx):
            others = [deep_gz[e, t, x].reshape(shape) for t in range(z_tiles - 1)]
            result[x] = tiles_from(planes[x], others)
        for side in range(2):
            for d in range(1, DEPTH + 1):
                own = deep_gx[e, side, DEPTH - d if side == 0 else d - 1].reshape(shape)
                others = [corner_tile(e, side, t, d) for t in range(z_tiles - 1)]
                result[-d if side == 0 else cx - 1 + d] = tiles_from(own, others)
        return result

    def along_y(p):
        last = p.ndim - 1
        lane = lax.broadcasted_iota(jnp.int32, p.shape, last)
        up, down = pltpu.roll(p, lanes - 1, last), pltpu.roll(p, 1, last)
        if p.ndim == 4:
            zero = jnp.zeros_like(p[:, :1])
            next_up = jnp.concatenate([up[:, 1:], zero], axis=1)
            next_down = jnp.concatenate([zero, down[:, :-1]], axis=1)
        else:
            zero = jnp.zeros_like(p[:1])
            next_up = jnp.concatenate([up[1:], zero], axis=0)
            next_down = jnp.concatenate([zero, down[:-1]], axis=0)
        return jnp.where(lane == lanes - 1, next_up, up), jnp.where(lane == 0, next_down, down)

    def along_z(p):
        at = lax.broadcasted_iota(jnp.int32, p.shape, 2)
        up, down = pltpu.roll(p, cz - 1, 2), pltpu.roll(p, 1, 2)
        zero = jnp.zeros_like(p[:1])
        next_up = jnp.concatenate([up[1:], zero], axis=0)
        next_down = jnp.concatenate([zero, down[:-1]], axis=0)
        return jnp.where(at == cz - 1, next_up, up), jnp.where(at == 0, next_down, down)

    for side, x in ((0, 0), (1, cx - 1)):
        near_x[side, 0] = own_flux[0][x].reshape(plane, lanes)
        near_x[side, 1] = own_void[x].reshape(plane, lanes)
    for x in range(cx):
        near_z[0, x] = own_flux[1][x].reshape(plane, lanes)
        near_z[1, x] = own_void[x].reshape(plane, lanes)
    each((0, 1, 2, 3), near_copy, "start")
    store_deep(0, own_void)
    each((0, 1, 4, 5, 6, 7), lambda i: deep_copy(0, i), "start")

    void_y = [along_y(v) for v in own_void]
    flux_y = [along_y(v) for v in own_flux[2]]
    each((0, 1, 2, 3), near_copy, "wait_recv", True)

    def with_ghosts(planes, field):
        low = near_gx[0, field].reshape(shape)
        high = near_gx[1, field].reshape(shape)
        return [low] + planes + [high]

    flux_x, void_x = with_ghosts(own_flux[0], 0), with_ghosts(own_void, 1)
    void_inner, pressure = [], []
    for x in range(cx):
        flux_z, void_z = [
            tiles_from(own[x], [near_gz[t, field, x].reshape(shape) for t in range(z_tiles - 1)])
            for field, own in ((0, own_flux[1]), (1, own_void))
        ]
        void_inner.append(void_z)
        flux_up, flux_down = [own_of(v) for v in along_z(flux_z)]
        void_up, void_down = [own_of(v) for v in along_z(void_z)]
        source = -0.5 * (
            flux_x[x + 2] - flux_x[x] + flux_up - flux_down + flux_y[x][0] - flux_y[x][1]
        )
        around = void_x[x + 2] + void_x[x] + void_up + void_down + void_y[x][0] + void_y[x][1]
        pressure.append(source / (0.5 * (6.0 * own_void[x] + around)))

    def start_pressure(e, planes):
        store_deep(e, planes)
        each(range(8), lambda i: deep_copy(e, i), "start")

    def wait_pressure(e, planes):
        each(range(8), lambda i: deep_copy(e, i), "wait_recv", True)
        return extended(e, planes)

    start_pressure(1, pressure)
    give_back([growth], sent_growth, 0)

    each((0, 1, 4, 5, 6, 7), lambda i: deep_copy(0, i), "wait_recv", True)
    shares = {x: void_inner[x] for x in range(cx)}
    for side in range(2):
        for d in range(1, DEPTH + 1):
            own = deep_gx[0, side, DEPTH - d if side == 0 else d - 1].reshape(shape)
            others = [corner_tile(0, side, t, d) for t in range(z_tiles - 1)]
            shares[-d if side == 0 else cx - 1 + d] = tiles_from(own, others)
    weights = {}
    for x in range(1 - DEPTH, cx + DEPTH - 1):
        here = shares[x]
        nearby = (shares[x + 1], shares[x - 1]) + along_z(here) + along_y(here)
        sums = [here + v for v in nearby]
        total = sums[0] + sums[1] + sums[2] + sums[3] + sums[4] + sums[5]
        factor = jnp.where(here > 0.0, 1.0 / total, 0.0)
        weights[x] = [v * factor for v in sums]

    event = 1
    current = wait_pressure(event, pressure)
    start_all(2, sent_growth, got_growth)
    begun = current
    radius = DEPTH
    for sweep in range(SWEEPS - 1):
        if radius == 0:
            event += 1
            pressure = [own_of(current[x]) for x in range(cx)]
            start_pressure(event, pressure)
            current = wait_pressure(event, pressure)
            radius = DEPTH
        radius -= 1
        later = {}
        for x in range(-radius, cx + radius):
            p, w = current[x], weights[x]
            z_up, z_down = along_z(p)
            y_up, y_down = along_y(p)
            later[x] = (
                begun[x]
                + (w[0] * current[x + 1] + w[1] * current[x - 1])
                + (w[2] * z_up + w[3] * z_down)
                + (w[4] * y_up + w[5] * y_down)
            )
        current = later
    pressure = [own_of(current[x]) for x in range(cx)]
    steps = [[], [], []]
    for x in range(cx):
        z_up, z_down = along_z(current[x])
        y_up, y_down = along_y(pressure[x])
        steps[0].append(own_of(current[x + 1]) - own_of(current[x - 1]))
        steps[1].append(own_of(z_up) - own_of(z_down))
        steps[2].append(y_up - y_down)
    following = [
        provisional[a] - 0.5 * jnp.concatenate(steps[a], axis=0).reshape(tiles, lanes)
        for a in range(3)
    ]
    give_back([growth * v for v in following], sent_next, 0)
    start_all(3, sent_next, got_next)

    for x in range(cx):
        for q in range(nq):
            cut = slice(q * lanes, (q + 1) * lanes)
            at = (x * nq + q) * cz
            pressure_ref[x, :, cut] = pressure[x][q]
            for a in range(3):
                next_ref[a, x, :, cut] = following[a][at : at + cz]

    slot_row = lax.broadcasted_iota(jnp.int32, (blocks, slots), 1).astype(f32)
    back = jnp.where(slot_row == placed_col, 1.0, 0.0).astype(bf16)

    def place_back(target, k, row):
        high, low = split(target[:, k].reshape(slots, lanes))
        out = dot(back, jnp.concatenate([high, low], axis=1))
        rows[pl.ds(row, blocks, stride=8), :] = out[:, :lanes]
        rows[pl.ds(4 + row, blocks, stride=8), :] = out[:, lanes:]

    wait_all(2, sent_growth, got_growth)
    place_back(got_growth, 0, 3)
    wait_all(3, sent_next, got_next)
    for k in range(3):
        place_back(got_next, k, k)

    for b in range(blocks):
        at = slice(b * 8, b * 8 + 8)
        products[at, :] = dot(rows[at, :].astype(bf16), turned_pieces[b])

    def sampled(k):
        top = products[pl.ds(k, blocks, stride=8), :]
        low = products[pl.ds(4 + k, blocks, stride=8), :]
        return (top + low)[:, :particles] + pltpu.roll(top, particles, 1)[:, :particles]

    fourth = sampled(3)
    for k in range(3):
        drag_ref[k] = volume * sampled(k) - carried[1 + k] * fourth

    for phase, source, target in (
        (0, sent_tiles, got_tiles),
        (1, sent, got),
        (2, sent_growth, got_growth),
        (3, sent_next, got_next),
    ):
        end_all(phase, source, target)
    each((0, 1, 2, 3), near_copy, "wait_send")
    each((0, 1, 4, 5, 6, 7), lambda i: deep_copy(0, i), "wait_send")
    for e in range(1, event + 1):
        each(range(8), lambda i: deep_copy(e, i), "wait_send")


def hand_over(*refs):
    sources, targets, sems = refs[:3], refs[3:6], refs[6]
    copies = [pltpu.make_async_copy(sources[i], targets[i], sems.at[i]) for i in range(3)]
    for copy in copies:
        copy.start()
    for copy in copies:
        copy.wait()


def solution(mesh):
    n_wide, n_narrow = mesh.shape["wide"], mesh.shape["narrow"]

    def local(kernel, volume, velocity, block_brick, block_tile, fluid_velocity):
        blocks, particles, lanes = kernel.shape
        _, cx, cz, ny = fluid_velocity.shape
        cap = max(2, (2 * blocks + n_wide - 1) // n_wide)
        cap = (cap + 7) // 8 * 8
        nq = ny // lanes
        plane = nq * cz
        vmem = pltpu.VMEM
        hbm_spec = pl.BlockSpec(memory_space=pltpu.HBM)
        vmem_spec = pl.BlockSpec(memory_space=pltpu.VMEM)
        flux = [
            vmem((n_wide, 1, lanes), f32),
            vmem((n_wide, 1, lanes), f32),
            vmem((n_wide, 4, cap, lanes), f32),
            vmem((n_wide, 4, cap, lanes), f32),
            vmem((n_wide, 1, cap, lanes), f32),
            vmem((n_wide, 1, cap, lanes), f32),
            vmem((n_wide, 3, cap, lanes), f32),
            vmem((n_wide, 3, cap, lanes), f32),
        ]
        events = 2 + (SWEEPS - 1) // DEPTH
        others = 1 if n_narrow == 2 else 2
        corner_rows = (DEPTH * (DEPTH - 1) // 2 * nq + 7) // 8 * 8
        halo = [
            vmem((2, 2, plane, lanes), f32),
            vmem((2, 2, plane, lanes), f32),
            vmem((2, cx, plane, lanes), f32),
            vmem((others, 2, cx, plane, lanes), f32),
            vmem((events, cx, plane, lanes), f32),
            vmem((events, 2, DEPTH, plane, lanes), f32),
            vmem((events, others, cx, plane, lanes), f32),
            vmem((events, 2, 2, corner_rows, lanes), f32),
            vmem((events, 2, others, corner_rows, lanes), f32),
        ]
        drag, pressure, following = pl.pallas_call(
            functools.partial(body, n_wide, n_narrow, cap),
            out_shape=(
                jax.ShapeDtypeStruct((3, blocks, particles), f32),
                jax.ShapeDtypeStruct((cx, cz, ny), f32),
                jax.ShapeDtypeStruct((3, cx, cz, ny), f32),
            ),
            in_specs=[hbm_spec] * 6,
            out_specs=(vmem_spec,) * 3,
            scratch_shapes=[
                vmem((blocks, particles, lanes), f32),
                vmem((blocks, particles), f32),
                vmem((3, blocks, particles), f32),
                vmem((1, blocks), jnp.int32),
                vmem((1, blocks), jnp.int32),
                vmem((3, cx, cz, ny), f32),
                vmem((blocks, 2 * particles, lanes), bf16),
                vmem((blocks, lanes, 2 * particles), bf16),
                vmem((blocks * 8, lanes), f32),
                vmem((blocks * 8, lanes), f32),
            ]
            + flux
            + halo
            + [
                pltpu.SemaphoreType.DMA((6,)),
                pltpu.SemaphoreType.DMA((4, n_wide)),
                pltpu.SemaphoreType.DMA((4, n_wide)),
                pltpu.SemaphoreType.DMA((events + 1, 8)),
                pltpu.SemaphoreType.DMA((events + 1, 8)),
            ],
            compiler_params=pltpu.CompilerParams(
                collective_id=0, has_side_effects=True, vmem_limit_bytes=40 * 1024 * 1024
            ),
        )(
            *[
                pltpu.with_memory_space_constraint(operand, pltpu.HBM)
                for operand in (
                    kernel,
                    volume,
                    jnp.transpose(velocity, (1, 0, 2)),
                    block_brick.reshape(1, blocks),
                    block_tile.reshape(1, blocks),
                    fluid_velocity,
                )
            ]
        )
        results = (drag, pressure, following)
        drag, pressure, following = pl.pallas_call(
            hand_over,
            out_shape=tuple(jax.ShapeDtypeStruct(r.shape, r.dtype) for r in results),
            in_specs=[vmem_spec] * 3,
            out_specs=(pl.BlockSpec(memory_space=pltpu.HBM),) * 3,
            scratch_shapes=[pltpu.SemaphoreType.DMA((3,))],
            compiler_params=pltpu.CompilerParams(vmem_limit_bytes=4 * 1024 * 1024),
        )(*results)
        return jnp.transpose(drag, (1, 0, 2)), pressure, following

    return jax.shard_map(
        local,
        mesh=mesh,
        in_specs=(
            P(("wide", "narrow"), None, None),
            P(("wide", "narrow"), None),
            P(("wide", "narrow"), None, None),
            P(("wide", "narrow"), None),
            P(("wide", "narrow")),
            P(None, "wide", "narrow", None),
        ),
        out_specs=(
            P(("wide", "narrow"), None, None),
            P("wide", "narrow", None),
            P(None, "wide", "narrow", None),
        ),
        check_vma=False,
    )
```

```python
import functools

import jax
import jax.numpy as jnp
from jax import lax
from jax.experimental import pallas as pl
from jax.experimental.pallas import tpu as pltpu
from jax.sharding import PartitionSpec as P

SWEEPS = 6
DEPTH = 3
LOAD_PARTS = 4
DIRECTIONS = ((-1, 0), (1, 0), (0, -1), (0, 1), (-1, -1), (-1, 1), (1, -1), (1, 1))
MESH = pl.DeviceIdType.MESH
f32 = jnp.float32
bf16 = jnp.bfloat16


def split(value):
    high = value.astype(bf16)
    return high, (value - high.astype(f32)).astype(bf16)


def dot(a, b):
    return jnp.dot(a, b, preferred_element_type=f32)


def body(
    n_wide, n_narrow, cap,
    kernel_hbm, volume_hbm, velocity_hbm, brick_hbm, tile_hbm, fluid_hbm,
    drag_ref, pressure_ref, next_ref,
    kernel_buf, volume_ref, velocity_ref, brick_ref, tile_ref, fluid_ref, pieces, turned_pieces, rows, products, sent_tiles, got_tiles, sent, got,
    sent_growth, got_growth, sent_next, got_next,
    near_x, near_gx, near_z, near_gz, deep, deep_gx, deep_gz, corner, corner_g,
    load_sem, send_sem, recv_sem, side_send, side_recv,
):
    wide, narrow = lax.axis_index("wide"), lax.axis_index("narrow")
    blocks, particles, lanes = kernel_buf.shape
    _, cx, cz, ny = fluid_ref.shape
    nq = ny // lanes
    plane = nq * cz
    tiles = cx * plane
    slots = n_wide * cap

    loads = [
        pltpu.make_async_copy(here, there, load_sem.at[i])
        for i, (here, there) in enumerate(
            (
                (brick_hbm, brick_ref),
                (tile_hbm, tile_ref),
                (volume_hbm, volume_ref),
                (velocity_hbm, velocity_ref),
                (fluid_hbm, fluid_ref),
            )
        )
    ]
    part = blocks // LOAD_PARTS
    for i in range(LOAD_PARTS):
        rows_of = pl.ds(i * part, part)
        loads.append(
            pltpu.make_async_copy(
                kernel_hbm.at[rows_of], kernel_buf.at[rows_of], load_sem.at[5 + i]
            )
        )
    for load in loads[:4] + loads[5:] + loads[4:5]:
        load.start()

    barrier = pltpu.get_barrier_semaphore()

    def greet(step, carry):
        pl.semaphore_signal(
            barrier, inc=1, device_id=(lax.rem(wide + step, n_wide), narrow), device_id_type=MESH
        )
        return carry

    lax.fori_loop(1, n_wide, greet, 0)
    z_tiles = near_gz.shape[0] + 1

    def exists(dx, dz):
        inside = (wide + dx >= 0) & (wide + dx < n_wide)
        return inside & (narrow + dz >= 0) & (narrow + dz < n_narrow)

    for dx, dz in DIRECTIONS:
        if dz:

            @pl.when(exists(dx, dz))
            def _():
                pl.semaphore_signal(
                    barrier, inc=1, device_id=(wide + dx, narrow + dz), device_id_type=MESH
                )

    def lands_x(dx):
        return 0 if dx > 0 else 1

    def lands_z(dz):
        return 0 if dz > 0 or z_tiles == 2 else 1

    for dx, dz in DIRECTIONS:
        if dz and z_tiles == 2:
            absent = jnp.logical_not(exists(-dx, 0)) if dx else None
            if dx and dz < 0:
                continue
        else:
            absent = jnp.logical_not(exists(-dx, -dz))
        if absent is None:
            continue

        @pl.when(absent)
        def _():
            events = deep.shape[0]
            if dz == 0:
                near_gx[lands_x(dx)] = jnp.zeros(near_gx.shape[1:], f32)
                for e in range(events):
                    deep_gx[e, lands_x(dx)] = jnp.zeros(deep_gx.shape[2:], f32)
            elif dx == 0:
                near_gz[lands_z(dz)] = jnp.zeros(near_gz.shape[1:], f32)
                for e in range(events):
                    deep_gz[e, lands_z(dz)] = jnp.zeros(deep_gz.shape[2:], f32)
            else:
                for e in range(events):
                    corner_g[e, lands_x(dx), lands_z(dz)] = jnp.zeros(corner_g.shape[3:], f32)

    loads[0].wait()
    loads[1].wait()
    rows_b = lax.broadcasted_iota(jnp.int32, (blocks, blocks), 0)
    cols_b = lax.broadcasted_iota(jnp.int32, (blocks, blocks), 1)
    target_row = jnp.broadcast_to(brick_ref[...].astype(f32), (blocks, blocks))
    target_col = jnp.sum(jnp.where(rows_b == cols_b, target_row, 0.0), axis=1, keepdims=True)
    same = jnp.where(target_col == target_row, 1.0, 0.0)
    position_row = jnp.sum(jnp.where(rows_b < cols_b, same, 0.0), axis=0, keepdims=True)
    position_col = jnp.sum(jnp.where(cols_b < rows_b, same, 0.0), axis=1, keepdims=True)
    placed_row = target_row[:1] * cap + position_row
    placed_col = target_col * cap + position_col
    slot_col = lax.broadcasted_iota(jnp.int32, (slots, blocks), 0).astype(f32)
    place = jnp.where(slot_col == placed_row, 1.0, 0.0)
    named = lax.broadcasted_iota(jnp.int32, (n_wide, blocks), 0).astype(f32) == target_row[:1]
    named = jnp.where(named, tile_ref[...].astype(f32), 0.0)
    at_lane = lax.broadcasted_iota(jnp.int32, (blocks, lanes), 1).astype(f32) == position_col
    at_lane = jnp.where(at_lane, 1.0, 0.0).astype(bf16)
    high, low = split(named)
    sent_tiles[...] = (dot(high, at_lane) + dot(low, at_lane)).reshape(n_wide, 1, lanes)

    def passing(phase, source, target, step):
        partner = lax.rem(wide + step, n_wide)
        return pltpu.make_async_remote_copy(
            src_ref=source.at[partner],
            dst_ref=target.at[wide],
            send_sem=send_sem.at[phase],
            recv_sem=recv_sem.at[phase],
            device_id=(partner, narrow),
            device_id_type=MESH,
        )

    def start_all(phase, source, target):
        def go(turn, carry):
            far = (turn + 1) // 2
            step = n_wide // 2 + far * (2 * (turn % 2) - 1)
            passing(phase, source, target, step).start()
            return carry

        lax.fori_loop(0, n_wide - 1, go, 0)
        target[wide] = source[wide]

    def whole(phase, source, target):
        others = pl.ds(0, n_wide - 1)
        return pltpu.make_async_remote_copy(
            src_ref=source.at[others],
            dst_ref=target.at[others],
            send_sem=send_sem.at[phase],
            recv_sem=recv_sem.at[phase],
            device_id=(lax.rem(wide + 1, n_wide), narrow),
            device_id_type=MESH,
        )

    def wait_all(phase, source, target):
        whole(phase, source, target).wait_recv()

    def end_all(phase, source, target):
        whole(phase, source, target).wait_send()

    loads[2].wait()
    loads[3].wait()
    volume = volume_ref[...]
    carried = [volume] + [volume * velocity_ref[a] for a in range(3)]
    for k in range(4):
        high = carried[k].astype(bf16).astype(f32)
        low = carried[k] - high
        rows[pl.ds(k, blocks, stride=8), :] = jnp.concatenate([high, high], axis=1)
        rows[pl.ds(4 + k, blocks, stride=8), :] = jnp.concatenate(
            [low, jnp.zeros_like(low)], axis=1
        )
    for b in range(blocks):
        if b % part == 0:
            loads[5 + b // part].wait()
        both = jnp.concatenate(split(kernel_buf[b]), axis=0)
        pieces[b] = both
        at = slice(b * 8, b * 8 + 8)
        products[at, :] = dot(rows[at, :].astype(bf16), both)
    own = [
        split(
            products[pl.ds(k, blocks, stride=8), :] + products[pl.ds(4 + k, blocks, stride=8), :]
        )
        for k in range(4)
    ]
    beside_x = jnp.where(wide > 0, 1, 0) + jnp.where(wide < n_wide - 1, 1, 0)
    beside_z = jnp.where(narrow > 0, 1, 0) + jnp.where(narrow < n_narrow - 1, 1, 0)
    pl.semaphore_wait(barrier, n_wide - 1 + beside_z * (1 + beside_x))

    start_all(0, sent_tiles, got_tiles)
    right = jnp.concatenate(
        [jnp.concatenate([o[0] for o in own], axis=1), jnp.concatenate([o[1] for o in own], axis=1)],
        axis=0,
    )
    place = jnp.concatenate([place, place], axis=1).astype(bf16)
    in_slots = dot(place, right)
    for k in range(4):
        sent[:, k] = in_slots[:, k * lanes : (k + 1) * lanes].reshape(n_wide, cap, lanes)
    start_all(1, sent, got)

    group = 8

    def turn(step, carry):
        for b in range(group):
            turned_pieces[step * group + b] = jnp.transpose(pieces[step * group + b])
        return carry

    lax.fori_loop(0, blocks // group, turn, 0)

    wait_all(0, sent_tiles, got_tiles)
    order = lax.broadcasted_iota(jnp.int32, (slots, tiles), 1)
    x_of, q_of, z_of = order // plane, (order // cz) % nq, order % cz
    tile_of = ((x_of * cz + z_of) * nq + q_of).astype(f32)
    tile_rows = jnp.broadcast_to(got_tiles[...], (n_wide, cap, lanes)).reshape(slots, lanes)
    slot_at = lax.broadcasted_iota(jnp.int32, (slots, lanes), 0) % cap
    lane_at = lax.broadcasted_iota(jnp.int32, (slots, lanes), 1)
    tile_slots = jnp.sum(jnp.where(slot_at == lane_at, tile_rows, 0.0), axis=1, keepdims=True)
    selector = jnp.where(tile_slots == tile_of, 1.0, 0.0)
    turned = jnp.transpose(selector).astype(bf16)
    selector = selector.astype(bf16)
    turned = jnp.concatenate([turned, turned], axis=1)
    selector = jnp.concatenate([selector, selector], axis=1)

    loads[4].wait()
    fluid = [
        jnp.concatenate(
            [
                fluid_ref[a, x, :, q * lanes : (q + 1) * lanes]
                for x in range(cx)
                for q in range(nq)
            ],
            axis=0,
        )
        for a in range(3)
    ]

    wait_all(1, sent, got)
    arrived = [split(got[:, k].reshape(slots, lanes)) for k in range(4)]
    right = jnp.concatenate(
        [jnp.concatenate([o[i] for o in arrived], axis=1) for i in range(2)], axis=0
    )
    spread = dot(turned, right)
    solid = spread[:, :lanes]
    growth = (1.0 + solid) * (1.0 + solid)
    scale = 1.0 / (1.0 + growth * solid)
    provisional = [
        (fluid[a] + growth * spread[:, (a + 1) * lanes : (a + 2) * lanes]) * scale
        for a in range(3)
    ]
    void = 1.0 / (1.0 + solid)
    shape = (nq, cz, lanes)

    def planes_of(value):
        return [value[x * plane : (x + 1) * plane].reshape(shape) for x in range(cx)]

    own_flux = [planes_of(void * provisional[a]) for a in range(3)]
    own_void = planes_of(void)

    def give_back(values, target, start):
        wide_values = [split(v) for v in values]
        right = jnp.concatenate(
            [jnp.concatenate([o[i] for o in wide_values], axis=1) for i in range(2)], axis=0
        )
        picked = dot(selector, right)
        for k in range(len(values)):
            target[:, start + k] = picked[:, k * lanes : (k + 1) * lanes].reshape(
                n_wide, cap, lanes
            )


    def ship(e, i, src, dst):
        dx, dz = DIRECTIONS[i]
        return pltpu.make_async_remote_copy(
            src_ref=src,
            dst_ref=dst,
            send_sem=side_send.at[e, i],
            recv_sem=side_recv.at[e, i],
            device_id=(wide + dx, narrow + dz),
            device_id_type=MESH,
        )

    def near_copy(i):
        dx, dz = DIRECTIONS[i]
        if dz == 0:
            return ship(0, i, near_x.at[0 if dx < 0 else 1], near_gx.at[lands_x(dx)])
        return ship(0, i, near_z, near_gz.at[lands_z(dz)])

    def deep_copy(e, i):
        dx, dz = DIRECTIONS[i]
        if dz == 0:
            start = 0 if dx < 0 else cx - DEPTH
            return ship(
                e + 1, i, deep.at[e, pl.ds(start, DEPTH)], deep_gx.at[e, lands_x(dx)]
            )
        if dx == 0:
            return ship(e + 1, i, deep.at[e], deep_gz.at[e, lands_z(dz)])
        return ship(
            e + 1,
            i,
            corner.at[e, 0 if dx < 0 else 1, 0 if dz < 0 else 1],
            corner_g.at[e, lands_x(dx), lands_z(dz)],
        )

    def each(directions, make, act, receiving=False):
        for i in directions:
            dx, dz = DIRECTIONS[i]

            @pl.when(exists(-dx, -dz) if receiving else exists(dx, dz))
            def _():
                getattr(make(i), act)()

    corner_spots = [(d, r) for d in range(1, DEPTH) for r in range(1, DEPTH + 1 - d)]

    def store_deep(e, planes):
        for x in range(cx):
            deep[e, x] = planes[x].reshape(plane, lanes)
        for sx in range(2):
            for sz in range(2):
                for n, (d, r) in enumerate(corner_spots):
                    x = d - 1 if sx == 0 else cx - d
                    z = r - 1 if sz == 0 else cz - r
                    corner[e, sx, sz, n * nq : (n + 1) * nq, :] = planes[x][:, z, :]

    row = lax.broadcasted_iota(jnp.int32, shape, 1)

    def tiles_from(own, others):
        if z_tiles == 2:
            first = narrow == 0
            return jnp.stack([jnp.where(first, own, others[0]), jnp.where(first, others[0], own)])
        return jnp.stack([others[0], own, others[1]])

    def own_of(value):
        if z_tiles == 2:
            return jnp.where(narrow == 0, value[0], value[1])
        return value[1]

    def corner_tile(e, side, which, d):
        tile = jnp.zeros(shape, f32)
        for n, (far, r) in enumerate(corner_spots):
            if far != d:
                continue
            spread_rows = jnp.stack(
                [
                    jnp.broadcast_to(
                        corner_g[e, side, which, n * nq + q : n * nq + q + 1, :], (cz, lanes)
                    )
                    for q in range(nq)
                ]
            )
            if z_tiles == 2:
                at = jnp.where(narrow == 0, r - 1, cz - r)
            else:
                at = cz - r if which == 0 else r - 1
            tile = jnp.where(row == at, spread_rows, tile)
        return tile

    def extended(e, planes):
        result = {}
        for x in range(cx):
            others = [deep_gz[e, t, x].reshape(shape) for t in range(z_tiles - 1)]
            result[x] = tiles_from(planes[x], others)
        for side in range(2):
            for d in range(1, DEPTH + 1):
                own = deep_gx[e, side, DEPTH - d if side == 0 else d - 1].reshape(shape)
                others = [corner_tile(e, side, t, d) for t in range(z_tiles - 1)]
                result[-d if side == 0 else cx - 1 + d] = tiles_from(own, others)
        return result

    def along_y(p):
        last = p.ndim - 1
        lane = lax.broadcasted_iota(jnp.int32, p.shape, last)
        up, down = pltpu.roll(p, lanes - 1, last), pltpu.roll(p, 1, last)
        if p.ndim == 4:
            zero = jnp.zeros_like(p[:, :1])
            next_up = jnp.concatenate([up[:, 1:], zero], axis=1)
            next_down = jnp.concatenate([zero, down[:, :-1]], axis=1)
        else:
            zero = jnp.zeros_like(p[:1])
            next_up = jnp.concatenate([up[1:], zero], axis=0)
            next_down = jnp.concatenate([zero, down[:-1]], axis=0)
        return jnp.where(lane == lanes - 1, next_up, up), jnp.where(lane == 0, next_down, down)

    def along_z(p):
        at = lax.broadcasted_iota(jnp.int32, p.shape, 2)
        up, down = pltpu.roll(p, cz - 1, 2), pltpu.roll(p, 1, 2)
        zero = jnp.zeros_like(p[:1])
        next_up = jnp.concatenate([up[1:], zero], axis=0)
        next_down = jnp.concatenate([zero, down[:-1]], axis=0)
        return jnp.where(at == cz - 1, next_up, up), jnp.where(at == 0, next_down, down)

    for side, x in ((0, 0), (1, cx - 1)):
        near_x[side, 0] = own_flux[0][x].reshape(plane, lanes)
        near_x[side, 1] = own_void[x].reshape(plane, lanes)
    for x in range(cx):
        near_z[0, x] = own_flux[1][x].reshape(plane, lanes)
        near_z[1, x] = own_void[x].reshape(plane, lanes)
    each((0, 1, 2, 3), near_copy, "start")
    store_deep(0, own_void)
    each((0, 1, 4, 5, 6, 7), lambda i: deep_copy(0, i), "start")

    void_y = [along_y(v) for v in own_void]
    flux_y = [along_y(v) for v in own_flux[2]]
    each((0, 1, 2, 3), near_copy, "wait_recv", True)

    def with_ghosts(planes, field):
        low = near_gx[0, field].reshape(shape)
        high = near_gx[1, field].reshape(shape)
        return [low] + planes + [high]

    flux_x, void_x = with_ghosts(own_flux[0], 0), with_ghosts(own_void, 1)
    void_inner, pressure = [], []
    for x in range(cx):
        flux_z, void_z = [
            tiles_from(own[x], [near_gz[t, field, x].reshape(shape) for t in range(z_tiles - 1)])
            for field, own in ((0, own_flux[1]), (1, own_void))
        ]
        void_inner.append(void_z)
        flux_up, flux_down = [own_of(v) for v in along_z(flux_z)]
        void_up, void_down = [own_of(v) for v in along_z(void_z)]
        source = -0.5 * (
            flux_x[x + 2] - flux_x[x] + flux_up - flux_down + flux_y[x][0] - flux_y[x][1]
        )
        around = void_x[x + 2] + void_x[x] + void_up + void_down + void_y[x][0] + void_y[x][1]
        pressure.append(source / (0.5 * (6.0 * own_void[x] + around)))

    def start_pressure(e, planes):
        store_deep(e, planes)
        each(range(8), lambda i: deep_copy(e, i), "start")

    def wait_pressure(e, planes):
        each(range(8), lambda i: deep_copy(e, i), "wait_recv", True)
        return extended(e, planes)

    start_pressure(1, pressure)
    give_back([growth], sent_growth, 0)
    end_all(0, sent_tiles, got_tiles)
    end_all(1, sent, got)
    each((0, 1, 2, 3), near_copy, "wait_send")

    each((0, 1, 4, 5, 6, 7), lambda i: deep_copy(0, i), "wait_recv", True)
    shares = {x: void_inner[x] for x in range(cx)}
    for side in range(2):
        for d in range(1, DEPTH + 1):
            own = deep_gx[0, side, DEPTH - d if side == 0 else d - 1].reshape(shape)
            others = [corner_tile(0, side, t, d) for t in range(z_tiles - 1)]
            shares[-d if side == 0 else cx - 1 + d] = tiles_from(own, others)
    weights = {}
    for x in range(1 - DEPTH, cx + DEPTH - 1):
        here = shares[x]
        nearby = (shares[x + 1], shares[x - 1]) + along_z(here) + along_y(here)
        sums = [here + v for v in nearby]
        total = sums[0] + sums[1] + sums[2] + sums[3] + sums[4] + sums[5]
        factor = jnp.where(here > 0.0, 1.0 / total, 0.0)
        weights[x] = [v * factor for v in sums]

    event = 1
    current = wait_pressure(event, pressure)
    start_all(2, sent_growth, got_growth)
    begun = current
    radius = DEPTH
    for sweep in range(SWEEPS - 1):
        if radius == 0:
            event += 1
            pressure = [own_of(current[x]) for x in range(cx)]
            start_pressure(event, pressure)
            current = wait_pressure(event, pressure)
            radius = DEPTH
        radius -= 1
        later = {}
        for x in range(-radius, cx + radius):
            p, w = current[x], weights[x]
            z_up, z_down = along_z(p)
            y_up, y_down = along_y(p)
            later[x] = (
                begun[x]
                + (w[0] * current[x + 1] + w[1] * current[x - 1])
                + (w[2] * z_up + w[3] * z_down)
                + (w[4] * y_up + w[5] * y_down)
            )
        current = later
    pressure = [own_of(current[x]) for x in range(cx)]
    steps = [[], [], []]
    for x in range(cx):
        z_up, z_down = along_z(current[x])
        y_up, y_down = along_y(pressure[x])
        steps[0].append(own_of(current[x + 1]) - own_of(current[x - 1]))
        steps[1].append(own_of(z_up) - own_of(z_down))
        steps[2].append(y_up - y_down)
    following = [
        provisional[a] - 0.5 * jnp.concatenate(steps[a], axis=0).reshape(tiles, lanes)
        for a in range(3)
    ]
    give_back([growth * v for v in following], sent_next, 0)
    start_all(3, sent_next, got_next)

    for x in range(cx):
        for q in range(nq):
            cut = slice(q * lanes, (q + 1) * lanes)
            at = (x * nq + q) * cz
            pressure_ref[x, :, cut] = pressure[x][q]
            for a in range(3):
                next_ref[a, x, :, cut] = following[a][at : at + cz]

    slot_row = lax.broadcasted_iota(jnp.int32, (blocks, slots), 1).astype(f32)
    back = jnp.where(slot_row == placed_col, 1.0, 0.0).astype(bf16)

    def place_back(target, k, row):
        high, low = split(target[:, k].reshape(slots, lanes))
        out = dot(back, jnp.concatenate([high, low], axis=1))
        rows[pl.ds(row, blocks, stride=8), :] = out[:, :lanes]
        rows[pl.ds(4 + row, blocks, stride=8), :] = out[:, lanes:]

    end_all(2, sent_growth, got_growth)
    each((0, 1, 4, 5, 6, 7), lambda i: deep_copy(0, i), "wait_send")
    for e in range(1, event + 1):
        each(range(8), lambda i: deep_copy(e, i), "wait_send")
    wait_all(2, sent_growth, got_growth)
    place_back(got_growth, 0, 3)
    wait_all(3, sent_next, got_next)
    for k in range(3):
        place_back(got_next, k, k)

    for b in range(blocks):
        at = slice(b * 8, b * 8 + 8)
        products[at, :] = dot(rows[at, :].astype(bf16), turned_pieces[b])

    def sampled(k):
        top = products[pl.ds(k, blocks, stride=8), :]
        low = products[pl.ds(4 + k, blocks, stride=8), :]
        return (top + low)[:, :particles] + pltpu.roll(top, particles, 1)[:, :particles]

    fourth = sampled(3)
    for k in range(3):
        drag_ref[k] = volume * sampled(k) - carried[1 + k] * fourth

    end_all(3, sent_next, got_next)


def hand_over(*refs):
    sources, targets, sems = refs[:3], refs[3:6], refs[6]
    copies = [pltpu.make_async_copy(sources[i], targets[i], sems.at[i]) for i in range(3)]
    for copy in copies:
        copy.start()
    for copy in copies:
        copy.wait()


def solution(mesh):
    n_wide, n_narrow = mesh.shape["wide"], mesh.shape["narrow"]

    def local(kernel, volume, velocity, block_brick, block_tile, fluid_velocity):
        blocks, particles, lanes = kernel.shape
        _, cx, cz, ny = fluid_velocity.shape
        cap = max(2, (2 * blocks + n_wide - 1) // n_wide)
        cap = (cap + 7) // 8 * 8
        nq = ny // lanes
        plane = nq * cz
        vmem = pltpu.VMEM
        hbm_spec = pl.BlockSpec(memory_space=pltpu.HBM)
        vmem_spec = pl.BlockSpec(memory_space=pltpu.VMEM)
        flux = [
            vmem((n_wide, 1, lanes), f32),
            vmem((n_wide, 1, lanes), f32),
            vmem((n_wide, 4, cap, lanes), f32),
            vmem((n_wide, 4, cap, lanes), f32),
            vmem((n_wide, 1, cap, lanes), f32),
            vmem((n_wide, 1, cap, lanes), f32),
            vmem((n_wide, 3, cap, lanes), f32),
            vmem((n_wide, 3, cap, lanes), f32),
        ]
        events = 2 + (SWEEPS - 1) // DEPTH
        others = 1 if n_narrow == 2 else 2
        corner_rows = (DEPTH * (DEPTH - 1) // 2 * nq + 7) // 8 * 8
        halo = [
            vmem((2, 2, plane, lanes), f32),
            vmem((2, 2, plane, lanes), f32),
            vmem((2, cx, plane, lanes), f32),
            vmem((others, 2, cx, plane, lanes), f32),
            vmem((events, cx, plane, lanes), f32),
            vmem((events, 2, DEPTH, plane, lanes), f32),
            vmem((events, others, cx, plane, lanes), f32),
            vmem((events, 2, 2, corner_rows, lanes), f32),
            vmem((events, 2, others, corner_rows, lanes), f32),
        ]
        drag, pressure, following = pl.pallas_call(
            functools.partial(body, n_wide, n_narrow, cap),
            out_shape=(
                jax.ShapeDtypeStruct((3, blocks, particles), f32),
                jax.ShapeDtypeStruct((cx, cz, ny), f32),
                jax.ShapeDtypeStruct((3, cx, cz, ny), f32),
            ),
            in_specs=[hbm_spec] * 6,
            out_specs=(vmem_spec,) * 3,
            scratch_shapes=[
                vmem((blocks, particles, lanes), f32),
                vmem((blocks, particles), f32),
                vmem((3, blocks, particles), f32),
                vmem((1, blocks), jnp.int32),
                vmem((1, blocks), jnp.int32),
                vmem((3, cx, cz, ny), f32),
                vmem((blocks, 2 * particles, lanes), bf16),
                vmem((blocks, lanes, 2 * particles), bf16),
                vmem((blocks * 8, lanes), f32),
                vmem((blocks * 8, lanes), f32),
            ]
            + flux
            + halo
            + [
                pltpu.SemaphoreType.DMA((5 + LOAD_PARTS,)),
                pltpu.SemaphoreType.DMA((4,)),
                pltpu.SemaphoreType.DMA((4,)),
                pltpu.SemaphoreType.DMA((events + 1, 8)),
                pltpu.SemaphoreType.DMA((events + 1, 8)),
            ],
            compiler_params=pltpu.CompilerParams(
                collective_id=0, has_side_effects=True, vmem_limit_bytes=40 * 1024 * 1024
            ),
        )(
            *[
                pltpu.with_memory_space_constraint(operand, pltpu.HBM)
                for operand in (
                    kernel,
                    volume,
                    jnp.transpose(velocity, (1, 0, 2)),
                    block_brick.reshape(1, blocks),
                    block_tile.reshape(1, blocks),
                    fluid_velocity,
                )
            ]
        )
        results = (drag, pressure, following)
        drag, pressure, following = pl.pallas_call(
            hand_over,
            out_shape=tuple(jax.ShapeDtypeStruct(r.shape, r.dtype) for r in results),
            in_specs=[vmem_spec] * 3,
            out_specs=(pl.BlockSpec(memory_space=pltpu.HBM),) * 3,
            scratch_shapes=[pltpu.SemaphoreType.DMA((3,))],
            compiler_params=pltpu.CompilerParams(vmem_limit_bytes=4 * 1024 * 1024),
        )(*results)
        return jnp.transpose(drag, (1, 0, 2)), pressure, following

    return jax.shard_map(
        local,
        mesh=mesh,
        in_specs=(
            P(("wide", "narrow"), None, None),
            P(("wide", "narrow"), None),
            P(("wide", "narrow"), None, None),
            P(("wide", "narrow"), None),
            P(("wide", "narrow")),
            P(None, "wide", "narrow", None),
        ),
        out_specs=(
            P(("wide", "narrow"), None, None),
            P("wide", "narrow", None),
            P(None, "wide", "narrow", None),
        ),
        check_vma=False,
    )
```

```python
import functools

import jax
import jax.numpy as jnp
from jax import lax
from jax.experimental import pallas as pl
from jax.experimental.pallas import tpu as pltpu
from jax.sharding import PartitionSpec as P

SWEEPS = 6
DEPTH = 3
LOAD_PARTS = 4
DIRECTIONS = ((-1, 0), (1, 0), (0, -1), (0, 1), (-1, -1), (-1, 1), (1, -1), (1, 1))
MESH = pl.DeviceIdType.MESH
f32 = jnp.float32
bf16 = jnp.bfloat16


def split(value):
    high = value.astype(bf16)
    return high, (value - high.astype(f32)).astype(bf16)


def dot(a, b):
    return jnp.dot(a, b, preferred_element_type=f32)


def body(
    n_wide, n_narrow, cap,
    kernel_hbm, volume_hbm, velocity_hbm, brick_hbm, tile_hbm, fluid_hbm,
    drag_ref, pressure_ref, next_ref,
    kernel_buf, volume_ref, velocity_ref, brick_ref, tile_ref, fluid_ref, pieces, turned_pieces, rows, products, sent_tiles, got_tiles, sent, got,
    sent_growth, got_growth, sent_next, got_next,
    near_x, near_gx, near_z, near_gz, deep, deep_gx, deep_gz, corner, corner_g,
    load_sem, send_sem, recv_sem, side_send, side_recv,
):
    wide, narrow = lax.axis_index("wide"), lax.axis_index("narrow")
    blocks, particles, lanes = kernel_buf.shape
    _, cx, cz, ny = fluid_ref.shape
    nq = ny // lanes
    plane = nq * cz
    tiles = cx * plane
    slots = n_wide * cap

    loads = [
        pltpu.make_async_copy(here, there, load_sem.at[i])
        for i, (here, there) in enumerate(
            (
                (brick_hbm, brick_ref),
                (tile_hbm, tile_ref),
                (volume_hbm, volume_ref),
                (velocity_hbm, velocity_ref),
                (fluid_hbm, fluid_ref),
            )
        )
    ]
    part = blocks // LOAD_PARTS
    for i in range(LOAD_PARTS):
        rows_of = pl.ds(i * part, part)
        loads.append(
            pltpu.make_async_copy(
                kernel_hbm.at[rows_of], kernel_buf.at[rows_of], load_sem.at[5 + i]
            )
        )
    for load in loads[:4] + loads[5:] + loads[4:5]:
        load.start()

    barrier = pltpu.get_barrier_semaphore()

    def greet(step, carry):
        pl.semaphore_signal(
            barrier, inc=1, device_id=(lax.rem(wide + step, n_wide), narrow), device_id_type=MESH
        )
        return carry

    lax.fori_loop(1, n_wide, greet, 0)
    z_tiles = near_gz.shape[0] + 1

    def exists(dx, dz):
        inside = (wide + dx >= 0) & (wide + dx < n_wide)
        return inside & (narrow + dz >= 0) & (narrow + dz < n_narrow)

    for dx, dz in DIRECTIONS:
        if dz:

            @pl.when(exists(dx, dz))
            def _():
                pl.semaphore_signal(
                    barrier, inc=1, device_id=(wide + dx, narrow + dz), device_id_type=MESH
                )

    def lands_x(dx):
        return 0 if dx > 0 else 1

    def lands_z(dz):
        return 0 if dz > 0 or z_tiles == 2 else 1

    for dx, dz in DIRECTIONS:
        if dz and z_tiles == 2:
            absent = jnp.logical_not(exists(-dx, 0)) if dx else None
            if dx and dz < 0:
                continue
        else:
            absent = jnp.logical_not(exists(-dx, -dz))
        if absent is None:
            continue

        @pl.when(absent)
        def _():
            events = deep.shape[0]
            if dz == 0:
                near_gx[lands_x(dx)] = jnp.zeros(near_gx.shape[1:], f32)
                for e in range(events):
                    deep_gx[e, lands_x(dx)] = jnp.zeros(deep_gx.shape[2:], f32)
            elif dx == 0:
                near_gz[lands_z(dz)] = jnp.zeros(near_gz.shape[1:], f32)
                for e in range(events):
                    deep_gz[e, lands_z(dz)] = jnp.zeros(deep_gz.shape[2:], f32)
            else:
                for e in range(events):
                    corner_g[e, lands_x(dx), lands_z(dz)] = jnp.zeros(corner_g.shape[3:], f32)

    loads[0].wait()
    loads[1].wait()
    rows_b = lax.broadcasted_iota(jnp.int32, (blocks, blocks), 0)
    cols_b = lax.broadcasted_iota(jnp.int32, (blocks, blocks), 1)
    target_row = jnp.broadcast_to(brick_ref[...].astype(f32), (blocks, blocks))
    target_col = jnp.sum(jnp.where(rows_b == cols_b, target_row, 0.0), axis=1, keepdims=True)
    same = jnp.where(target_col == target_row, 1.0, 0.0)
    position_row = jnp.sum(jnp.where(rows_b < cols_b, same, 0.0), axis=0, keepdims=True)
    position_col = jnp.sum(jnp.where(cols_b < rows_b, same, 0.0), axis=1, keepdims=True)
    placed_row = target_row[:1] * cap + position_row
    placed_col = target_col * cap + position_col
    slot_col = lax.broadcasted_iota(jnp.int32, (slots, blocks), 0).astype(f32)
    place = jnp.where(slot_col == placed_row, 1.0, 0.0)
    named = lax.broadcasted_iota(jnp.int32, (n_wide, blocks), 0).astype(f32) == target_row[:1]
    named = jnp.where(named, tile_ref[...].astype(f32), 0.0)
    at_lane = lax.broadcasted_iota(jnp.int32, (blocks, lanes), 1).astype(f32) == position_col
    at_lane = jnp.where(at_lane, 1.0, 0.0).astype(bf16)
    high, low = split(named)
    sent_tiles[...] = (dot(high, at_lane) + dot(low, at_lane)).reshape(n_wide, 1, lanes)

    def passing(phase, source, target, step):
        partner = lax.rem(wide + step, n_wide)
        return pltpu.make_async_remote_copy(
            src_ref=source.at[partner],
            dst_ref=target.at[wide],
            send_sem=send_sem.at[phase],
            recv_sem=recv_sem.at[phase],
            device_id=(partner, narrow),
            device_id_type=MESH,
        )

    def start_all(phase, source, target):
        for turn in range(n_wide - 1):
            far = (turn + 1) // 2
            step = n_wide // 2 + far * (2 * (turn % 2) - 1)
            passing(phase, source, target, step).start()
        target[wide] = source[wide]

    def whole(phase, source, target):
        others = pl.ds(0, n_wide - 1)
        return pltpu.make_async_remote_copy(
            src_ref=source.at[others],
            dst_ref=target.at[others],
            send_sem=send_sem.at[phase],
            recv_sem=recv_sem.at[phase],
            device_id=(lax.rem(wide + 1, n_wide), narrow),
            device_id_type=MESH,
        )

    def wait_all(phase, source, target):
        whole(phase, source, target).wait_recv()

    def end_all(phase, source, target):
        whole(phase, source, target).wait_send()

    loads[2].wait()
    loads[3].wait()
    volume = volume_ref[...]
    carried = [volume] + [volume * velocity_ref[a] for a in range(3)]
    for k in range(4):
        high = carried[k].astype(bf16).astype(f32)
        low = carried[k] - high
        rows[pl.ds(k, blocks, stride=8), :] = jnp.concatenate([high, high], axis=1)
        rows[pl.ds(4 + k, blocks, stride=8), :] = jnp.concatenate(
            [low, jnp.zeros_like(low)], axis=1
        )
    for b in range(blocks):
        if b % part == 0:
            loads[5 + b // part].wait()
        both = jnp.concatenate(split(kernel_buf[b]), axis=0)
        pieces[b] = both
        at = slice(b * 8, b * 8 + 8)
        products[at, :] = dot(rows[at, :].astype(bf16), both)
    own = [
        split(
            products[pl.ds(k, blocks, stride=8), :] + products[pl.ds(4 + k, blocks, stride=8), :]
        )
        for k in range(4)
    ]
    beside_x = jnp.where(wide > 0, 1, 0) + jnp.where(wide < n_wide - 1, 1, 0)
    beside_z = jnp.where(narrow > 0, 1, 0) + jnp.where(narrow < n_narrow - 1, 1, 0)
    pl.semaphore_wait(barrier, n_wide - 1 + beside_z * (1 + beside_x))

    start_all(0, sent_tiles, got_tiles)
    right = jnp.concatenate(
        [jnp.concatenate([o[0] for o in own], axis=1), jnp.concatenate([o[1] for o in own], axis=1)],
        axis=0,
    )
    place = jnp.concatenate([place, place], axis=1).astype(bf16)
    in_slots = dot(place, right)
    for k in range(4):
        sent[:, k] = in_slots[:, k * lanes : (k + 1) * lanes].reshape(n_wide, cap, lanes)
    start_all(1, sent, got)

    group = 8

    def turn(step, carry):
        for b in range(group):
            turned_pieces[step * group + b] = jnp.transpose(pieces[step * group + b])
        return carry

    lax.fori_loop(0, blocks // group, turn, 0)

    wait_all(0, sent_tiles, got_tiles)
    order = lax.broadcasted_iota(jnp.int32, (slots, tiles), 1)
    x_of, q_of, z_of = order // plane, (order // cz) % nq, order % cz
    tile_of = ((x_of * cz + z_of) * nq + q_of).astype(f32)
    tile_rows = jnp.broadcast_to(got_tiles[...], (n_wide, cap, lanes)).reshape(slots, lanes)
    slot_at = lax.broadcasted_iota(jnp.int32, (slots, lanes), 0) % cap
    lane_at = lax.broadcasted_iota(jnp.int32, (slots, lanes), 1)
    tile_slots = jnp.sum(jnp.where(slot_at == lane_at, tile_rows, 0.0), axis=1, keepdims=True)
    selector = jnp.where(tile_slots == tile_of, 1.0, 0.0)
    turned = jnp.transpose(selector).astype(bf16)
    selector = selector.astype(bf16)
    turned = jnp.concatenate([turned, turned], axis=1)
    selector = jnp.concatenate([selector, selector], axis=1)

    loads[4].wait()
    fluid = [
        jnp.concatenate(
            [
                fluid_ref[a, x, :, q * lanes : (q + 1) * lanes]
                for x in range(cx)
                for q in range(nq)
            ],
            axis=0,
        )
        for a in range(3)
    ]

    wait_all(1, sent, got)
    arrived = [split(got[:, k].reshape(slots, lanes)) for k in range(4)]
    right = jnp.concatenate(
        [jnp.concatenate([o[i] for o in arrived], axis=1) for i in range(2)], axis=0
    )
    spread = dot(turned, right)
    solid = spread[:, :lanes]
    growth = (1.0 + solid) * (1.0 + solid)
    scale = 1.0 / (1.0 + growth * solid)
    provisional = [
        (fluid[a] + growth * spread[:, (a + 1) * lanes : (a + 2) * lanes]) * scale
        for a in range(3)
    ]
    void = 1.0 / (1.0 + solid)
    shape = (nq, cz, lanes)

    def planes_of(value):
        return [value[x * plane : (x + 1) * plane].reshape(shape) for x in range(cx)]

    own_flux = [planes_of(void * provisional[a]) for a in range(3)]
    own_void = planes_of(void)

    def give_back(values, target, start):
        wide_values = [split(v) for v in values]
        right = jnp.concatenate(
            [jnp.concatenate([o[i] for o in wide_values], axis=1) for i in range(2)], axis=0
        )
        picked = dot(selector, right)
        for k in range(len(values)):
            target[:, start + k] = picked[:, k * lanes : (k + 1) * lanes].reshape(
                n_wide, cap, lanes
            )


    def ship(e, i, src, dst):
        dx, dz = DIRECTIONS[i]
        return pltpu.make_async_remote_copy(
            src_ref=src,
            dst_ref=dst,
            send_sem=side_send.at[e, i],
            recv_sem=side_recv.at[e, i],
            device_id=(wide + dx, narrow + dz),
            device_id_type=MESH,
        )

    def near_copy(i):
        dx, dz = DIRECTIONS[i]
        if dz == 0:
            return ship(0, i, near_x.at[0 if dx < 0 else 1], near_gx.at[lands_x(dx)])
        return ship(0, i, near_z, near_gz.at[lands_z(dz)])

    def deep_copy(e, i):
        dx, dz = DIRECTIONS[i]
        if dz == 0:
            start = 0 if dx < 0 else cx - DEPTH
            return ship(
                e + 1, i, deep.at[e, pl.ds(start, DEPTH)], deep_gx.at[e, lands_x(dx)]
            )
        if dx == 0:
            return ship(e + 1, i, deep.at[e], deep_gz.at[e, lands_z(dz)])
        return ship(
            e + 1,
            i,
            corner.at[e, 0 if dx < 0 else 1, 0 if dz < 0 else 1],
            corner_g.at[e, lands_x(dx), lands_z(dz)],
        )

    def each(directions, make, act, receiving=False):
        for i in directions:
            dx, dz = DIRECTIONS[i]

            @pl.when(exists(-dx, -dz) if receiving else exists(dx, dz))
            def _():
                getattr(make(i), act)()

    corner_spots = [(d, r) for d in range(1, DEPTH) for r in range(1, DEPTH + 1 - d)]

    def send_deep(e, planes, directions):
        for x in range(cx):
            deep[e, x] = planes[x].reshape(plane, lanes)
        each(directions, lambda i: deep_copy(e, i), "start")
        for sx in range(2):
            for sz in range(2):
                for n, (d, r) in enumerate(corner_spots):
                    x = d - 1 if sx == 0 else cx - d
                    z = r - 1 if sz == 0 else cz - r
                    corner[e, sx, sz, n * nq : (n + 1) * nq, :] = planes[x][:, z, :]
        each((4, 5, 6, 7), lambda i: deep_copy(e, i), "start")

    row = lax.broadcasted_iota(jnp.int32, shape, 1)

    def tiles_from(own, others):
        if z_tiles == 2:
            first = narrow == 0
            return jnp.stack([jnp.where(first, own, others[0]), jnp.where(first, others[0], own)])
        return jnp.stack([others[0], own, others[1]])

    def own_of(value):
        if z_tiles == 2:
            return jnp.where(narrow == 0, value[0], value[1])
        return value[1]

    def corner_tile(e, side, which, d):
        tile = jnp.zeros(shape, f32)
        for n, (far, r) in enumerate(corner_spots):
            if far != d:
                continue
            spread_rows = jnp.stack(
                [
                    jnp.broadcast_to(
                        corner_g[e, side, which, n * nq + q : n * nq + q + 1, :], (cz, lanes)
                    )
                    for q in range(nq)
                ]
            )
            if z_tiles == 2:
                at = jnp.where(narrow == 0, r - 1, cz - r)
            else:
                at = cz - r if which == 0 else r - 1
            tile = jnp.where(row == at, spread_rows, tile)
        return tile

    def extended(e, planes):
        result = {}
        for x in range(cx):
            others = [deep_gz[e, t, x].reshape(shape) for t in range(z_tiles - 1)]
            result[x] = tiles_from(planes[x], others)
        for side in range(2):
            for d in range(1, DEPTH + 1):
                own = deep_gx[e, side, DEPTH - d if side == 0 else d - 1].reshape(shape)
                others = [corner_tile(e, side, t, d) for t in range(z_tiles - 1)]
                result[-d if side == 0 else cx - 1 + d] = tiles_from(own, others)
        return result

    def along_y(p):
        last = p.ndim - 1
        lane = lax.broadcasted_iota(jnp.int32, p.shape, last)
        up, down = pltpu.roll(p, lanes - 1, last), pltpu.roll(p, 1, last)
        if p.ndim == 4:
            zero = jnp.zeros_like(p[:, :1])
            next_up = jnp.concatenate([up[:, 1:], zero], axis=1)
            next_down = jnp.concatenate([zero, down[:, :-1]], axis=1)
        else:
            zero = jnp.zeros_like(p[:1])
            next_up = jnp.concatenate([up[1:], zero], axis=0)
            next_down = jnp.concatenate([zero, down[:-1]], axis=0)
        return jnp.where(lane == lanes - 1, next_up, up), jnp.where(lane == 0, next_down, down)

    def along_z(p):
        at = lax.broadcasted_iota(jnp.int32, p.shape, 2)
        up, down = pltpu.roll(p, cz - 1, 2), pltpu.roll(p, 1, 2)
        zero = jnp.zeros_like(p[:1])
        next_up = jnp.concatenate([up[1:], zero], axis=0)
        next_down = jnp.concatenate([zero, down[:-1]], axis=0)
        return jnp.where(at == cz - 1, next_up, up), jnp.where(at == 0, next_down, down)

    for side, x in ((0, 0), (1, cx - 1)):
        near_x[side, 0] = own_flux[0][x].reshape(plane, lanes)
        near_x[side, 1] = own_void[x].reshape(plane, lanes)
    each((0, 1), near_copy, "start")
    for x in range(cx):
        near_z[0, x] = own_flux[1][x].reshape(plane, lanes)
        near_z[1, x] = own_void[x].reshape(plane, lanes)
    each((2, 3), near_copy, "start")
    send_deep(0, own_void, (0, 1))

    give_back([growth], sent_growth, 0)
    start_all(2, sent_growth, got_growth)

    void_y = [along_y(v) for v in own_void]
    flux_y = [along_y(v) for v in own_flux[2]]
    each((0, 1, 2, 3), near_copy, "wait_recv", True)

    def with_ghosts(planes, field):
        low = near_gx[0, field].reshape(shape)
        high = near_gx[1, field].reshape(shape)
        return [low] + planes + [high]

    flux_x, void_x = with_ghosts(own_flux[0], 0), with_ghosts(own_void, 1)
    void_inner, pressure = [], []
    for x in range(cx):
        flux_z, void_z = [
            tiles_from(own[x], [near_gz[t, field, x].reshape(shape) for t in range(z_tiles - 1)])
            for field, own in ((0, own_flux[1]), (1, own_void))
        ]
        void_inner.append(void_z)
        flux_up, flux_down = [own_of(v) for v in along_z(flux_z)]
        void_up, void_down = [own_of(v) for v in along_z(void_z)]
        source = -0.5 * (
            flux_x[x + 2] - flux_x[x] + flux_up - flux_down + flux_y[x][0] - flux_y[x][1]
        )
        around = void_x[x + 2] + void_x[x] + void_up + void_down + void_y[x][0] + void_y[x][1]
        pressure.append(source / (0.5 * (6.0 * own_void[x] + around)))

    def start_pressure(e, planes):
        send_deep(e, planes, (0, 1, 2, 3))

    def wait_pressure(e, planes):
        each(range(8), lambda i: deep_copy(e, i), "wait_recv", True)
        return extended(e, planes)

    start_pressure(1, pressure)
    end_all(0, sent_tiles, got_tiles)
    end_all(1, sent, got)
    each((0, 1, 2, 3), near_copy, "wait_send")

    each((0, 1, 4, 5, 6, 7), lambda i: deep_copy(0, i), "wait_recv", True)
    shares = {x: void_inner[x] for x in range(cx)}
    for side in range(2):
        for d in range(1, DEPTH + 1):
            own = deep_gx[0, side, DEPTH - d if side == 0 else d - 1].reshape(shape)
            others = [corner_tile(0, side, t, d) for t in range(z_tiles - 1)]
            shares[-d if side == 0 else cx - 1 + d] = tiles_from(own, others)
    weights = {}
    for x in range(1 - DEPTH, cx + DEPTH - 1):
        here = shares[x]
        nearby = (shares[x + 1], shares[x - 1]) + along_z(here) + along_y(here)
        sums = [here + v for v in nearby]
        total = sums[0] + sums[1] + sums[2] + sums[3] + sums[4] + sums[5]
        factor = jnp.where(here > 0.0, 1.0 / total, 0.0)
        weights[x] = [v * factor for v in sums]

    event = 1
    current = wait_pressure(event, pressure)
    begun = current
    radius = DEPTH
    for sweep in range(SWEEPS - 1):
        if radius == 0:
            event += 1
            pressure = [own_of(current[x]) for x in range(cx)]
            start_pressure(event, pressure)
            current = wait_pressure(event, pressure)
            radius = DEPTH
        radius -= 1
        later = {}
        for x in range(-radius, cx + radius):
            p, w = current[x], weights[x]
            z_up, z_down = along_z(p)
            y_up, y_down = along_y(p)
            later[x] = (
                begun[x]
                + (w[0] * current[x + 1] + w[1] * current[x - 1])
                + (w[2] * z_up + w[3] * z_down)
                + (w[4] * y_up + w[5] * y_down)
            )
        current = later
    pressure = [own_of(current[x]) for x in range(cx)]
    steps = [[], [], []]
    for x in range(cx):
        z_up, z_down = along_z(current[x])
        y_up, y_down = along_y(pressure[x])
        steps[0].append(own_of(current[x + 1]) - own_of(current[x - 1]))
        steps[1].append(own_of(z_up) - own_of(z_down))
        steps[2].append(y_up - y_down)
    following = [
        provisional[a] - 0.5 * jnp.concatenate(steps[a], axis=0).reshape(tiles, lanes)
        for a in range(3)
    ]
    give_back([growth * v for v in following], sent_next, 0)
    start_all(3, sent_next, got_next)

    for x in range(cx):
        for q in range(nq):
            cut = slice(q * lanes, (q + 1) * lanes)
            at = (x * nq + q) * cz
            pressure_ref[x, :, cut] = pressure[x][q]
            for a in range(3):
                next_ref[a, x, :, cut] = following[a][at : at + cz]

    slot_row = lax.broadcasted_iota(jnp.int32, (blocks, slots), 1).astype(f32)
    back = jnp.where(slot_row == placed_col, 1.0, 0.0).astype(bf16)

    def place_back(target, k, row):
        high, low = split(target[:, k].reshape(slots, lanes))
        out = dot(back, jnp.concatenate([high, low], axis=1))
        rows[pl.ds(row, blocks, stride=8), :] = out[:, :lanes]
        rows[pl.ds(4 + row, blocks, stride=8), :] = out[:, lanes:]

    end_all(2, sent_growth, got_growth)
    each((0, 1, 4, 5, 6, 7), lambda i: deep_copy(0, i), "wait_send")
    for e in range(1, event + 1):
        each(range(8), lambda i: deep_copy(e, i), "wait_send")
    wait_all(2, sent_growth, got_growth)
    place_back(got_growth, 0, 3)
    wait_all(3, sent_next, got_next)
    for k in range(3):
        place_back(got_next, k, k)

    for b in range(blocks):
        at = slice(b * 8, b * 8 + 8)
        products[at, :] = dot(rows[at, :].astype(bf16), turned_pieces[b])

    def sampled(k):
        top = products[pl.ds(k, blocks, stride=8), :]
        low = products[pl.ds(4 + k, blocks, stride=8), :]
        return (top + low)[:, :particles] + pltpu.roll(top, particles, 1)[:, :particles]

    fourth = sampled(3)
    for k in range(3):
        drag_ref[k] = volume * sampled(k) - carried[1 + k] * fourth

    end_all(3, sent_next, got_next)


def hand_over(*refs):
    sources, targets, sems = refs[:3], refs[3:6], refs[6]
    copies = [pltpu.make_async_copy(sources[i], targets[i], sems.at[i]) for i in range(3)]
    for copy in copies:
        copy.start()
    for copy in copies:
        copy.wait()


def solution(mesh):
    n_wide, n_narrow = mesh.shape["wide"], mesh.shape["narrow"]

    def local(kernel, volume, velocity, block_brick, block_tile, fluid_velocity):
        blocks, particles, lanes = kernel.shape
        _, cx, cz, ny = fluid_velocity.shape
        cap = max(2, (2 * blocks + n_wide - 1) // n_wide)
        cap = (cap + 7) // 8 * 8
        nq = ny // lanes
        plane = nq * cz
        vmem = pltpu.VMEM
        hbm_spec = pl.BlockSpec(memory_space=pltpu.HBM)
        vmem_spec = pl.BlockSpec(memory_space=pltpu.VMEM)
        flux = [
            vmem((n_wide, 1, lanes), f32),
            vmem((n_wide, 1, lanes), f32),
            vmem((n_wide, 4, cap, lanes), f32),
            vmem((n_wide, 4, cap, lanes), f32),
            vmem((n_wide, 1, cap, lanes), f32),
            vmem((n_wide, 1, cap, lanes), f32),
            vmem((n_wide, 3, cap, lanes), f32),
            vmem((n_wide, 3, cap, lanes), f32),
        ]
        events = 2 + (SWEEPS - 1) // DEPTH
        others = 1 if n_narrow == 2 else 2
        corner_rows = (DEPTH * (DEPTH - 1) // 2 * nq + 7) // 8 * 8
        halo = [
            vmem((2, 2, plane, lanes), f32),
            vmem((2, 2, plane, lanes), f32),
            vmem((2, cx, plane, lanes), f32),
            vmem((others, 2, cx, plane, lanes), f32),
            vmem((events, cx, plane, lanes), f32),
            vmem((events, 2, DEPTH, plane, lanes), f32),
            vmem((events, others, cx, plane, lanes), f32),
            vmem((events, 2, 2, corner_rows, lanes), f32),
            vmem((events, 2, others, corner_rows, lanes), f32),
        ]
        drag, pressure, following = pl.pallas_call(
            functools.partial(body, n_wide, n_narrow, cap),
            out_shape=(
                jax.ShapeDtypeStruct((3, blocks, particles), f32),
                jax.ShapeDtypeStruct((cx, cz, ny), f32),
                jax.ShapeDtypeStruct((3, cx, cz, ny), f32),
            ),
            in_specs=[hbm_spec] * 6,
            out_specs=(vmem_spec,) * 3,
            scratch_shapes=[
                vmem((blocks, particles, lanes), f32),
                vmem((blocks, particles), f32),
                vmem((3, blocks, particles), f32),
                vmem((1, blocks), jnp.int32),
                vmem((1, blocks), jnp.int32),
                vmem((3, cx, cz, ny), f32),
                vmem((blocks, 2 * particles, lanes), bf16),
                vmem((blocks, lanes, 2 * particles), bf16),
                vmem((blocks * 8, lanes), f32),
                vmem((blocks * 8, lanes), f32),
            ]
            + flux
            + halo
            + [
                pltpu.SemaphoreType.DMA((5 + LOAD_PARTS,)),
                pltpu.SemaphoreType.DMA((4,)),
                pltpu.SemaphoreType.DMA((4,)),
                pltpu.SemaphoreType.DMA((events + 1, 8)),
                pltpu.SemaphoreType.DMA((events + 1, 8)),
            ],
            compiler_params=pltpu.CompilerParams(
                collective_id=0, has_side_effects=True, vmem_limit_bytes=40 * 1024 * 1024
            ),
        )(
            *[
                pltpu.with_memory_space_constraint(operand, pltpu.HBM)
                for operand in (
                    kernel,
                    volume,
                    jnp.transpose(velocity, (1, 0, 2)),
                    block_brick.reshape(1, blocks),
                    block_tile.reshape(1, blocks),
                    fluid_velocity,
                )
            ]
        )
        results = (drag, pressure, following)
        drag, pressure, following = pl.pallas_call(
            hand_over,
            out_shape=tuple(jax.ShapeDtypeStruct(r.shape, r.dtype) for r in results),
            in_specs=[vmem_spec] * 3,
            out_specs=(pl.BlockSpec(memory_space=pltpu.HBM),) * 3,
            scratch_shapes=[pltpu.SemaphoreType.DMA((3,))],
            compiler_params=pltpu.CompilerParams(vmem_limit_bytes=4 * 1024 * 1024),
        )(*results)
        return jnp.transpose(drag, (1, 0, 2)), pressure, following

    return jax.shard_map(
        local,
        mesh=mesh,
        in_specs=(
            P(("wide", "narrow"), None, None),
            P(("wide", "narrow"), None),
            P(("wide", "narrow"), None, None),
            P(("wide", "narrow"), None),
            P(("wide", "narrow")),
            P(None, "wide", "narrow", None),
        ),
        out_specs=(
            P(("wide", "narrow"), None, None),
            P("wide", "narrow", None),
            P(None, "wide", "narrow", None),
        ),
        check_vma=False,
    )
```

```python
import functools

import jax
import jax.numpy as jnp
from jax import lax
from jax.experimental import pallas as pl
from jax.experimental.pallas import tpu as pltpu
from jax.sharding import PartitionSpec as P

SWEEPS = 6
DEPTH = 3
LOAD_PARTS = 4
DIRECTIONS = ((-1, 0), (1, 0), (0, -1), (0, 1), (-1, -1), (-1, 1), (1, -1), (1, 1))
MESH = pl.DeviceIdType.MESH
f32 = jnp.float32
bf16 = jnp.bfloat16


def split(value):
    high = value.astype(bf16)
    return high, (value - high.astype(f32)).astype(bf16)


def dot(a, b):
    return jnp.dot(a, b, preferred_element_type=f32)


def body(
    n_wide, n_narrow, cap,
    kernel_hbm, volume_hbm, velocity_hbm, brick_hbm, tile_hbm, fluid_hbm,
    drag_ref, pressure_ref, next_ref,
    kernel_buf, volume_ref, velocity_ref, brick_ref, tile_ref, fluid_ref, pieces, turned_pieces, rows, products, sent_tiles, got_tiles, sent, got,
    sent_growth, got_growth, sent_next, got_next,
    near_x, near_gx, near_z, near_gz, deep, deep_gx, deep_gz, corner, corner_g,
    load_sem, send_sem, recv_sem, side_send, side_recv,
):
    wide, narrow = lax.axis_index("wide"), lax.axis_index("narrow")
    blocks, particles, lanes = kernel_buf.shape
    _, cx, cz, ny = fluid_ref.shape
    nq = ny // lanes
    plane = nq * cz
    tiles = cx * plane
    slots = n_wide * cap

    loads = [
        pltpu.make_async_copy(here, there, load_sem.at[i])
        for i, (here, there) in enumerate(
            (
                (brick_hbm, brick_ref),
                (tile_hbm, tile_ref),
                (volume_hbm, volume_ref),
                (velocity_hbm, velocity_ref),
                (fluid_hbm, fluid_ref),
            )
        )
    ]
    part = blocks // LOAD_PARTS
    for i in range(LOAD_PARTS):
        rows_of = pl.ds(i * part, part)
        loads.append(
            pltpu.make_async_copy(
                kernel_hbm.at[rows_of], kernel_buf.at[rows_of], load_sem.at[5 + i]
            )
        )
    for load in loads[:4] + loads[5:] + loads[4:5]:
        load.start()

    barrier = pltpu.get_barrier_semaphore()

    def greet(step, carry):
        pl.semaphore_signal(
            barrier, inc=1, device_id=(lax.rem(wide + step, n_wide), narrow), device_id_type=MESH
        )
        return carry

    lax.fori_loop(1, n_wide, greet, 0)
    z_tiles = near_gz.shape[0] + 1

    def exists(dx, dz):
        inside = (wide + dx >= 0) & (wide + dx < n_wide)
        return inside & (narrow + dz >= 0) & (narrow + dz < n_narrow)

    for dx, dz in DIRECTIONS:
        if dz:

            @pl.when(exists(dx, dz))
            def _():
                pl.semaphore_signal(
                    barrier, inc=1, device_id=(wide + dx, narrow + dz), device_id_type=MESH
                )

    def lands_x(dx):
        return 0 if dx > 0 else 1

    def lands_z(dz):
        return 0 if dz > 0 or z_tiles == 2 else 1

    for dx, dz in DIRECTIONS:
        if dz and z_tiles == 2:
            absent = jnp.logical_not(exists(-dx, 0)) if dx else None
            if dx and dz < 0:
                continue
        else:
            absent = jnp.logical_not(exists(-dx, -dz))
        if absent is None:
            continue

        @pl.when(absent)
        def _():
            events = deep.shape[0]
            if dz == 0:
                near_gx[lands_x(dx)] = jnp.zeros(near_gx.shape[1:], f32)
                for e in range(events):
                    deep_gx[e, lands_x(dx)] = jnp.zeros(deep_gx.shape[2:], f32)
            elif dx == 0:
                near_gz[lands_z(dz)] = jnp.zeros(near_gz.shape[1:], f32)
                for e in range(events):
                    deep_gz[e, lands_z(dz)] = jnp.zeros(deep_gz.shape[2:], f32)
            else:
                for e in range(events):
                    corner_g[e, lands_x(dx), lands_z(dz)] = jnp.zeros(corner_g.shape[3:], f32)

    loads[0].wait()
    loads[1].wait()
    rows_b = lax.broadcasted_iota(jnp.int32, (blocks, blocks), 0)
    cols_b = lax.broadcasted_iota(jnp.int32, (blocks, blocks), 1)
    target_row = jnp.broadcast_to(brick_ref[...].astype(f32), (blocks, blocks))
    target_col = jnp.sum(jnp.where(rows_b == cols_b, target_row, 0.0), axis=1, keepdims=True)
    same = jnp.where(target_col == target_row, 1.0, 0.0)
    position_row = jnp.sum(jnp.where(rows_b < cols_b, same, 0.0), axis=0, keepdims=True)
    position_col = jnp.sum(jnp.where(cols_b < rows_b, same, 0.0), axis=1, keepdims=True)
    placed_row = target_row[:1] * cap + position_row
    placed_col = target_col * cap + position_col
    slot_col = lax.broadcasted_iota(jnp.int32, (slots, blocks), 0).astype(f32)
    place = jnp.where(slot_col == placed_row, 1.0, 0.0)
    named = lax.broadcasted_iota(jnp.int32, (n_wide, blocks), 0).astype(f32) == target_row[:1]
    named = jnp.where(named, tile_ref[...].astype(f32), 0.0)
    at_lane = lax.broadcasted_iota(jnp.int32, (blocks, lanes), 1).astype(f32) == position_col
    at_lane = jnp.where(at_lane, 1.0, 0.0).astype(bf16)
    high, low = split(named)
    sent_tiles[...] = (dot(high, at_lane) + dot(low, at_lane)).reshape(n_wide, 1, lanes)

    def passing(phase, source, target, step):
        partner = lax.rem(wide + step, n_wide)
        return pltpu.make_async_remote_copy(
            src_ref=source.at[partner],
            dst_ref=target.at[wide],
            send_sem=send_sem.at[phase],
            recv_sem=recv_sem.at[phase],
            device_id=(partner, narrow),
            device_id_type=MESH,
        )

    def start_all(phase, source, target):
        for turn in range(n_wide - 1):
            far = (turn + 1) // 2
            step = n_wide // 2 + far * (2 * (turn % 2) - 1)
            passing(phase, source, target, step).start()
        target[wide] = source[wide]

    def whole(phase, source, target):
        others = pl.ds(0, n_wide - 1)
        return pltpu.make_async_remote_copy(
            src_ref=source.at[others],
            dst_ref=target.at[others],
            send_sem=send_sem.at[phase],
            recv_sem=recv_sem.at[phase],
            device_id=(lax.rem(wide + 1, n_wide), narrow),
            device_id_type=MESH,
        )

    def wait_all(phase, source, target):
        whole(phase, source, target).wait_recv()

    def end_all(phase, source, target):
        whole(phase, source, target).wait_send()

    loads[2].wait()
    loads[3].wait()
    volume = volume_ref[...]
    carried = [volume] + [volume * velocity_ref[a] for a in range(3)]
    for k in range(4):
        high = carried[k].astype(bf16).astype(f32)
        low = carried[k] - high
        rows[pl.ds(k, blocks, stride=8), :] = jnp.concatenate([high, high], axis=1)
        rows[pl.ds(4 + k, blocks, stride=8), :] = jnp.concatenate(
            [low, jnp.zeros_like(low)], axis=1
        )
    for b in range(blocks):
        if b % part == 0:
            loads[5 + b // part].wait()
        both = jnp.concatenate(split(kernel_buf[b]), axis=0)
        pieces[b] = both
        at = slice(b * 8, b * 8 + 8)
        products[at, :] = dot(rows[at, :].astype(bf16), both)
    own = [
        split(
            products[pl.ds(k, blocks, stride=8), :] + products[pl.ds(4 + k, blocks, stride=8), :]
        )
        for k in range(4)
    ]
    right = jnp.concatenate(
        [jnp.concatenate([o[0] for o in own], axis=1), jnp.concatenate([o[1] for o in own], axis=1)],
        axis=0,
    )
    place = jnp.concatenate([place, place], axis=1).astype(bf16)
    in_slots = dot(place, right)
    for k in range(4):
        sent[:, k] = in_slots[:, k * lanes : (k + 1) * lanes].reshape(n_wide, cap, lanes)
    beside_x = jnp.where(wide > 0, 1, 0) + jnp.where(wide < n_wide - 1, 1, 0)
    beside_z = jnp.where(narrow > 0, 1, 0) + jnp.where(narrow < n_narrow - 1, 1, 0)
    pl.semaphore_wait(barrier, n_wide - 1 + beside_z * (1 + beside_x))

    start_all(1, sent, got)
    start_all(0, sent_tiles, got_tiles)

    group = 8

    def turn(step, carry):
        for b in range(group):
            turned_pieces[step * group + b] = jnp.transpose(pieces[step * group + b])
        return carry

    turned_first = blocks // group * 3 // 4
    lax.fori_loop(0, turned_first, turn, 0)

    wait_all(0, sent_tiles, got_tiles)
    order = lax.broadcasted_iota(jnp.int32, (slots, tiles), 1)
    x_of, q_of, z_of = order // plane, (order // cz) % nq, order % cz
    tile_of = ((x_of * cz + z_of) * nq + q_of).astype(f32)
    tile_rows = jnp.broadcast_to(got_tiles[...], (n_wide, cap, lanes)).reshape(slots, lanes)
    slot_at = lax.broadcasted_iota(jnp.int32, (slots, lanes), 0) % cap
    lane_at = lax.broadcasted_iota(jnp.int32, (slots, lanes), 1)
    tile_slots = jnp.sum(jnp.where(slot_at == lane_at, tile_rows, 0.0), axis=1, keepdims=True)
    selector = jnp.where(tile_slots == tile_of, 1.0, 0.0)
    turned = jnp.transpose(selector).astype(bf16)
    selector = selector.astype(bf16)
    turned = jnp.concatenate([turned, turned], axis=1)
    selector = jnp.concatenate([selector, selector], axis=1)

    loads[4].wait()
    fluid = [
        jnp.concatenate(
            [
                fluid_ref[a, x, :, q * lanes : (q + 1) * lanes]
                for x in range(cx)
                for q in range(nq)
            ],
            axis=0,
        )
        for a in range(3)
    ]

    wait_all(1, sent, got)
    arrived = [split(got[:, k].reshape(slots, lanes)) for k in range(4)]
    right = jnp.concatenate(
        [jnp.concatenate([o[i] for o in arrived], axis=1) for i in range(2)], axis=0
    )
    spread = dot(turned, right)
    solid = spread[:, :lanes]
    growth = (1.0 + solid) * (1.0 + solid)
    scale = 1.0 / (1.0 + growth * solid)
    provisional = [
        (fluid[a] + growth * spread[:, (a + 1) * lanes : (a + 2) * lanes]) * scale
        for a in range(3)
    ]
    void = 1.0 / (1.0 + solid)
    shape = (nq, cz, lanes)

    def planes_of(value):
        return [value[x * plane : (x + 1) * plane].reshape(shape) for x in range(cx)]

    own_flux = [planes_of(void * provisional[a]) for a in range(3)]
    own_void = planes_of(void)

    def give_back(values, target, start):
        wide_values = [split(v) for v in values]
        right = jnp.concatenate(
            [jnp.concatenate([o[i] for o in wide_values], axis=1) for i in range(2)], axis=0
        )
        picked = dot(selector, right)
        for k in range(len(values)):
            target[:, start + k] = picked[:, k * lanes : (k + 1) * lanes].reshape(
                n_wide, cap, lanes
            )


    def ship(e, i, src, dst):
        dx, dz = DIRECTIONS[i]
        return pltpu.make_async_remote_copy(
            src_ref=src,
            dst_ref=dst,
            send_sem=side_send.at[e, i],
            recv_sem=side_recv.at[e, i],
            device_id=(wide + dx, narrow + dz),
            device_id_type=MESH,
        )

    def near_copy(i):
        dx, dz = DIRECTIONS[i]
        if dz == 0:
            return ship(0, i, near_x.at[0 if dx < 0 else 1], near_gx.at[lands_x(dx)])
        return ship(0, i, near_z, near_gz.at[lands_z(dz)])

    def deep_copy(e, i):
        dx, dz = DIRECTIONS[i]
        if dz == 0:
            start = 0 if dx < 0 else cx - DEPTH
            return ship(
                e + 1, i, deep.at[e, pl.ds(start, DEPTH)], deep_gx.at[e, lands_x(dx)]
            )
        if dx == 0:
            return ship(e + 1, i, deep.at[e], deep_gz.at[e, lands_z(dz)])
        return ship(
            e + 1,
            i,
            corner.at[e, 0 if dx < 0 else 1, 0 if dz < 0 else 1],
            corner_g.at[e, lands_x(dx), lands_z(dz)],
        )

    def each(directions, make, act, receiving=False):
        for i in directions:
            dx, dz = DIRECTIONS[i]

            @pl.when(exists(-dx, -dz) if receiving else exists(dx, dz))
            def _():
                getattr(make(i), act)()

    corner_spots = [(d, r) for d in range(1, DEPTH) for r in range(1, DEPTH + 1 - d)]

    def send_deep(e, planes, directions):
        for x in range(cx):
            deep[e, x] = planes[x].reshape(plane, lanes)
        each(directions, lambda i: deep_copy(e, i), "start")
        for sx in range(2):
            for sz in range(2):
                for n, (d, r) in enumerate(corner_spots):
                    x = d - 1 if sx == 0 else cx - d
                    z = r - 1 if sz == 0 else cz - r
                    corner[e, sx, sz, n * nq : (n + 1) * nq, :] = planes[x][:, z, :]
        each((4, 5, 6, 7), lambda i: deep_copy(e, i), "start")

    row = lax.broadcasted_iota(jnp.int32, shape, 1)

    def tiles_from(own, others):
        if z_tiles == 2:
            first = narrow == 0
            return jnp.stack([jnp.where(first, own, others[0]), jnp.where(first, others[0], own)])
        return jnp.stack([others[0], own, others[1]])

    def own_of(value):
        if z_tiles == 2:
            return jnp.where(narrow == 0, value[0], value[1])
        return value[1]

    def corner_tile(e, side, which, d):
        tile = jnp.zeros(shape, f32)
        for n, (far, r) in enumerate(corner_spots):
            if far != d:
                continue
            spread_rows = jnp.stack(
                [
                    jnp.broadcast_to(
                        corner_g[e, side, which, n * nq + q : n * nq + q + 1, :], (cz, lanes)
                    )
                    for q in range(nq)
                ]
            )
            if z_tiles == 2:
                at = jnp.where(narrow == 0, r - 1, cz - r)
            else:
                at = cz - r if which == 0 else r - 1
            tile = jnp.where(row == at, spread_rows, tile)
        return tile

    def extended(e, planes):
        result = {}
        for x in range(cx):
            others = [deep_gz[e, t, x].reshape(shape) for t in range(z_tiles - 1)]
            result[x] = tiles_from(planes[x], others)
        for side in range(2):
            for d in range(1, DEPTH + 1):
                own = deep_gx[e, side, DEPTH - d if side == 0 else d - 1].reshape(shape)
                others = [corner_tile(e, side, t, d) for t in range(z_tiles - 1)]
                result[-d if side == 0 else cx - 1 + d] = tiles_from(own, others)
        return result

    def along_y(p):
        last = p.ndim - 1
        lane = lax.broadcasted_iota(jnp.int32, p.shape, last)
        up, down = pltpu.roll(p, lanes - 1, last), pltpu.roll(p, 1, last)
        if p.ndim == 4:
            zero = jnp.zeros_like(p[:, :1])
            next_up = jnp.concatenate([up[:, 1:], zero], axis=1)
            next_down = jnp.concatenate([zero, down[:, :-1]], axis=1)
        else:
            zero = jnp.zeros_like(p[:1])
            next_up = jnp.concatenate([up[1:], zero], axis=0)
            next_down = jnp.concatenate([zero, down[:-1]], axis=0)
        return jnp.where(lane == lanes - 1, next_up, up), jnp.where(lane == 0, next_down, down)

    def along_z(p):
        at = lax.broadcasted_iota(jnp.int32, p.shape, 2)
        up, down = pltpu.roll(p, cz - 1, 2), pltpu.roll(p, 1, 2)
        zero = jnp.zeros_like(p[:1])
        next_up = jnp.concatenate([up[1:], zero], axis=0)
        next_down = jnp.concatenate([zero, down[:-1]], axis=0)
        return jnp.where(at == cz - 1, next_up, up), jnp.where(at == 0, next_down, down)

    for side, x in ((0, 0), (1, cx - 1)):
        near_x[side, 0] = own_flux[0][x].reshape(plane, lanes)
        near_x[side, 1] = own_void[x].reshape(plane, lanes)
    each((0, 1), near_copy, "start")
    for x in range(cx):
        near_z[0, x] = own_flux[1][x].reshape(plane, lanes)
        near_z[1, x] = own_void[x].reshape(plane, lanes)
    each((2, 3), near_copy, "start")
    send_deep(0, own_void, (0, 1))

    give_back([growth], sent_growth, 0)
    start_all(2, sent_growth, got_growth)

    void_y = [along_y(v) for v in own_void]
    flux_y = [along_y(v) for v in own_flux[2]]
    each((0, 1, 2, 3), near_copy, "wait_recv", True)

    def with_ghosts(planes, field):
        low = near_gx[0, field].reshape(shape)
        high = near_gx[1, field].reshape(shape)
        return [low] + planes + [high]

    flux_x, void_x = with_ghosts(own_flux[0], 0), with_ghosts(own_void, 1)
    void_inner, pressure = [], []
    for x in range(cx):
        flux_z, void_z = [
            tiles_from(own[x], [near_gz[t, field, x].reshape(shape) for t in range(z_tiles - 1)])
            for field, own in ((0, own_flux[1]), (1, own_void))
        ]
        void_inner.append(void_z)
        flux_up, flux_down = [own_of(v) for v in along_z(flux_z)]
        void_up, void_down = [own_of(v) for v in along_z(void_z)]
        source = -0.5 * (
            flux_x[x + 2] - flux_x[x] + flux_up - flux_down + flux_y[x][0] - flux_y[x][1]
        )
        around = void_x[x + 2] + void_x[x] + void_up + void_down + void_y[x][0] + void_y[x][1]
        pressure.append(source / (0.5 * (6.0 * own_void[x] + around)))

    def start_pressure(e, planes):
        send_deep(e, planes, (0, 1, 2, 3))

    def wait_pressure(e, planes):
        each(range(8), lambda i: deep_copy(e, i), "wait_recv", True)
        return extended(e, planes)

    start_pressure(1, pressure)
    end_all(0, sent_tiles, got_tiles)
    end_all(1, sent, got)
    each((0, 1, 2, 3), near_copy, "wait_send")

    each((0, 1, 4, 5, 6, 7), lambda i: deep_copy(0, i), "wait_recv", True)
    shares = {x: void_inner[x] for x in range(cx)}
    for side in range(2):
        for d in range(1, DEPTH + 1):
            own = deep_gx[0, side, DEPTH - d if side == 0 else d - 1].reshape(shape)
            others = [corner_tile(0, side, t, d) for t in range(z_tiles - 1)]
            shares[-d if side == 0 else cx - 1 + d] = tiles_from(own, others)
    weights = {}
    for x in range(1 - DEPTH, cx + DEPTH - 1):
        here = shares[x]
        nearby = (shares[x + 1], shares[x - 1]) + along_z(here) + along_y(here)
        sums = [here + v for v in nearby]
        total = sums[0] + sums[1] + sums[2] + sums[3] + sums[4] + sums[5]
        factor = jnp.where(here > 0.0, 1.0 / total, 0.0)
        weights[x] = [v * factor for v in sums]

    event = 1
    current = wait_pressure(event, pressure)
    begun = current
    radius = DEPTH
    for sweep in range(SWEEPS - 1):
        if radius == 0:
            event += 1
            pressure = [own_of(current[x]) for x in range(cx)]
            start_pressure(event, pressure)
            if event == 2:
                lax.fori_loop(turned_first, blocks // group, turn, 0)
            current = wait_pressure(event, pressure)
            radius = DEPTH
        radius -= 1
        later = {}
        for x in range(-radius, cx + radius):
            p, w = current[x], weights[x]
            z_up, z_down = along_z(p)
            y_up, y_down = along_y(p)
            later[x] = (
                begun[x]
                + (w[0] * current[x + 1] + w[1] * current[x - 1])
                + (w[2] * z_up + w[3] * z_down)
                + (w[4] * y_up + w[5] * y_down)
            )
        current = later
    pressure = [own_of(current[x]) for x in range(cx)]
    steps = [[], [], []]
    for x in range(cx):
        z_up, z_down = along_z(current[x])
        y_up, y_down = along_y(pressure[x])
        steps[0].append(own_of(current[x + 1]) - own_of(current[x - 1]))
        steps[1].append(own_of(z_up) - own_of(z_down))
        steps[2].append(y_up - y_down)
    following = [
        provisional[a] - 0.5 * jnp.concatenate(steps[a], axis=0).reshape(tiles, lanes)
        for a in range(3)
    ]
    give_back([growth * v for v in following], sent_next, 0)
    start_all(3, sent_next, got_next)

    for x in range(cx):
        for q in range(nq):
            cut = slice(q * lanes, (q + 1) * lanes)
            at = (x * nq + q) * cz
            pressure_ref[x, :, cut] = pressure[x][q]
            for a in range(3):
                next_ref[a, x, :, cut] = following[a][at : at + cz]

    slot_row = lax.broadcasted_iota(jnp.int32, (blocks, slots), 1).astype(f32)
    back = jnp.where(slot_row == placed_col, 1.0, 0.0).astype(bf16)

    def place_back(target, found):
        parts = [split(target[:, k].reshape(slots, lanes)) for k in range(len(found))]
        out = dot(back, jnp.concatenate([half for pair in parts for half in pair], axis=1))
        for k, row in enumerate(found):
            for half in range(2):
                cut = slice((2 * k + half) * lanes, (2 * k + half + 1) * lanes)
                rows[pl.ds(4 * half + row, blocks, stride=8), :] = out[:, cut]

    end_all(2, sent_growth, got_growth)
    each((0, 1, 4, 5, 6, 7), lambda i: deep_copy(0, i), "wait_send")
    for e in range(1, event + 1):
        each(range(8), lambda i: deep_copy(e, i), "wait_send")
    wait_all(2, sent_growth, got_growth)
    place_back(got_growth, (3,))
    wait_all(3, sent_next, got_next)
    place_back(got_next, (0, 1, 2))

    for b in range(blocks):
        at = slice(b * 8, b * 8 + 8)
        products[at, :] = dot(rows[at, :].astype(bf16), turned_pieces[b])

    def sampled(k):
        top = products[pl.ds(k, blocks, stride=8), :]
        low = products[pl.ds(4 + k, blocks, stride=8), :]
        return (top + low)[:, :particles] + pltpu.roll(top, particles, 1)[:, :particles]

    fourth = sampled(3)
    for k in range(3):
        drag_ref[k] = volume * sampled(k) - carried[1 + k] * fourth

    end_all(3, sent_next, got_next)


def hand_over(*refs):
    sources, targets, sems = refs[:3], refs[3:6], refs[6]
    copies = [pltpu.make_async_copy(sources[i], targets[i], sems.at[i]) for i in range(3)]
    for copy in copies:
        copy.start()
    for copy in copies:
        copy.wait()


def solution(mesh):
    n_wide, n_narrow = mesh.shape["wide"], mesh.shape["narrow"]

    def local(kernel, volume, velocity, block_brick, block_tile, fluid_velocity):
        blocks, particles, lanes = kernel.shape
        _, cx, cz, ny = fluid_velocity.shape
        cap = max(2, (2 * blocks + n_wide - 1) // n_wide)
        cap = (cap + 7) // 8 * 8
        nq = ny // lanes
        plane = nq * cz
        vmem = pltpu.VMEM
        hbm_spec = pl.BlockSpec(memory_space=pltpu.HBM)
        vmem_spec = pl.BlockSpec(memory_space=pltpu.VMEM)
        flux = [
            vmem((n_wide, 1, lanes), f32),
            vmem((n_wide, 1, lanes), f32),
            vmem((n_wide, 4, cap, lanes), f32),
            vmem((n_wide, 4, cap, lanes), f32),
            vmem((n_wide, 1, cap, lanes), f32),
            vmem((n_wide, 1, cap, lanes), f32),
            vmem((n_wide, 3, cap, lanes), f32),
            vmem((n_wide, 3, cap, lanes), f32),
        ]
        events = 2 + (SWEEPS - 1) // DEPTH
        others = 1 if n_narrow == 2 else 2
        corner_rows = (DEPTH * (DEPTH - 1) // 2 * nq + 7) // 8 * 8
        halo = [
            vmem((2, 2, plane, lanes), f32),
            vmem((2, 2, plane, lanes), f32),
            vmem((2, cx, plane, lanes), f32),
            vmem((others, 2, cx, plane, lanes), f32),
            vmem((events, cx, plane, lanes), f32),
            vmem((events, 2, DEPTH, plane, lanes), f32),
            vmem((events, others, cx, plane, lanes), f32),
            vmem((events, 2, 2, corner_rows, lanes), f32),
            vmem((events, 2, others, corner_rows, lanes), f32),
        ]
        drag, pressure, following = pl.pallas_call(
            functools.partial(body, n_wide, n_narrow, cap),
            out_shape=(
                jax.ShapeDtypeStruct((3, blocks, particles), f32),
                jax.ShapeDtypeStruct((cx, cz, ny), f32),
                jax.ShapeDtypeStruct((3, cx, cz, ny), f32),
            ),
            in_specs=[hbm_spec] * 6,
            out_specs=(vmem_spec,) * 3,
            scratch_shapes=[
                vmem((blocks, particles, lanes), f32),
                vmem((blocks, particles), f32),
                vmem((3, blocks, particles), f32),
                vmem((1, blocks), jnp.int32),
                vmem((1, blocks), jnp.int32),
                vmem((3, cx, cz, ny), f32),
                vmem((blocks, 2 * particles, lanes), bf16),
                vmem((blocks, lanes, 2 * particles), bf16),
                vmem((blocks * 8, lanes), f32),
                vmem((blocks * 8, lanes), f32),
            ]
            + flux
            + halo
            + [
                pltpu.SemaphoreType.DMA((5 + LOAD_PARTS,)),
                pltpu.SemaphoreType.DMA((4,)),
                pltpu.SemaphoreType.DMA((4,)),
                pltpu.SemaphoreType.DMA((events + 1, 8)),
                pltpu.SemaphoreType.DMA((events + 1, 8)),
            ],
            compiler_params=pltpu.CompilerParams(
                collective_id=0, has_side_effects=True, vmem_limit_bytes=40 * 1024 * 1024
            ),
        )(
            *[
                pltpu.with_memory_space_constraint(operand, pltpu.HBM)
                for operand in (
                    kernel,
                    volume,
                    jnp.transpose(velocity, (1, 0, 2)),
                    block_brick.reshape(1, blocks),
                    block_tile.reshape(1, blocks),
                    fluid_velocity,
                )
            ]
        )
        results = (drag, pressure, following)
        drag, pressure, following = pl.pallas_call(
            hand_over,
            out_shape=tuple(jax.ShapeDtypeStruct(r.shape, r.dtype) for r in results),
            in_specs=[vmem_spec] * 3,
            out_specs=(pl.BlockSpec(memory_space=pltpu.HBM),) * 3,
            scratch_shapes=[pltpu.SemaphoreType.DMA((3,))],
            compiler_params=pltpu.CompilerParams(vmem_limit_bytes=4 * 1024 * 1024),
        )(*results)
        return jnp.transpose(drag, (1, 0, 2)), pressure, following

    return jax.shard_map(
        local,
        mesh=mesh,
        in_specs=(
            P(("wide", "narrow"), None, None),
            P(("wide", "narrow"), None),
            P(("wide", "narrow"), None, None),
            P(("wide", "narrow"), None),
            P(("wide", "narrow")),
            P(None, "wide", "narrow", None),
        ),
        out_specs=(
            P(("wide", "narrow"), None, None),
            P("wide", "narrow", None),
            P(None, "wide", "narrow", None),
        ),
        check_vma=False,
    )
```
